32 devices in a mesh: row: 4 (over x, core), col: 4 (over z), layer: 2 (over y).
Axes of the slice: x: 2, y: 2, z: 4, core: 2. Of those that a mesh axis runs over, the one named last changes fastest.
Arguments:
- values: bfloat16 [2048, 2048], P('row', 'col'), may hold values from 0.0099487305 to 1
- tile_mask: int32 [16, 16], P('row', 'col'), may hold values from 0 to 1, as said below
Outputs:
- clustered: float32 [2048, 2048], P('row', ('col', 'layer'))
The draws below stay inside these ranges and needn't reach their ends.
Inputs may be any that keep to these rules, and one draw needn't show every extreme that they name: `tile_mask`: every diagonal tile is nonzero. The blocks of (16 / 4) x 4 tiles that one device holds each have at most 8 nonzero tiles and at least 4; the block in the first grid row and first grid column has exactly 8.
All inputs are finite; a program needn't handle non-finite values.
Results may differ from the reference program's by a relative error of at most 0.0065.
Values may be sent and summed in bfloat16 or wider, within the bound.
A program may use at most 128 MiB of HBM per device.

```python
import math
import jax
import jax.numpy as jnp
from jax import lax

TILE = 128
TC = 4
NT = 16
N = 2048
LIVE = 8
N_ROW = 4
N_COL = 4


def draw_tile_mask(key, part):
    key_score = jax.random.fold_in(key, 11)
    key_count = jax.random.fold_in(key, 12)
    block_rows = NT // N_ROW
    cells = block_rows * TC
    rows_idx = lax.broadcasted_iota(jnp.int32, (NT, NT), 0)
    cols_idx = lax.broadcasted_iota(jnp.int32, (NT, NT), 1)
    local = rows_idx % block_rows * TC + cols_idx % TC
    scores = jax.random.randint(key_score, (NT, NT), 0, 2 ** 20) * cells + local
    scores = jnp.where(rows_idx == cols_idx, scores + 2 ** 28, scores)
    blocks = scores.reshape(N_ROW, block_rows, N_COL, TC).transpose(0, 2, 1, 3).reshape(N_ROW, N_COL, cells)
    order = jnp.argsort(-blocks, axis=-1, stable=True)
    rank = jnp.argsort(order, axis=-1, stable=True).astype(jnp.int32)
    counts = jax.random.randint(key_count, (N_ROW, N_COL), TC, LIVE + 1)
    counts = counts.at[0, 0].set(LIVE)
    active = (rank < counts[:, :, None]).astype(jnp.int32)
    active = active.reshape(N_ROW, N_COL, block_rows, TC).transpose(0, 2, 1, 3).reshape(NT, NT)
    return active.astype(jnp.int32)


def block_levels(own_key, shape, pieces, least, largest):
    gain = 1.0
    for dim, blocks in pieces:
        steps = jax.random.uniform(jax.random.fold_in(jax.random.fold_in(own_key, 6), dim), (blocks,), jnp.float32, least / len(pieces), largest / len(pieces))
        gain = gain * jnp.repeat(jnp.exp(steps), shape[dim] // blocks).reshape((-1,) + (1,) * (len(shape) - 1 - dim))
    return gain


def setup_inputs(seed: int = 0) -> dict:
    keys = jax.random.split(jax.random.key(seed), 3)
    return {
        "values": jnp.clip(jnp.exp(math.log(1.0) - 4.61031033 * jax.random.uniform(keys[0], (N, N), jnp.float32) ** block_levels(keys[0], (N, N), ((0, 4), (1, 4)), -0.2, 0.2)), 0.0099487305, 1.0).astype(jnp.bfloat16),
        "tile_mask": draw_tile_mask(jax.random.fold_in(keys[2], 71), 0),
    }


def reference(values, tile_mask):
    grid = values.reshape(NT, TILE, NT, TILE) * tile_mask.astype(jnp.bfloat16)[:, None, :, None]
    masked = grid.reshape(N, N)
    mass = jnp.sum(masked, axis=0, dtype=jnp.float32)
    stochastic = (masked.astype(jnp.float32) / mass[None, :]).astype(jnp.bfloat16)
    expanded = jnp.dot(stochastic, stochastic, preferred_element_type=jnp.float32)
    inflated = expanded * expanded
    weight = jnp.sum(inflated, axis=0)
    return (N * 1.0) * inflated / weight[None, :]
```

```python
import functools

import jax
import jax.numpy as jnp
from jax import lax
from jax.experimental import pallas as pl
from jax.experimental.pallas import tpu as pltpu
from jax.sharding import PartitionSpec as P

MESH = pl.DeviceIdType.MESH
EDGE = 128
CHUNKS = 2


def kernel(
    dims, v_ref, m_ref, infl_ref, scale_ref,
    by_tile, pack, rbuf, acc, mask_all, ranks, mpart, mass, wpart, *rest,
):
    n_row, n_col, n_layer, tiles_r, tiles_c, live = dims
    steps = n_col - 1
    from_left = rest[:steps]
    from_right = rest[steps : 2 * steps]
    (z_send, z_recv, y_send, y_recv, x_send, x_recv, mask_send, mask_recv,
     mp_send, mp_recv, ms_send, ms_recv, w_send, w_recv) = rest[2 * steps :]
    height, width = tiles_r * EDGE, tiles_c * EDGE
    half = width // n_layer
    half_tiles = tiles_c // n_layer
    tiles = tiles_r * tiles_c
    part = live // n_layer
    chunk = part // CHUNKS
    per = height // width
    r = lax.axis_index("row")
    c = lax.axis_index("col")
    l = lax.axis_index("layer")

    barrier = pltpu.get_barrier_semaphore()
    for axis, me, size in (("col", c, n_col), ("row", r, n_row), ("layer", l, n_layer)):
        for j in range(1, size):
            pl.semaphore_signal(
                barrier, inc=1, device_id={axis: lax.rem(me + j, size)}, device_id_type=MESH
            )

    def rank_list(flags):
        count = jnp.int32(0)
        out = []
        for flag in flags:
            out.append(flag * count + (1 - flag) * live)
            count = count + flag
        return out

    flags = [m_ref[t // tiles_c, t % tiles_c] for t in range(tiles)]
    for t in range(tiles):
        tr, tc = t // tiles_c, t % tiles_c
        by_tile[t] = v_ref[tr * EDGE : (tr + 1) * EDGE, tc * EDGE : (tc + 1) * EDGE]
    count = jnp.int32(0)
    upto = []
    for t in range(tiles):
        count = count + flags[t]
        upto.append(count)
    zero_tile = jnp.zeros((EDGE, EDGE), jnp.bfloat16)
    for s in range(live):
        index = jnp.int32(0)
        for t in range(tiles - 1):
            index = index + lax.select(upto[t] <= s, jnp.int32(1), jnp.int32(0))
        pack[s] = by_tile[index]
    pack[live] = zero_tile
    own_ranks = rank_list(flags)
    for t in range(tiles):
        ranks[t] = own_ranks[t]
    for buf in (*from_left, *from_right):
        buf[live] = zero_tile
    for t in range(tiles):
        mask_all[c, t // tiles_c, t % tiles_c] = flags[t]

    pl.semaphore_wait(barrier, n_col - 1 + n_row - 1 + n_layer - 1)

    sends = []

    def slots(layer, ch):
        return pl.ds(layer * part + ch * chunk, chunk)

    def z_copy(way, s, ch):
        bufs = from_left if way == 0 else from_right
        src = pack if s == 1 else bufs[s - 2]
        where = slots(l, ch)
        return pltpu.make_async_remote_copy(
            src_ref=src.at[where], dst_ref=bufs[s - 1].at[where],
            send_sem=z_send.at[way, s - 1, ch], recv_sem=z_recv.at[way, s - 1, ch],
            device_id={"col": c + 1 if way == 0 else c - 1}, device_id_type=MESH,
        )

    def y_copy(way, s, ch, j, layer):
        buf = (from_left if way == 0 else from_right)[s - 1]
        where = slots(layer, ch)
        return pltpu.make_async_remote_copy(
            src_ref=buf.at[where], dst_ref=buf.at[where],
            send_sem=y_send.at[way, s - 1, ch, j - 1], recv_sem=y_recv.at[way, s - 1, ch, j - 1],
            device_id={"layer": lax.rem(l + j, n_layer)}, device_id_type=MESH,
        )

    def here(way, s):
        return c >= s if way == 0 else c + s < n_col

    def sends_on(way, s):
        if way == 0:
            return (c + 1 < n_col) & (c >= s - 1)
        return (c >= 1) & (c + s - 1 < n_col)

    def z_start(s, ch):
        for way in (0, 1):
            @pl.when(sends_on(way, s))
            def _():
                z_copy(way, s, ch).start()

    for ch in range(CHUNKS):
        z_start(1, ch)

    def to_peers(axis, me, size, ref, send, recv):
        copies = []
        for j in range(1, size):
            copy = pltpu.make_async_remote_copy(
                src_ref=ref.at[me], dst_ref=ref.at[me],
                send_sem=send.at[j - 1], recv_sem=recv.at[j - 1],
                device_id={axis: lax.rem(me + j, size)}, device_id_type=MESH,
            )
            copy.start()
            sends.append(copy)
            copies.append(copy)
        return copies

    mask_copies = to_peers("col", c, n_col, mask_all, mask_send, mask_recv)

    for tc in range(tiles_c):
        total = jnp.zeros((EDGE, EDGE), jnp.float32)
        for tr in range(tiles_r):
            total = total + pack[own_ranks[tr * tiles_c + tc]].astype(jnp.float32)
        mpart[r, :, tc * EDGE : (tc + 1) * EDGE] = jnp.sum(total, axis=0, keepdims=True)
    mp_copies = to_peers("row", r, n_row, mpart, mp_send, mp_recv)

    for tr in range(tiles_r):
        for j in range(half_tiles):
            rank = ranks[tr * tiles_c + l * half_tiles + j]
            rbuf[r, tr * EDGE : (tr + 1) * EDGE, j * EDGE : (j + 1) * EDGE] = pack[rank]

    sibling = r + 1 - 2 * lax.rem(r, 2)
    pairs = n_row // 2

    def x_copy(k, section, target):
        return pltpu.make_async_remote_copy(
            src_ref=rbuf.at[section], dst_ref=rbuf.at[section],
            send_sem=x_send.at[k], recv_sem=x_recv.at[k],
            device_id={"row": target}, device_id_type=MESH,
        )

    across = [lax.rem(r + 2 * j, n_row) for j in range(1, pairs)]
    for j, target in enumerate(across):
        x_copy(1 + j, r, target).start()
    x_copy(0, r, sibling).start()

    for copy in mp_copies:
        copy.wait_recv()
    total = mpart[0]
    for j in range(1, n_row):
        total = total + mpart[j]
    mass[c] = total
    ms_copies = to_peers("col", c, n_col, mass, ms_send, ms_recv)

    def forward(s):
        for ch in range(CHUNKS):
            for way in (0, 1):
                @pl.when(here(way, s))
                def _():
                    z_copy(way, s, ch).wait_recv()
                    if s < steps:
                        @pl.when(sends_on(way, s + 1))
                        def _():
                            z_copy(way, s + 1, ch).start()
                    for j in range(1, n_layer):
                        y_copy(way, s, ch, j, l).start()

    def product(buf, block):
        scale = 1.0 / mass[block]
        flags = [mask_all[block, t // tiles_c, t % tiles_c] for t in range(tiles)]
        local = rank_list(flags)
        section, offset = block // per, (block % per) * width
        right = rbuf[section, pl.ds(pl.multiple_of(offset, EDGE), width), :]
        rows_at_once = min(tiles_r, 4)
        for first in range(0, tiles_r, rows_at_once):
            rows = []
            for tr in range(first, first + rows_at_once):
                row = []
                for tc in range(tiles_c):
                    tile = buf[local[tr * tiles_c + tc]].astype(jnp.float32)
                    row.append((tile * scale[:, tc * EDGE : (tc + 1) * EDGE]).astype(jnp.bfloat16))
                rows.append(jnp.concatenate(row, axis=1))
            left = jnp.concatenate(rows, axis=0)
            span = slice(first * EDGE, (first + rows_at_once) * EDGE)
            acc[span, :] += jnp.dot(left, right, preferred_element_type=jnp.float32)

    def foreign(s):
        for way in (0, 1):
            @pl.when(here(way, s))
            def _():
                for ch in range(CHUNKS):
                    for j in range(1, n_layer):
                        y_copy(way, s, ch, j, lax.rem(l + n_layer - j, n_layer)).wait_recv()
                product(
                    (from_left if way == 0 else from_right)[s - 1],
                    c - s if way == 0 else c + s,
                )

    acc[...] = jnp.zeros_like(acc)
    for s in range(1, max(steps, 2)):
        forward(s)
    for j, target in enumerate(across):
        x_copy(1 + j, lax.rem(r + n_row - 2 * (j + 1), n_row), target).wait_recv()
        x_copy(pairs + j, lax.rem(r + n_row - 2 * (j + 1), n_row), sibling).start()
    x_copy(0, sibling, sibling).wait_recv()
    for j in range(len(across)):
        x_copy(pairs + j, lax.rem(sibling + n_row - 2 * (j + 1), n_row), sibling).wait_recv()
    for copy in (*mask_copies, *ms_copies):
        copy.wait_recv()
    product(pack, c)
    for s in range(1, steps - 1):
        foreign(s)
    if steps >= 2:
        forward(steps)
    for s in range(max(steps - 1, 1), steps + 1):
        foreign(s)

    inflated = acc[...] * acc[...]
    infl_ref[...] = inflated
    wpart[r] = jnp.sum(inflated, axis=0, keepdims=True)
    for copy in to_peers("row", r, n_row, wpart, w_send, w_recv):
        copy.wait_recv()
    total = wpart[0]
    for j in range(1, n_row):
        total = total + wpart[j]
    scale_ref[...] = (height * n_row * 1.0) / total

    for copy in sends:
        copy.wait_send()
    for j, target in enumerate(across):
        x_copy(1 + j, r, target).wait_send()
        x_copy(pairs + j, r, sibling).wait_send()
    x_copy(0, r, sibling).wait_send()
    for s in range(1, steps + 1):
        for way in (0, 1):
            @pl.when(sends_on(way, s))
            def _():
                for ch in range(CHUNKS):
                    z_copy(way, s, ch).wait_send()

            @pl.when(here(way, s))
            def _():
                for ch in range(CHUNKS):
                    for j in range(1, n_layer):
                        y_copy(way, s, ch, j, l).wait_send()


def shards(values, tile_mask):
    n_row, n_col, n_layer = (lax.axis_size(a) for a in ("row", "col", "layer"))
    height, width = values.shape
    tiles_r, tiles_c = tile_mask.shape
    live = tiles_r * tiles_c // 2
    half = width // n_layer
    dims = (n_row, n_col, n_layer, tiles_r, tiles_c, live)
    steps = n_col - 1
    dma = pltpu.SemaphoreType.DMA
    inflated, scale = pl.pallas_call(
        functools.partial(kernel, dims),
        out_shape=(
            jax.ShapeDtypeStruct((height, half), jnp.float32),
            jax.ShapeDtypeStruct((1, half), jnp.float32),
        ),
        in_specs=[
            pl.BlockSpec(memory_space=pltpu.VMEM),
            pl.BlockSpec(memory_space=pltpu.SMEM),
        ],
        out_specs=(pl.BlockSpec(memory_space=pltpu.VMEM),) * 2,
        scratch_shapes=[
            pltpu.VMEM((tiles_r * tiles_c, EDGE, EDGE), jnp.bfloat16),
            pltpu.VMEM((live + 1, EDGE, EDGE), jnp.bfloat16),
            pltpu.VMEM((n_row, height, half), jnp.bfloat16),
            pltpu.VMEM((height, half), jnp.float32),
            pltpu.SMEM((n_col, tiles_r, tiles_c), jnp.int32),
            pltpu.SMEM((tiles_r * tiles_c,), jnp.int32),
            pltpu.VMEM((n_row, 1, width), jnp.float32),
            pltpu.VMEM((n_col, 1, width), jnp.float32),
            pltpu.VMEM((n_row, 1, half), jnp.float32),
            *[pltpu.VMEM((live + 1, EDGE, EDGE), jnp.bfloat16)] * (2 * steps),
            dma((2, steps, CHUNKS)),
            dma((2, steps, CHUNKS)),
            dma((2, steps, CHUNKS, n_layer - 1)),
            dma((2, steps, CHUNKS, n_layer - 1)),
            dma((n_row,)),
            dma((n_row,)),
            dma((n_col - 1,)),
            dma((n_col - 1,)),
            dma((n_row - 1,)),
            dma((n_row - 1,)),
            dma((n_col - 1,)),
            dma((n_col - 1,)),
            dma((n_row - 1,)),
            dma((n_row - 1,)),
        ],
        compiler_params=pltpu.CompilerParams(
            collective_id=0, has_side_effects=True, vmem_limit_bytes=56 * 2**20
        ),
        name="markov_step",
    )(values, tile_mask)
    return inflated * scale


def solution(mesh):
    return jax.shard_map(
        shards,
        mesh=mesh,
        in_specs=(P("row", "col"), P("row", "col")),
        out_specs=P("row", ("col", "layer")),
        check_vma=False,
    )
```

```python
import functools

import jax
import jax.numpy as jnp
from jax import lax
from jax.experimental import pallas as pl
from jax.experimental.pallas import tpu as pltpu
from jax.sharding import PartitionSpec as P

MESH = pl.DeviceIdType.MESH
EDGE = 128
CHUNKS = 2


def kernel(
    dims, v_ref, m_ref, out_ref,
    by_tile, pack, rbuf, acc, mask_all, ranks, mpart, mass, wpart, *rest,
):
    n_row, n_col, n_layer, tiles_r, tiles_c, live = dims
    steps = n_col - 1
    from_left = rest[:steps]
    from_right = rest[steps : 2 * steps]
    (in_sem, z_send, z_recv, y_send, y_recv, x_send, x_recv, mask_send, mask_recv,
     mp_send, mp_recv, ms_send, ms_recv, w_send, w_recv) = rest[2 * steps :]
    height, width = tiles_r * EDGE, tiles_c * EDGE
    half = width // n_layer
    half_tiles = tiles_c // n_layer
    tiles = tiles_r * tiles_c
    part = live // n_layer
    chunk = part // CHUNKS
    per = height // width
    r = lax.axis_index("row")
    c = lax.axis_index("col")
    l = lax.axis_index("layer")

    barrier = pltpu.get_barrier_semaphore()
    for axis, me, size in (("row", r, n_row), ("layer", l, n_layer)):
        for j in range(1, size):
            pl.semaphore_signal(
                barrier, inc=1, device_id={axis: lax.rem(me + j, size)}, device_id_type=MESH
            )

    @pl.when(c > 0)
    def _():
        pl.semaphore_signal(barrier, inc=1, device_id={"col": c - 1}, device_id_type=MESH)

    @pl.when(c + 1 < n_col)
    def _():
        pl.semaphore_signal(barrier, inc=1, device_id={"col": c + 1}, device_id_type=MESH)

    mask_in = pltpu.make_async_copy(m_ref, mask_all.at[c], in_sem.at[0])
    mask_in.start()
    for t in range(tiles):
        tr, tc = t // tiles_c, t % tiles_c
        pltpu.make_async_copy(
            v_ref.at[tr * EDGE : (tr + 1) * EDGE, tc * EDGE : (tc + 1) * EDGE],
            by_tile.at[t], in_sem.at[1],
        ).start()
    zero_tile = jnp.zeros((EDGE, EDGE), jnp.bfloat16)
    for buf in (pack, *from_left, *from_right):
        buf[live] = zero_tile
    acc[...] = jnp.zeros_like(acc)
    mask_in.wait()

    def rank_list(flags):
        count = jnp.int32(0)
        out = []
        for flag in flags:
            out.append(flag * count + (1 - flag) * live)
            count = count + flag
        return out

    flags = [mask_all[c, t // tiles_c, t % tiles_c] for t in range(tiles)]
    count = jnp.int32(0)
    upto = []
    for t in range(tiles):
        count = count + flags[t]
        upto.append(count)
    pltpu.make_async_copy(by_tile, by_tile, in_sem.at[1]).wait()
    for s in range(live):
        index = jnp.int32(0)
        for t in range(tiles - 1):
            index = index + lax.select(upto[t] <= s, jnp.int32(1), jnp.int32(0))
        pack[s] = by_tile[index]
    own_ranks = rank_list(flags)
    for t in range(tiles):
        ranks[t] = own_ranks[t]

    for tc in range(tiles_c):
        total = jnp.zeros((EDGE, EDGE), jnp.float32)
        for tr in range(tiles_r):
            total = total + pack[own_ranks[tr * tiles_c + tc]].astype(jnp.float32)
        mpart[r, :, tc * EDGE : (tc + 1) * EDGE] = jnp.sum(total, axis=0, keepdims=True)

    for tr in range(tiles_r):
        for j in range(half_tiles):
            rank = ranks[tr * tiles_c + l * half_tiles + j]
            rbuf[r, tr * EDGE : (tr + 1) * EDGE, j * EDGE : (j + 1) * EDGE] = pack[rank]

    neighbours = lax.select(c > 0, 1, 0) + lax.select(c + 1 < n_col, 1, 0)
    pl.semaphore_wait(barrier, n_row - 1 + n_layer - 1 + neighbours)

    sends = []

    def slots(layer, ch):
        return pl.ds(layer * part + ch * chunk, chunk)

    def z_copy(way, s, ch):
        bufs = from_left if way == 0 else from_right
        src = pack if s == 1 else bufs[s - 2]
        where = slots(l, ch)
        return pltpu.make_async_remote_copy(
            src_ref=src.at[where], dst_ref=bufs[s - 1].at[where],
            send_sem=z_send.at[way, s - 1, ch], recv_sem=z_recv.at[way, s - 1, ch],
            device_id={"col": c + 1 if way == 0 else c - 1}, device_id_type=MESH,
        )

    def y_copy(way, s, ch, j, layer):
        buf = (from_left if way == 0 else from_right)[s - 1]
        where = slots(layer, ch)
        return pltpu.make_async_remote_copy(
            src_ref=buf.at[where], dst_ref=buf.at[where],
            send_sem=y_send.at[way, s - 1, ch, j - 1], recv_sem=y_recv.at[way, s - 1, ch, j - 1],
            device_id={"layer": lax.rem(l + j, n_layer)}, device_id_type=MESH,
        )

    def here(way, s):
        return c >= s if way == 0 else c + s < n_col

    def sends_on(way, s):
        if way == 0:
            return (c + 1 < n_col) & (c >= s - 1)
        return (c >= 1) & (c + s - 1 < n_col)

    def z_start(s, ch):
        for way in (0, 1):
            @pl.when(sends_on(way, s))
            def _():
                z_copy(way, s, ch).start()

    for ch in range(CHUNKS):
        z_start(1, ch)

    def to_peers(axis, me, size, ref, send, recv):
        copies = []
        for j in range(1, size):
            copy = pltpu.make_async_remote_copy(
                src_ref=ref.at[me], dst_ref=ref.at[me],
                send_sem=send.at[j - 1], recv_sem=recv.at[j - 1],
                device_id={axis: lax.rem(me + j, size)}, device_id_type=MESH,
            )
            copy.start()
            sends.append(copy)
            copies.append(copy)
        return copies

    def hand_on(ref, send, recv, way, s):
        block = c - (s - 1) if way == 0 else c + (s - 1)
        return pltpu.make_async_remote_copy(
            src_ref=ref.at[block], dst_ref=ref.at[block],
            send_sem=send.at[way, s - 1], recv_sem=recv.at[way, s - 1],
            device_id={"col": c + 1 if way == 0 else c - 1}, device_id_type=MESH,
        )

    def received(ref, send, recv, way, s):
        block = c - s if way == 0 else c + s
        return pltpu.make_async_remote_copy(
            src_ref=ref.at[block], dst_ref=ref.at[block],
            send_sem=send.at[way, s - 1], recv_sem=recv.at[way, s - 1],
            device_id={"col": c + 1 if way == 0 else c - 1}, device_id_type=MESH,
        )

    small = ((mask_all, mask_send, mask_recv), (mass, ms_send, ms_recv))

    mp_copies = to_peers("row", r, n_row, mpart, mp_send, mp_recv)
    for way in (0, 1):
        @pl.when(sends_on(way, 1))
        def _():
            hand_on(*small[0], way, 1).start()

    sibling = r + 1 - 2 * lax.rem(r, 2)
    pairs = n_row // 2

    def x_copy(k, section, target):
        return pltpu.make_async_remote_copy(
            src_ref=rbuf.at[section], dst_ref=rbuf.at[section],
            send_sem=x_send.at[k], recv_sem=x_recv.at[k],
            device_id={"row": target}, device_id_type=MESH,
        )

    across = [lax.rem(r + 2 * j, n_row) for j in range(1, pairs)]
    for j, target in enumerate(across):
        x_copy(1 + j, r, target).start()
    x_copy(0, r, sibling).start()

    for copy in mp_copies:
        copy.wait_recv()
    total = mpart[0]
    for j in range(1, n_row):
        total = total + mpart[j]
    mass[c] = total
    for way in (0, 1):
        @pl.when(sends_on(way, 1))
        def _():
            hand_on(*small[1], way, 1).start()

    def forward(s):
        for ch in range(CHUNKS):
            for way in (0, 1):
                @pl.when(here(way, s))
                def _():
                    z_copy(way, s, ch).wait_recv()
                    if s < steps:
                        @pl.when(sends_on(way, s + 1))
                        def _():
                            z_copy(way, s + 1, ch).start()
                    for j in range(1, n_layer):
                        y_copy(way, s, ch, j, l).start()
        for way in (0, 1):
            @pl.when(here(way, s))
            def _():
                for group in small:
                    received(*group, way, s).wait_recv()
                if s < steps:
                    @pl.when(sends_on(way, s + 1))
                    def _():
                        for group in small:
                            hand_on(*group, way, s + 1).start()

    def product(buf, block):
        scale = 1.0 / mass[block]
        flags = [mask_all[block, t // tiles_c, t % tiles_c] for t in range(tiles)]
        local = rank_list(flags)
        section, offset = block // per, (block % per) * width
        right = rbuf[section, pl.ds(pl.multiple_of(offset, EDGE), width), :]
        rows_at_once = min(tiles_r, 4)
        for first in range(0, tiles_r, rows_at_once):
            rows = []
            for tr in range(first, first + rows_at_once):
                row = []
                for tc in range(tiles_c):
                    tile = buf[local[tr * tiles_c + tc]].astype(jnp.float32)
                    row.append((tile * scale[:, tc * EDGE : (tc + 1) * EDGE]).astype(jnp.bfloat16))
                rows.append(jnp.concatenate(row, axis=1))
            left = jnp.concatenate(rows, axis=0)
            span = slice(first * EDGE, (first + rows_at_once) * EDGE)
            acc[span, :] += jnp.dot(left, right, preferred_element_type=jnp.float32)

    def foreign(s):
        for way in (0, 1):
            @pl.when(here(way, s))
            def _():
                for ch in range(CHUNKS):
                    for j in range(1, n_layer):
                        y_copy(way, s, ch, j, lax.rem(l + n_layer - j, n_layer)).wait_recv()
                product(
                    (from_left if way == 0 else from_right)[s - 1],
                    c - s if way == 0 else c + s,
                )

    for s in range(1, max(steps, 2)):
        forward(s)
    for j, target in enumerate(across):
        x_copy(1 + j, lax.rem(r + n_row - 2 * (j + 1), n_row), target).wait_recv()
        x_copy(pairs + j, lax.rem(r + n_row - 2 * (j + 1), n_row), sibling).start()
    x_copy(0, sibling, sibling).wait_recv()
    for j in range(len(across)):
        x_copy(pairs + j, lax.rem(sibling + n_row - 2 * (j + 1), n_row), sibling).wait_recv()
    product(pack, c)
    for s in range(1, steps - 1):
        foreign(s)
    if steps >= 2:
        forward(steps)
    for s in range(max(steps - 1, 1), steps + 1):
        foreign(s)

    inflated = acc[...] * acc[...]
    acc[...] = inflated
    wpart[r] = jnp.sum(inflated, axis=0, keepdims=True)
    for copy in to_peers("row", r, n_row, wpart, w_send, w_recv):
        copy.wait_recv()
    total = wpart[0]
    for j in range(1, n_row):
        total = total + wpart[j]
    out_ref[...] = acc[...] * ((height * n_row * 1.0) / total)

    for copy in sends:
        copy.wait_send()
    for j, target in enumerate(across):
        x_copy(1 + j, r, target).wait_send()
        x_copy(pairs + j, r, sibling).wait_send()
    x_copy(0, r, sibling).wait_send()
    for s in range(1, steps + 1):
        for way in (0, 1):
            @pl.when(sends_on(way, s))
            def _():
                for ch in range(CHUNKS):
                    z_copy(way, s, ch).wait_send()
                for group in small:
                    hand_on(*group, way, s).wait_send()

            @pl.when(here(way, s))
            def _():
                for ch in range(CHUNKS):
                    for j in range(1, n_layer):
                        y_copy(way, s, ch, j, l).wait_send()


def shards(values, tile_mask):
    n_row, n_col, n_layer = (lax.axis_size(a) for a in ("row", "col", "layer"))
    height, width = values.shape
    tiles_r, tiles_c = tile_mask.shape
    live = tiles_r * tiles_c // 2
    half = width // n_layer
    dims = (n_row, n_col, n_layer, tiles_r, tiles_c, live)
    steps = n_col - 1
    dma = pltpu.SemaphoreType.DMA
    return pl.pallas_call(
        functools.partial(kernel, dims),
        out_shape=jax.ShapeDtypeStruct((height, half), jnp.float32),
        in_specs=[pl.BlockSpec(memory_space=pl.ANY)] * 2,
        out_specs=pl.BlockSpec(memory_space=pltpu.VMEM),
        scratch_shapes=[
            pltpu.VMEM((tiles_r * tiles_c, EDGE, EDGE), jnp.bfloat16),
            pltpu.VMEM((live + 1, EDGE, EDGE), jnp.bfloat16),
            pltpu.VMEM((n_row, height, half), jnp.bfloat16),
            pltpu.VMEM((height, half), jnp.float32),
            pltpu.SMEM((n_col, tiles_r, tiles_c), jnp.int32),
            pltpu.SMEM((tiles_r * tiles_c,), jnp.int32),
            pltpu.VMEM((n_row, 1, width), jnp.float32),
            pltpu.VMEM((n_col, 1, width), jnp.float32),
            pltpu.VMEM((n_row, 1, half), jnp.float32),
            *[pltpu.VMEM((live + 1, EDGE, EDGE), jnp.bfloat16)] * (2 * steps),
            dma((2,)),
            dma((2, steps, CHUNKS)),
            dma((2, steps, CHUNKS)),
            dma((2, steps, CHUNKS, n_layer - 1)),
            dma((2, steps, CHUNKS, n_layer - 1)),
            dma((n_row,)),
            dma((n_row,)),
            dma((2, steps)),
            dma((2, steps)),
            dma((n_row - 1,)),
            dma((n_row - 1,)),
            dma((2, steps)),
            dma((2, steps)),
            dma((n_row - 1,)),
            dma((n_row - 1,)),
        ],
        compiler_params=pltpu.CompilerParams(
            collective_id=0, has_side_effects=True, vmem_limit_bytes=56 * 2**20
        ),
        name="markov_step",
    )(values, tile_mask)


def solution(mesh):
    return jax.shard_map(
        shards,
        mesh=mesh,
        in_specs=(P("row", "col"), P("row", "col")),
        out_specs=P("row", ("col", "layer")),
        check_vma=False,
    )
```

```python
import functools

import jax
import jax.numpy as jnp
from jax import lax
from jax.experimental import pallas as pl
from jax.experimental.pallas import tpu as pltpu
from jax.sharding import PartitionSpec as P

MESH = pl.DeviceIdType.MESH
EDGE = 128
CHUNKS = 4


def kernel(
    dims, v_ref, m_ref, out_ref,
    by_tile, pack, rbuf, acc, mask_all, ranks, mpart, mass, wpart, *rest,
):
    n_row, n_col, n_layer, tiles_r, tiles_c, live = dims
    steps = n_col - 1
    from_left = rest[:steps]
    from_right = rest[steps : 2 * steps]
    (in_sem, z_send, z_recv, y_send, y_recv, x_send, x_recv, mask_send, mask_recv,
     mp_send, mp_recv, ms_send, ms_recv, w_send, w_recv) = rest[2 * steps :]
    height, width = tiles_r * EDGE, tiles_c * EDGE
    half = width // n_layer
    half_tiles = tiles_c // n_layer
    tiles = tiles_r * tiles_c
    part = live // n_layer
    chunk = part // CHUNKS
    per = height // width
    r = lax.axis_index("row")
    c = lax.axis_index("col")
    l = lax.axis_index("layer")

    barrier = pltpu.get_barrier_semaphore()
    for axis, me, size in (("row", r, n_row), ("layer", l, n_layer)):
        for j in range(1, size):
            pl.semaphore_signal(
                barrier, inc=1, device_id={axis: lax.rem(me + j, size)}, device_id_type=MESH
            )

    @pl.when(c > 0)
    def _():
        pl.semaphore_signal(barrier, inc=1, device_id={"col": c - 1}, device_id_type=MESH)

    @pl.when(c + 1 < n_col)
    def _():
        pl.semaphore_signal(barrier, inc=1, device_id={"col": c + 1}, device_id_type=MESH)

    mask_in = pltpu.make_async_copy(m_ref, mask_all.at[c], in_sem.at[0])
    mask_in.start()
    for t in range(tiles):
        tr, tc = t // tiles_c, t % tiles_c
        pltpu.make_async_copy(
            v_ref.at[tr * EDGE : (tr + 1) * EDGE, tc * EDGE : (tc + 1) * EDGE],
            by_tile.at[t], in_sem.at[1],
        ).start()
    zero_tile = jnp.zeros((EDGE, EDGE), jnp.bfloat16)
    for buf in (pack, *from_left, *from_right):
        buf[live] = zero_tile
    acc[...] = jnp.zeros_like(acc)
    mask_in.wait()

    def rank_list(flags):
        count = jnp.int32(0)
        out = []
        for flag in flags:
            out.append(flag * count + (1 - flag) * live)
            count = count + flag
        return out

    flags = [mask_all[c, t // tiles_c, t % tiles_c] for t in range(tiles)]
    count = jnp.int32(0)
    upto = []
    for t in range(tiles):
        count = count + flags[t]
        upto.append(count)
    pltpu.make_async_copy(by_tile, by_tile, in_sem.at[1]).wait()
    for s in range(live):
        index = jnp.int32(0)
        for t in range(tiles - 1):
            index = index + lax.select(upto[t] <= s, jnp.int32(1), jnp.int32(0))
        pack[s] = by_tile[index]
    own_ranks = rank_list(flags)
    for t in range(tiles):
        ranks[t] = own_ranks[t]

    for tc in range(tiles_c):
        total = jnp.zeros((EDGE, EDGE), jnp.float32)
        for tr in range(tiles_r):
            total = total + pack[own_ranks[tr * tiles_c + tc]].astype(jnp.float32)
        mpart[r, :, tc * EDGE : (tc + 1) * EDGE] = jnp.sum(total, axis=0, keepdims=True)

    for tr in range(tiles_r):
        for j in range(half_tiles):
            rank = ranks[tr * tiles_c + l * half_tiles + j]
            rbuf[r, tr * EDGE : (tr + 1) * EDGE, j * EDGE : (j + 1) * EDGE] = pack[rank]

    neighbours = lax.select(c > 0, 1, 0) + lax.select(c + 1 < n_col, 1, 0)
    pl.semaphore_wait(barrier, n_row - 1 + n_layer - 1 + neighbours)

    sends = []

    def slots(layer, ch):
        return pl.ds(layer * part + ch * chunk, chunk)

    def z_copy(way, s, ch):
        bufs = from_left if way == 0 else from_right
        src = pack if s == 1 else bufs[s - 2]
        where = slots(l, ch)
        return pltpu.make_async_remote_copy(
            src_ref=src.at[where], dst_ref=bufs[s - 1].at[where],
            send_sem=z_send.at[way, s - 1, ch], recv_sem=z_recv.at[way, s - 1, ch],
            device_id={"col": c + 1 if way == 0 else c - 1}, device_id_type=MESH,
        )

    def y_copy(way, s, ch, j, layer):
        buf = (from_left if way == 0 else from_right)[s - 1]
        where = slots(layer, ch)
        return pltpu.make_async_remote_copy(
            src_ref=buf.at[where], dst_ref=buf.at[where],
            send_sem=y_send.at[way, s - 1, ch, j - 1], recv_sem=y_recv.at[way, s - 1, ch, j - 1],
            device_id={"layer": lax.rem(l + j, n_layer)}, device_id_type=MESH,
        )

    def here(way, s):
        return c >= s if way == 0 else c + s < n_col

    def sends_on(way, s):
        if way == 0:
            return (c + 1 < n_col) & (c >= s - 1)
        return (c >= 1) & (c + s - 1 < n_col)

    def z_start(s, ch):
        for way in (0, 1):
            @pl.when(sends_on(way, s))
            def _():
                z_copy(way, s, ch).start()

    for ch in range(CHUNKS):
        z_start(1, ch)

    def to_peers(axis, me, size, ref, send, recv):
        copies = []
        for j in range(1, size):
            copy = pltpu.make_async_remote_copy(
                src_ref=ref.at[me], dst_ref=ref.at[me],
                send_sem=send.at[j - 1], recv_sem=recv.at[j - 1],
                device_id={axis: lax.rem(me + j, size)}, device_id_type=MESH,
            )
            copy.start()
            sends.append(copy)
            copies.append(copy)
        return copies

    def hand_on(ref, send, recv, way, s):
        block = c - (s - 1) if way == 0 else c + (s - 1)
        return pltpu.make_async_remote_copy(
            src_ref=ref.at[block], dst_ref=ref.at[block],
            send_sem=send.at[way, s - 1], recv_sem=recv.at[way, s - 1],
            device_id={"col": c + 1 if way == 0 else c - 1}, device_id_type=MESH,
        )

    def received(ref, send, recv, way, s):
        block = c - s if way == 0 else c + s
        return pltpu.make_async_remote_copy(
            src_ref=ref.at[block], dst_ref=ref.at[block],
            send_sem=send.at[way, s - 1], recv_sem=recv.at[way, s - 1],
            device_id={"col": c + 1 if way == 0 else c - 1}, device_id_type=MESH,
        )

    small = ((mask_all, mask_send, mask_recv), (mass, ms_send, ms_recv))

    mp_copies = to_peers("row", r, n_row, mpart, mp_send, mp_recv)
    for way in (0, 1):
        @pl.when(sends_on(way, 1))
        def _():
            hand_on(*small[0], way, 1).start()

    sibling = r + 1 - 2 * lax.rem(r, 2)
    pairs = n_row // 2

    def x_copy(k, section, target):
        return pltpu.make_async_remote_copy(
            src_ref=rbuf.at[section], dst_ref=rbuf.at[section],
            send_sem=x_send.at[k], recv_sem=x_recv.at[k],
            device_id={"row": target}, device_id_type=MESH,
        )

    across = [lax.rem(r + 2 * j, n_row) for j in range(1, pairs)]
    for j, target in enumerate(across):
        x_copy(1 + j, r, target).start()
    x_copy(0, r, sibling).start()

    for copy in mp_copies:
        copy.wait_recv()
    total = mpart[0]
    for j in range(1, n_row):
        total = total + mpart[j]
    mass[c] = total
    for way in (0, 1):
        @pl.when(sends_on(way, 1))
        def _():
            hand_on(*small[1], way, 1).start()

    def forward(s):
        for ch in range(CHUNKS):
            for way in (0, 1):
                @pl.when(here(way, s))
                def _():
                    z_copy(way, s, ch).wait_recv()
                    if s < steps:
                        @pl.when(sends_on(way, s + 1))
                        def _():
                            z_copy(way, s + 1, ch).start()
                    for j in range(1, n_layer):
                        y_copy(way, s, ch, j, l).start()
        for way in (0, 1):
            @pl.when(here(way, s))
            def _():
                for group in small:
                    received(*group, way, s).wait_recv()
                if s < steps:
                    @pl.when(sends_on(way, s + 1))
                    def _():
                        for group in small:
                            hand_on(*group, way, s + 1).start()

    def product(buf, block):
        scale = 1.0 / mass[block]
        flags = [mask_all[block, t // tiles_c, t % tiles_c] for t in range(tiles)]
        local = rank_list(flags)
        section, offset = block // per, (block % per) * width
        right = rbuf[section, pl.ds(pl.multiple_of(offset, EDGE), width), :]
        rows_at_once = min(tiles_r, 4)
        for first in range(0, tiles_r, rows_at_once):
            rows = []
            for tr in range(first, first + rows_at_once):
                row = []
                for tc in range(tiles_c):
                    tile = buf[local[tr * tiles_c + tc]].astype(jnp.float32)
                    row.append((tile * scale[:, tc * EDGE : (tc + 1) * EDGE]).astype(jnp.bfloat16))
                rows.append(jnp.concatenate(row, axis=1))
            left = jnp.concatenate(rows, axis=0)
            span = slice(first * EDGE, (first + rows_at_once) * EDGE)
            acc[span, :] += jnp.dot(left, right, preferred_element_type=jnp.float32)

    def foreign(s):
        for way in (0, 1):
            @pl.when(here(way, s))
            def _():
                for ch in range(CHUNKS):
                    for j in range(1, n_layer):
                        y_copy(way, s, ch, j, lax.rem(l + n_layer - j, n_layer)).wait_recv()
                product(
                    (from_left if way == 0 else from_right)[s - 1],
                    c - s if way == 0 else c + s,
                )

    for s in range(1, max(steps, 2)):
        forward(s)
    for j, target in enumerate(across):
        x_copy(1 + j, lax.rem(r + n_row - 2 * (j + 1), n_row), target).wait_recv()
        x_copy(pairs + j, lax.rem(r + n_row - 2 * (j + 1), n_row), sibling).start()
    x_copy(0, sibling, sibling).wait_recv()
    for j in range(len(across)):
        x_copy(pairs + j, lax.rem(sibling + n_row - 2 * (j + 1), n_row), sibling).wait_recv()
    product(pack, c)
    for s in range(1, steps - 1):
        foreign(s)
    if steps >= 2:
        forward(steps)
    for s in range(max(steps - 1, 1), steps + 1):
        foreign(s)

    inflated = acc[...] * acc[...]
    acc[...] = inflated
    wpart[r] = jnp.sum(inflated, axis=0, keepdims=True)
    for copy in to_peers("row", r, n_row, wpart, w_send, w_recv):
        copy.wait_recv()
    total = wpart[0]
    for j in range(1, n_row):
        total = total + wpart[j]
    out_ref[...] = acc[...] * ((height * n_row * 1.0) / total)

    for copy in sends:
        copy.wait_send()
    for j, target in enumerate(across):
        x_copy(1 + j, r, target).wait_send()
        x_copy(pairs + j, r, sibling).wait_send()
    x_copy(0, r, sibling).wait_send()
    for s in range(1, steps + 1):
        for way in (0, 1):
            @pl.when(sends_on(way, s))
            def _():
                for ch in range(CHUNKS):
                    z_copy(way, s, ch).wait_send()
                for group in small:
                    hand_on(*group, way, s).wait_send()

            @pl.when(here(way, s))
            def _():
                for ch in range(CHUNKS):
                    for j in range(1, n_layer):
                        y_copy(way, s, ch, j, l).wait_send()


def shards(values, tile_mask):
    n_row, n_col, n_layer = (lax.axis_size(a) for a in ("row", "col", "layer"))
    height, width = values.shape
    tiles_r, tiles_c = tile_mask.shape
    live = tiles_r * tiles_c // 2
    half = width // n_layer
    dims = (n_row, n_col, n_layer, tiles_r, tiles_c, live)
    steps = n_col - 1
    dma = pltpu.SemaphoreType.DMA
    return pl.pallas_call(
        functools.partial(kernel, dims),
        out_shape=jax.ShapeDtypeStruct((height, half), jnp.float32),
        in_specs=[pl.BlockSpec(memory_space=pl.ANY)] * 2,
        out_specs=pl.BlockSpec(memory_space=pltpu.VMEM),
        scratch_shapes=[
            pltpu.VMEM((tiles_r * tiles_c, EDGE, EDGE), jnp.bfloat16),
            pltpu.VMEM((live + 1, EDGE, EDGE), jnp.bfloat16),
            pltpu.VMEM((n_row, height, half), jnp.bfloat16),
            pltpu.VMEM((height, half), jnp.float32),
            pltpu.SMEM((n_col, tiles_r, tiles_c), jnp.int32),
            pltpu.SMEM((tiles_r * tiles_c,), jnp.int32),
            pltpu.VMEM((n_row, 1, width), jnp.float32),
            pltpu.VMEM((n_col, 1, width), jnp.float32),
            pltpu.VMEM((n_row, 1, half), jnp.float32),
            *[pltpu.VMEM((live + 1, EDGE, EDGE), jnp.bfloat16)] * (2 * steps),
            dma((2,)),
            dma((2, steps, CHUNKS)),
            dma((2, steps, CHUNKS)),
            dma((2, steps, CHUNKS, n_layer - 1)),
            dma((2, steps, CHUNKS, n_layer - 1)),
            dma((n_row,)),
            dma((n_row,)),
            dma((2, steps)),
            dma((2, steps)),
            dma((n_row - 1,)),
            dma((n_row - 1,)),
            dma((2, steps)),
            dma((2, steps)),
            dma((n_row - 1,)),
            dma((n_row - 1,)),
        ],
        compiler_params=pltpu.CompilerParams(
            collective_id=0, has_side_effects=True, vmem_limit_bytes=56 * 2**20
        ),
        name="markov_step",
    )(values, tile_mask)


def solution(mesh):
    return jax.shard_map(
        shards,
        mesh=mesh,
        in_specs=(P("row", "col"), P("row", "col")),
        out_specs=P("row", ("col", "layer")),
        check_vma=False,
    )
```

```python
import functools

import jax
import jax.numpy as jnp
from jax import lax
from jax.experimental import pallas as pl
from jax.experimental.pallas import tpu as pltpu
from jax.sharding import PartitionSpec as P

MESH = pl.DeviceIdType.MESH
EDGE = 128
CHUNKS = 2


def kernel(
    dims, v_ref, m_ref, acc, scale_ref,
    by_tile, pack, rbuf, left, mask, ranks, mpart, mass, wpart, *rest,
):
    n_row, n_col, n_layer, tiles_r, tiles_c, live = dims
    steps = n_col - 1
    from_left = rest[:steps]
    from_right = from_left[::-1]
    (in_sem, z_send, z_recv, y_send, y_recv, x_send, x_recv, rank_send, rank_recv,
     mp_send, mp_recv, ms_send, ms_recv, w_send, w_recv) = rest[steps:]
    height, width = tiles_r * EDGE, tiles_c * EDGE
    half = width // n_layer
    half_tiles = tiles_c // n_layer
    tiles = tiles_r * tiles_c
    part = live // n_layer
    chunk = part // CHUNKS
    per = height // width
    r = lax.axis_index("row")
    c = lax.axis_index("col")
    l = lax.axis_index("layer")

    barrier = pltpu.get_barrier_semaphore()
    for axis, me, size in (("row", r, n_row), ("layer", l, n_layer)):
        for j in range(1, size):
            pl.semaphore_signal(
                barrier, inc=1, device_id={axis: lax.rem(me + j, size)}, device_id_type=MESH
            )

    @pl.when(c > 0)
    def _():
        pl.semaphore_signal(barrier, inc=1, device_id={"col": c - 1}, device_id_type=MESH)

    @pl.when(c + 1 < n_col)
    def _():
        pl.semaphore_signal(barrier, inc=1, device_id={"col": c + 1}, device_id_type=MESH)

    mask_in = pltpu.make_async_copy(m_ref, mask, in_sem.at[0])
    mask_in.start()
    for t in range(tiles):
        tr, tc = t // tiles_c, t % tiles_c
        pltpu.make_async_copy(
            v_ref.at[tr * EDGE : (tr + 1) * EDGE, tc * EDGE : (tc + 1) * EDGE],
            by_tile.at[t], in_sem.at[1],
        ).start()
    zero_tile = jnp.zeros((EDGE, EDGE), jnp.bfloat16)
    for buf in (pack, *from_left):
        buf[live] = zero_tile
    acc[...] = jnp.zeros_like(acc)
    mask_in.wait()

    def rank_list(flags):
        count = jnp.int32(0)
        out = []
        for flag in flags:
            out.append(flag * count + (1 - flag) * live)
            count = count + flag
        return out

    flags = [mask[t // tiles_c, t % tiles_c] for t in range(tiles)]
    count = jnp.int32(0)
    upto = []
    for t in range(tiles):
        count = count + flags[t]
        upto.append(count)
    pltpu.make_async_copy(by_tile, by_tile, in_sem.at[1]).wait()
    for s in range(live):
        index = jnp.int32(0)
        for t in range(tiles - 1):
            index = index + lax.select(upto[t] <= s, jnp.int32(1), jnp.int32(0))
        pack[s] = by_tile[index]
    own_ranks = rank_list(flags)
    for t in range(tiles):
        ranks[c, t // tiles_c, t % tiles_c] = own_ranks[t]

    for tc in range(tiles_c):
        total = jnp.zeros((EDGE, EDGE), jnp.float32)
        for tr in range(tiles_r):
            total = total + pack[own_ranks[tr * tiles_c + tc]].astype(jnp.float32)
        mpart[r, :, tc * EDGE : (tc + 1) * EDGE] = jnp.sum(total, axis=0, keepdims=True)

    for tr in range(tiles_r):
        for j in range(half_tiles):
            rank = ranks[c, tr, l * half_tiles + j]
            rbuf[r, tr * EDGE : (tr + 1) * EDGE, j * EDGE : (j + 1) * EDGE] = pack[rank]

    neighbours = lax.select(c > 0, 1, 0) + lax.select(c + 1 < n_col, 1, 0)
    pl.semaphore_wait(barrier, n_row - 1 + n_layer - 1 + neighbours)

    sends = []

    def slots(layer, ch):
        return pl.ds(layer * part + ch * chunk, chunk)

    def z_copy(way, s, ch):
        bufs = from_left if way == 0 else from_right
        src = pack if s == 1 else bufs[s - 2]
        where = slots(l, ch)
        return pltpu.make_async_remote_copy(
            src_ref=src.at[where], dst_ref=bufs[s - 1].at[where],
            send_sem=z_send.at[way, s - 1, ch], recv_sem=z_recv.at[way, s - 1, ch],
            device_id={"col": c + 1 if way == 0 else c - 1}, device_id_type=MESH,
        )

    def y_copy(way, s, ch, j, layer):
        buf = (from_left if way == 0 else from_right)[s - 1]
        where = slots(layer, ch)
        return pltpu.make_async_remote_copy(
            src_ref=buf.at[where], dst_ref=buf.at[where],
            send_sem=y_send.at[way, s - 1, ch, j - 1], recv_sem=y_recv.at[way, s - 1, ch, j - 1],
            device_id={"layer": lax.rem(l + j, n_layer)}, device_id_type=MESH,
        )

    def here(way, s):
        return c >= s if way == 0 else c + s < n_col

    def sends_on(way, s):
        if way == 0:
            return (c + 1 < n_col) & (c >= s - 1)
        return (c >= 1) & (c + s - 1 < n_col)

    def z_start(s, ch):
        for way in (0, 1):
            @pl.when(sends_on(way, s))
            def _():
                z_copy(way, s, ch).start()

    for ch in range(CHUNKS):
        z_start(1, ch)

    def to_peers(axis, me, size, ref, send, recv):
        copies = []
        for j in range(1, size):
            copy = pltpu.make_async_remote_copy(
                src_ref=ref.at[me], dst_ref=ref.at[me],
                send_sem=send.at[j - 1], recv_sem=recv.at[j - 1],
                device_id={axis: lax.rem(me + j, size)}, device_id_type=MESH,
            )
            copy.start()
            sends.append(copy)
            copies.append(copy)
        return copies

    def hand_on(ref, send, recv, way, s):
        block = c - (s - 1) if way == 0 else c + (s - 1)
        return pltpu.make_async_remote_copy(
            src_ref=ref.at[block], dst_ref=ref.at[block],
            send_sem=send.at[way, s - 1], recv_sem=recv.at[way, s - 1],
            device_id={"col": c + 1 if way == 0 else c - 1}, device_id_type=MESH,
        )

    def received(ref, send, recv, way, s):
        block = c - s if way == 0 else c + s
        return pltpu.make_async_remote_copy(
            src_ref=ref.at[block], dst_ref=ref.at[block],
            send_sem=send.at[way, s - 1], recv_sem=recv.at[way, s - 1],
            device_id={"col": c + 1 if way == 0 else c - 1}, device_id_type=MESH,
        )

    small = ((ranks, rank_send, rank_recv), (mass, ms_send, ms_recv))

    mp_copies = to_peers("row", r, n_row, mpart, mp_send, mp_recv)
    for way in (0, 1):
        @pl.when(sends_on(way, 1))
        def _():
            hand_on(*small[0], way, 1).start()

    sibling = r + 1 - 2 * lax.rem(r, 2)
    pairs = n_row // 2

    def x_copy(k, section, target):
        return pltpu.make_async_remote_copy(
            src_ref=rbuf.at[section], dst_ref=rbuf.at[section],
            send_sem=x_send.at[k], recv_sem=x_recv.at[k],
            device_id={"row": target}, device_id_type=MESH,
        )

    across = [lax.rem(r + 2 * j, n_row) for j in range(1, pairs)]
    for j, target in enumerate(across):
        x_copy(1 + j, r, target).start()
    x_copy(0, r, sibling).start()

    for copy in mp_copies:
        copy.wait_recv()
    total = mpart[0]
    for j in range(1, n_row):
        total = total + mpart[j]
    mass[c] = total
    for way in (0, 1):
        @pl.when(sends_on(way, 1))
        def _():
            hand_on(*small[1], way, 1).start()

    def forward(s):
        for ch in range(CHUNKS):
            for way in (0, 1):
                @pl.when(here(way, s))
                def _():
                    z_copy(way, s, ch).wait_recv()
                    if s < steps:
                        @pl.when(sends_on(way, s + 1))
                        def _():
                            z_copy(way, s + 1, ch).start()
                    for j in range(1, n_layer):
                        y_copy(way, s, ch, j, l).start()
        for way in (0, 1):
            @pl.when(here(way, s))
            def _():
                for group in small:
                    received(*group, way, s).wait_recv()
                if s < steps:
                    @pl.when(sends_on(way, s + 1))
                    def _():
                        for group in small:
                            hand_on(*group, way, s + 1).start()

    def unpack(buf, block):
        scale = 1.0 / mass[block]

        def tile_row(tr, carry):
            rows = pl.ds(pl.multiple_of(tr * EDGE, EDGE), EDGE)
            for tc in range(tiles_c):
                cols = slice(tc * EDGE, (tc + 1) * EDGE)
                tile = buf[ranks[block, tr, tc]].astype(jnp.float32)
                left[block, rows, cols] = (tile * scale[:, cols]).astype(jnp.bfloat16)
            return carry

        lax.fori_loop(0, tiles_r, tile_row, 0)

    def foreign(s):
        for way in (0, 1):
            @pl.when(here(way, s))
            def _():
                for ch in range(CHUNKS):
                    for j in range(1, n_layer):
                        y_copy(way, s, ch, j, lax.rem(l + n_layer - j, n_layer)).wait_recv()
                unpack(
                    (from_left if way == 0 else from_right)[s - 1],
                    c - s if way == 0 else c + s,
                )

    chunk_rows = min(height, 512)

    def products(near, far):
        def one(block, carry):
            distance = jnp.abs(block - c)

            @pl.when((distance >= near) & (distance < far))
            def _():
                section, offset = block // per, (block % per) * width
                right = rbuf[section, pl.ds(pl.multiple_of(offset, EDGE), width), :]

                def rows(i, inner):
                    span = pl.ds(pl.multiple_of(i * chunk_rows, EDGE), chunk_rows)
                    acc[span, :] += jnp.dot(
                        left[block, span, :], right, preferred_element_type=jnp.float32
                    )
                    return inner

                lax.fori_loop(0, height // chunk_rows, rows, 0)

            return carry

        lax.fori_loop(0, n_col, one, 0)

    for s in range(1, max(steps, 2)):
        forward(s)
    for j, target in enumerate(across):
        x_copy(1 + j, lax.rem(r + n_row - 2 * (j + 1), n_row), target).wait_recv()
        x_copy(pairs + j, lax.rem(r + n_row - 2 * (j + 1), n_row), sibling).start()
    x_copy(0, sibling, sibling).wait_recv()
    for j in range(len(across)):
        x_copy(pairs + j, lax.rem(sibling + n_row - 2 * (j + 1), n_row), sibling).wait_recv()
    unpack(pack, c)
    for s in range(1, steps - 1):
        foreign(s)
    products(0, max(steps - 1, 1))
    if steps >= 2:
        forward(steps)
    for s in range(max(steps - 1, 1), steps + 1):
        foreign(s)
    products(max(steps - 1, 1), n_col)

    inflated = acc[...] * acc[...]
    acc[...] = inflated
    wpart[r] = jnp.sum(inflated, axis=0, keepdims=True)
    for copy in to_peers("row", r, n_row, wpart, w_send, w_recv):
        copy.wait_recv()
    total = wpart[0]
    for j in range(1, n_row):
        total = total + wpart[j]
    scale_ref[...] = (height * n_row * 1.0) / total

    for copy in sends:
        copy.wait_send()
    for j, target in enumerate(across):
        x_copy(1 + j, r, target).wait_send()
        x_copy(pairs + j, r, sibling).wait_send()
    x_copy(0, r, sibling).wait_send()
    for s in range(1, steps + 1):
        for way in (0, 1):
            @pl.when(sends_on(way, s))
            def _():
                for ch in range(CHUNKS):
                    z_copy(way, s, ch).wait_send()
                for group in small:
                    hand_on(*group, way, s).wait_send()

            @pl.when(here(way, s))
            def _():
                for ch in range(CHUNKS):
                    for j in range(1, n_layer):
                        y_copy(way, s, ch, j, l).wait_send()


def scaled(inflated_ref, scale_ref, out_ref):
    out_ref[...] = inflated_ref[...] * scale_ref[...]


def shards(values, tile_mask):
    n_row, n_col, n_layer = (lax.axis_size(a) for a in ("row", "col", "layer"))
    height, width = values.shape
    tiles_r, tiles_c = tile_mask.shape
    live = tiles_r * tiles_c // 2
    half = width // n_layer
    dims = (n_row, n_col, n_layer, tiles_r, tiles_c, live)
    steps = n_col - 1
    dma = pltpu.SemaphoreType.DMA
    inflated, scale = pl.pallas_call(
        functools.partial(kernel, dims),
        out_shape=(
            pltpu.VMEM((height, half), jnp.float32),
            pltpu.VMEM((1, half), jnp.float32),
        ),
        in_specs=[pl.BlockSpec(memory_space=pl.ANY)] * 2,
        out_specs=(pl.BlockSpec(memory_space=pltpu.VMEM),) * 2,
        scratch_shapes=[
            pltpu.VMEM((tiles_r * tiles_c, EDGE, EDGE), jnp.bfloat16),
            pltpu.VMEM((live + 1, EDGE, EDGE), jnp.bfloat16),
            pltpu.VMEM((n_row, height, half), jnp.bfloat16),
            pltpu.VMEM((n_col, height, width), jnp.bfloat16),
            pltpu.SMEM((tiles_r, tiles_c), jnp.int32),
            pltpu.SMEM((n_col, tiles_r, tiles_c), jnp.int32),
            pltpu.VMEM((n_row, 1, width), jnp.float32),
            pltpu.VMEM((n_col, 1, width), jnp.float32),
            pltpu.VMEM((n_row, 1, half), jnp.float32),
            *[pltpu.VMEM((live + 1, EDGE, EDGE), jnp.bfloat16)] * steps,
            dma((2,)),
            dma((2, steps, CHUNKS)),
            dma((2, steps, CHUNKS)),
            dma((2, steps, CHUNKS, n_layer - 1)),
            dma((2, steps, CHUNKS, n_layer - 1)),
            dma((n_row,)),
            dma((n_row,)),
            dma((2, steps)),
            dma((2, steps)),
            dma((n_row - 1,)),
            dma((n_row - 1,)),
            dma((2, steps)),
            dma((2, steps)),
            dma((n_row - 1,)),
            dma((n_row - 1,)),
        ],
        compiler_params=pltpu.CompilerParams(
            collective_id=0, has_side_effects=True, vmem_limit_bytes=56 * 2**20
        ),
        name="markov_step",
    )(values, tile_mask)
    return pl.pallas_call(
        scaled,
        out_shape=jax.ShapeDtypeStruct((height, half), jnp.float32),
        in_specs=[pl.BlockSpec(memory_space=pltpu.VMEM)] * 2,
        out_specs=pl.BlockSpec(memory_space=pltpu.VMEM),
        compiler_params=pltpu.CompilerParams(vmem_limit_bytes=8 * 2**20),
        name="scaled",
    )(inflated, scale)


def solution(mesh):
    return jax.shard_map(
        shards,
        mesh=mesh,
        in_specs=(P("row", "col"), P("row", "col")),
        out_specs=P("row", ("col", "layer")),
        check_vma=False,
    )
```

```python
import functools

import jax
import jax.numpy as jnp
from jax import lax
from jax.experimental import pallas as pl
from jax.experimental.pallas import tpu as pltpu
from jax.sharding import PartitionSpec as P

MESH = pl.DeviceIdType.MESH
EDGE = 128
CHUNKS = 2


def kernel(
    dims, v_ref, m_ref, acc, scale_ref,
    by_tile, pack, rbuf, left, mask, ranks, mpart, mass, wpart, *rest,
):
    n_row, n_col, n_layer, tiles_r, tiles_c, live = dims
    steps = n_col - 1
    from_left = rest[:steps]
    from_right = from_left[::-1]
    (in_sem, z_send, z_recv, y_send, y_recv, x_send, x_recv, rank_send, rank_recv,
     mp_send, mp_recv, ms_send, ms_recv, w_send, w_recv) = rest[steps:]
    height, width = tiles_r * EDGE, tiles_c * EDGE
    half = width // n_layer
    half_tiles = tiles_c // n_layer
    tiles = tiles_r * tiles_c
    part = live // n_layer
    chunk = part // CHUNKS
    per = height // width
    r = lax.axis_index("row")
    c = lax.axis_index("col")
    l = lax.axis_index("layer")

    barrier = pltpu.get_barrier_semaphore()
    for axis, me, size in (("row", r, n_row), ("layer", l, n_layer)):
        for j in range(1, size):
            pl.semaphore_signal(
                barrier, inc=1, device_id={axis: lax.rem(me + j, size)}, device_id_type=MESH
            )

    @pl.when(c > 0)
    def _():
        pl.semaphore_signal(barrier, inc=1, device_id={"col": c - 1}, device_id_type=MESH)

    @pl.when(c + 1 < n_col)
    def _():
        pl.semaphore_signal(barrier, inc=1, device_id={"col": c + 1}, device_id_type=MESH)

    mask_in = pltpu.make_async_copy(m_ref, mask, in_sem.at[0])
    mask_in.start()
    for t in range(tiles):
        tr, tc = t // tiles_c, t % tiles_c
        pltpu.make_async_copy(
            v_ref.at[tr * EDGE : (tr + 1) * EDGE, tc * EDGE : (tc + 1) * EDGE],
            by_tile.at[t], in_sem.at[1],
        ).start()
    zero_tile = jnp.zeros((EDGE, EDGE), jnp.bfloat16)
    for buf in (pack, *from_left):
        buf[live] = zero_tile
    acc[...] = jnp.zeros_like(acc)
    mask_in.wait()

    def rank_list(flags):
        count = jnp.int32(0)
        out = []
        for flag in flags:
            out.append(flag * count + (1 - flag) * live)
            count = count + flag
        return out

    flags = [mask[t // tiles_c, t % tiles_c] for t in range(tiles)]
    count = jnp.int32(0)
    upto = []
    for t in range(tiles):
        count = count + flags[t]
        upto.append(count)
    pltpu.make_async_copy(by_tile, by_tile, in_sem.at[1]).wait()
    for s in range(live):
        index = jnp.int32(0)
        for t in range(tiles - 1):
            index = index + lax.select(upto[t] <= s, jnp.int32(1), jnp.int32(0))
        pack[s] = by_tile[index]
    own_ranks = rank_list(flags)
    for t in range(tiles):
        ranks[c, t // tiles_c, t % tiles_c] = own_ranks[t]

    neighbours = lax.select(c > 0, 1, 0) + lax.select(c + 1 < n_col, 1, 0)
    pl.semaphore_wait(barrier, n_row - 1 + n_layer - 1 + neighbours)

    sends = []

    def slots(layer, ch):
        return pl.ds(layer * part + ch * chunk, chunk)

    def z_copy(way, s, ch):
        bufs = from_left if way == 0 else from_right
        src = pack if s == 1 else bufs[s - 2]
        where = slots(l, ch)
        return pltpu.make_async_remote_copy(
            src_ref=src.at[where], dst_ref=bufs[s - 1].at[where],
            send_sem=z_send.at[way, s - 1, ch], recv_sem=z_recv.at[way, s - 1, ch],
            device_id={"col": c + 1 if way == 0 else c - 1}, device_id_type=MESH,
        )

    def y_copy(way, s, ch, j, layer):
        buf = (from_left if way == 0 else from_right)[s - 1]
        where = slots(layer, ch)
        return pltpu.make_async_remote_copy(
            src_ref=buf.at[where], dst_ref=buf.at[where],
            send_sem=y_send.at[way, s - 1, ch, j - 1], recv_sem=y_recv.at[way, s - 1, ch, j - 1],
            device_id={"layer": lax.rem(l + j, n_layer)}, device_id_type=MESH,
        )

    def here(way, s):
        return c >= s if way == 0 else c + s < n_col

    def sends_on(way, s):
        if way == 0:
            return (c + 1 < n_col) & (c >= s - 1)
        return (c >= 1) & (c + s - 1 < n_col)

    def z_start(s, ch):
        for way in (0, 1):
            @pl.when(sends_on(way, s))
            def _():
                z_copy(way, s, ch).start()

    z_start(1, 0)

    def to_peers(axis, me, size, ref, send, recv):
        copies = []
        for j in range(1, size):
            copy = pltpu.make_async_remote_copy(
                src_ref=ref.at[me], dst_ref=ref.at[me],
                send_sem=send.at[j - 1], recv_sem=recv.at[j - 1],
                device_id={axis: lax.rem(me + j, size)}, device_id_type=MESH,
            )
            copy.start()
            sends.append(copy)
            copies.append(copy)
        return copies

    def hand_on(ref, send, recv, way, s):
        block = c - (s - 1) if way == 0 else c + (s - 1)
        return pltpu.make_async_remote_copy(
            src_ref=ref.at[block], dst_ref=ref.at[block],
            send_sem=send.at[way, s - 1], recv_sem=recv.at[way, s - 1],
            device_id={"col": c + 1 if way == 0 else c - 1}, device_id_type=MESH,
        )

    def received(ref, send, recv, way, s):
        block = c - s if way == 0 else c + s
        return pltpu.make_async_remote_copy(
            src_ref=ref.at[block], dst_ref=ref.at[block],
            send_sem=send.at[way, s - 1], recv_sem=recv.at[way, s - 1],
            device_id={"col": c + 1 if way == 0 else c - 1}, device_id_type=MESH,
        )

    small = ((ranks, rank_send, rank_recv), (mass, ms_send, ms_recv))

    for way in (0, 1):
        @pl.when(sends_on(way, 1))
        def _():
            hand_on(*small[0], way, 1).start()

    for tc in range(tiles_c):
        total = jnp.zeros((EDGE, EDGE), jnp.float32)
        for tr in range(tiles_r):
            total = total + pack[own_ranks[tr * tiles_c + tc]].astype(jnp.float32)
        mpart[r, :, tc * EDGE : (tc + 1) * EDGE] = jnp.sum(total, axis=0, keepdims=True)

    mp_copies = to_peers("row", r, n_row, mpart, mp_send, mp_recv)

    for tr in range(tiles_r):
        for j in range(half_tiles):
            rank = ranks[c, tr, l * half_tiles + j]
            rbuf[r, tr * EDGE : (tr + 1) * EDGE, j * EDGE : (j + 1) * EDGE] = pack[rank]

    sibling = r + 1 - 2 * lax.rem(r, 2)
    pairs = n_row // 2

    def x_copy(k, section, target):
        return pltpu.make_async_remote_copy(
            src_ref=rbuf.at[section], dst_ref=rbuf.at[section],
            send_sem=x_send.at[k], recv_sem=x_recv.at[k],
            device_id={"row": target}, device_id_type=MESH,
        )

    across = [lax.rem(r + 2 * j, n_row) for j in range(1, pairs)]
    for j, target in enumerate(across):
        x_copy(1 + j, r, target).start()
    x_copy(0, r, sibling).start()

    for ch in range(1, CHUNKS):
        for way in (0, 1):
            @pl.when(sends_on(way, 1))
            def _():
                z_copy(way, 1, ch - 1).wait_send()
                z_copy(way, 1, ch).start()

    for copy in mp_copies:
        copy.wait_recv()
    total = mpart[0]
    for j in range(1, n_row):
        total = total + mpart[j]
    mass[c] = total
    for way in (0, 1):
        @pl.when(sends_on(way, 1))
        def _():
            hand_on(*small[1], way, 1).start()

    def forward(s):
        for ch in range(CHUNKS):
            for way in (0, 1):
                @pl.when(here(way, s))
                def _():
                    z_copy(way, s, ch).wait_recv()
                    if s < steps:
                        @pl.when(sends_on(way, s + 1))
                        def _():
                            z_copy(way, s + 1, ch).start()
                    for j in range(1, n_layer):
                        y_copy(way, s, ch, j, l).start()

    def forward_small(s):
        for way in (0, 1):
            @pl.when(here(way, s))
            def _():
                for group in small:
                    received(*group, way, s).wait_recv()
                if s < steps:
                    @pl.when(sends_on(way, s + 1))
                    def _():
                        for group in small:
                            hand_on(*group, way, s + 1).start()

    def unpack(buf, block):
        scale = 1.0 / mass[block]

        def tile_row(tr, carry):
            rows = pl.ds(pl.multiple_of(tr * EDGE, EDGE), EDGE)
            for tc in range(tiles_c):
                cols = slice(tc * EDGE, (tc + 1) * EDGE)
                tile = buf[ranks[block, tr, tc]].astype(jnp.float32)
                left[block, rows, cols] = (tile * scale[:, cols]).astype(jnp.bfloat16)
            return carry

        lax.fori_loop(0, tiles_r, tile_row, 0)

    def foreign(s):
        for way in (0, 1):
            @pl.when(here(way, s))
            def _():
                for ch in range(CHUNKS):
                    for j in range(1, n_layer):
                        y_copy(way, s, ch, j, lax.rem(l + n_layer - j, n_layer)).wait_recv()
                unpack(
                    (from_left if way == 0 else from_right)[s - 1],
                    c - s if way == 0 else c + s,
                )

    chunk_rows = min(height, 512)

    def products(near, far):
        def one(block, carry):
            distance = jnp.abs(block - c)

            @pl.when((distance >= near) & (distance < far))
            def _():
                section, offset = block // per, (block % per) * width
                right = rbuf[section, pl.ds(pl.multiple_of(offset, EDGE), width), :]

                def rows(i, inner):
                    span = pl.ds(pl.multiple_of(i * chunk_rows, EDGE), chunk_rows)
                    acc[span, :] += jnp.dot(
                        left[block, span, :], right, preferred_element_type=jnp.float32
                    )
                    return inner

                lax.fori_loop(0, height // chunk_rows, rows, 0)

            return carry

        lax.fori_loop(0, n_col, one, 0)

    for s in range(1, max(steps, 2)):
        forward(s)
        if s > 1:
            forward_small(s - 1)
    forward_small(max(steps - 1, 1))
    for j, target in enumerate(across):
        x_copy(1 + j, lax.rem(r + n_row - 2 * (j + 1), n_row), target).wait_recv()
        x_copy(pairs + j, lax.rem(r + n_row - 2 * (j + 1), n_row), sibling).start()
    x_copy(0, sibling, sibling).wait_recv()
    for j in range(len(across)):
        x_copy(pairs + j, lax.rem(sibling + n_row - 2 * (j + 1), n_row), sibling).wait_recv()
    unpack(pack, c)
    for s in range(1, steps - 1):
        foreign(s)
    products(0, max(steps - 1, 1))
    if steps >= 2:
        forward(steps)
        forward_small(steps)
    for s in range(max(steps - 1, 1), steps + 1):
        foreign(s)
    products(max(steps - 1, 1), n_col)

    inflated = acc[...] * acc[...]
    acc[...] = inflated
    wpart[r] = jnp.sum(inflated, axis=0, keepdims=True)
    for copy in to_peers("row", r, n_row, wpart, w_send, w_recv):
        copy.wait_recv()
    total = wpart[0]
    for j in range(1, n_row):
        total = total + wpart[j]
    scale_ref[...] = (height * n_row * 1.0) / total

    for copy in sends:
        copy.wait_send()
    for j, target in enumerate(across):
        x_copy(1 + j, r, target).wait_send()
        x_copy(pairs + j, r, sibling).wait_send()
    x_copy(0, r, sibling).wait_send()
    for s in range(1, steps + 1):
        for way in (0, 1):
            @pl.when(sends_on(way, s))
            def _():
                for ch in range(CHUNKS - 1 if s == 1 else 0, CHUNKS):
                    z_copy(way, s, ch).wait_send()
                for group in small:
                    hand_on(*group, way, s).wait_send()

            @pl.when(here(way, s))
            def _():
                for ch in range(CHUNKS):
                    for j in range(1, n_layer):
                        y_copy(way, s, ch, j, l).wait_send()


def scaled(inflated_ref, scale_ref, out_ref):
    out_ref[...] = inflated_ref[...] * scale_ref[...]


def shards(values, tile_mask):
    n_row, n_col, n_layer = (lax.axis_size(a) for a in ("row", "col", "layer"))
    height, width = values.shape
    tiles_r, tiles_c = tile_mask.shape
    live = tiles_r * tiles_c // 2
    half = width // n_layer
    dims = (n_row, n_col, n_layer, tiles_r, tiles_c, live)
    steps = n_col - 1
    dma = pltpu.SemaphoreType.DMA
    inflated, scale = pl.pallas_call(
        functools.partial(kernel, dims),
        out_shape=(
            pltpu.VMEM((height, half), jnp.float32),
            pltpu.VMEM((1, half), jnp.float32),
        ),
        in_specs=[pl.BlockSpec(memory_space=pl.ANY)] * 2,
        out_specs=(pl.BlockSpec(memory_space=pltpu.VMEM),) * 2,
        scratch_shapes=[
            pltpu.VMEM((tiles_r * tiles_c, EDGE, EDGE), jnp.bfloat16),
            pltpu.VMEM((live + 1, EDGE, EDGE), jnp.bfloat16),
            pltpu.VMEM((n_row, height, half), jnp.bfloat16),
            pltpu.VMEM((n_col, height, width), jnp.bfloat16),
            pltpu.SMEM((tiles_r, tiles_c), jnp.int32),
            pltpu.SMEM((n_col, tiles_r, tiles_c), jnp.int32),
            pltpu.VMEM((n_row, 1, width), jnp.float32),
            pltpu.VMEM((n_col, 1, width), jnp.float32),
            pltpu.VMEM((n_row, 1, half), jnp.float32),
            *[pltpu.VMEM((live + 1, EDGE, EDGE), jnp.bfloat16)] * steps,
            dma((2,)),
            dma((2, steps, CHUNKS)),
            dma((2, steps, CHUNKS)),
            dma((2, steps, CHUNKS, n_layer - 1)),
            dma((2, steps, CHUNKS, n_layer - 1)),
            dma((n_row,)),
            dma((n_row,)),
            dma((2, steps)),
            dma((2, steps)),
            dma((n_row - 1,)),
            dma((n_row - 1,)),
            dma((2, steps)),
            dma((2, steps)),
            dma((n_row - 1,)),
            dma((n_row - 1,)),
        ],
        compiler_params=pltpu.CompilerParams(
            collective_id=0, has_side_effects=True, vmem_limit_bytes=56 * 2**20
        ),
        name="markov_step",
    )(values, tile_mask)
    return pl.pallas_call(
        scaled,
        out_shape=jax.ShapeDtypeStruct((height, half), jnp.float32),
        in_specs=[pl.BlockSpec(memory_space=pltpu.VMEM)] * 2,
        out_specs=pl.BlockSpec(memory_space=pltpu.VMEM),
        compiler_params=pltpu.CompilerParams(vmem_limit_bytes=8 * 2**20),
        name="scaled",
    )(inflated, scale)


def solution(mesh):
    return jax.shard_map(
        shards,
        mesh=mesh,
        in_specs=(P("row", "col"), P("row", "col")),
        out_specs=P("row", ("col", "layer")),
        check_vma=False,
    )
```

```python
import functools

import jax
import jax.numpy as jnp
from jax import lax
from jax.experimental import pallas as pl
from jax.experimental.pallas import tpu as pltpu
from jax.sharding import PartitionSpec as P

MESH = pl.DeviceIdType.MESH
EDGE = 128
CHUNKS = 2


def kernel(
    dims, v_ref, m_ref, acc, scale_ref,
    by_tile, pack, rbuf, left, mask, ranks, mpart, mass, wpart, *rest,
):
    n_row, n_col, n_layer, tiles_r, tiles_c, live = dims
    steps = n_col - 1
    from_left = rest[:steps]
    from_right = from_left[::-1]
    (in_sem, z_send, z_recv, y_send, y_recv, x_send, x_recv, rank_send, rank_recv,
     mp_send, mp_recv, ms_send, ms_recv, w_send, w_recv) = rest[steps:]
    height, width = tiles_r * EDGE, tiles_c * EDGE
    half = width // n_layer
    half_tiles = tiles_c // n_layer
    tiles = tiles_r * tiles_c
    part = live // n_layer
    chunk = part // CHUNKS
    per = height // width
    r = lax.axis_index("row")
    c = lax.axis_index("col")
    l = lax.axis_index("layer")

    barrier = pltpu.get_barrier_semaphore()
    for axis, me, size in (("col", c, n_col), ("row", r, n_row), ("layer", l, n_layer)):
        for j in range(1, size):
            pl.semaphore_signal(
                barrier, inc=1, device_id={axis: lax.rem(me + j, size)}, device_id_type=MESH
            )

    mask_in = pltpu.make_async_copy(m_ref, mask, in_sem.at[0])
    mask_in.start()
    for t in range(tiles):
        tr, tc = t // tiles_c, t % tiles_c
        pltpu.make_async_copy(
            v_ref.at[tr * EDGE : (tr + 1) * EDGE, tc * EDGE : (tc + 1) * EDGE],
            by_tile.at[t], in_sem.at[1],
        ).start()
    zero_tile = jnp.zeros((EDGE, EDGE), jnp.bfloat16)
    for buf in (pack, *from_left):
        buf[live] = zero_tile
    acc[...] = jnp.zeros_like(acc)
    mask_in.wait()

    def rank_list(flags):
        count = jnp.int32(0)
        out = []
        for flag in flags:
            out.append(flag * count + (1 - flag) * live)
            count = count + flag
        return out

    flags = [mask[t // tiles_c, t % tiles_c] for t in range(tiles)]
    count = jnp.int32(0)
    upto = []
    for t in range(tiles):
        count = count + flags[t]
        upto.append(count)
    pltpu.make_async_copy(by_tile, by_tile, in_sem.at[1]).wait()
    for s in range(live):
        index = jnp.int32(0)
        for t in range(tiles - 1):
            index = index + lax.select(upto[t] <= s, jnp.int32(1), jnp.int32(0))
        pack[s] = by_tile[index]
    own_ranks = rank_list(flags)
    for t in range(tiles):
        ranks[c, t // tiles_c, t % tiles_c] = own_ranks[t]

    pl.semaphore_wait(barrier, n_col - 1 + n_row - 1 + n_layer - 1)

    sends = []

    def slots(layer, ch):
        return pl.ds(layer * part + ch * chunk, chunk)

    def z_copy(way, s, ch):
        bufs = from_left if way == 0 else from_right
        where = slots(l, ch)
        return pltpu.make_async_remote_copy(
            src_ref=pack.at[where], dst_ref=bufs[s - 1].at[where],
            send_sem=z_send.at[way, s - 1, ch], recv_sem=z_recv.at[way, s - 1, ch],
            device_id={"col": c + s if way == 0 else c - s}, device_id_type=MESH,
        )

    def y_copy(way, s, ch, j, layer):
        buf = (from_left if way == 0 else from_right)[s - 1]
        where = slots(layer, ch)
        return pltpu.make_async_remote_copy(
            src_ref=buf.at[where], dst_ref=buf.at[where],
            send_sem=y_send.at[way, s - 1, ch, j - 1], recv_sem=y_recv.at[way, s - 1, ch, j - 1],
            device_id={"layer": lax.rem(l + j, n_layer)}, device_id_type=MESH,
        )

    def here(way, s):
        return c >= s if way == 0 else c + s < n_col

    def sends_on(way, s):
        return c + s < n_col if way == 0 else c >= s

    for s in range(steps, 0, -1):
        for way in (0, 1):
            @pl.when(sends_on(way, s))
            def _():
                for ch in range(CHUNKS):
                    z_copy(way, s, ch).start()

    def to_peers(axis, me, size, ref, send, recv):
        copies = []
        for j in range(1, size):
            copy = pltpu.make_async_remote_copy(
                src_ref=ref.at[me], dst_ref=ref.at[me],
                send_sem=send.at[j - 1], recv_sem=recv.at[j - 1],
                device_id={axis: lax.rem(me + j, size)}, device_id_type=MESH,
            )
            copy.start()
            sends.append(copy)
            copies.append(copy)
        return copies

    rank_copies = to_peers("col", c, n_col, ranks, rank_send, rank_recv)

    for tc in range(tiles_c):
        total = jnp.zeros((EDGE, EDGE), jnp.float32)
        for tr in range(tiles_r):
            total = total + pack[own_ranks[tr * tiles_c + tc]].astype(jnp.float32)
        mpart[r, :, tc * EDGE : (tc + 1) * EDGE] = jnp.sum(total, axis=0, keepdims=True)

    mp_copies = to_peers("row", r, n_row, mpart, mp_send, mp_recv)

    for tr in range(tiles_r):
        for j in range(half_tiles):
            rank = ranks[c, tr, l * half_tiles + j]
            rbuf[r, tr * EDGE : (tr + 1) * EDGE, j * EDGE : (j + 1) * EDGE] = pack[rank]

    sibling = r + 1 - 2 * lax.rem(r, 2)
    pairs = n_row // 2

    def x_copy(k, section, target):
        return pltpu.make_async_remote_copy(
            src_ref=rbuf.at[section], dst_ref=rbuf.at[section],
            send_sem=x_send.at[k], recv_sem=x_recv.at[k],
            device_id={"row": target}, device_id_type=MESH,
        )

    across = [lax.rem(r + 2 * j, n_row) for j in range(1, pairs)]
    for j, target in enumerate(across):
        x_copy(1 + j, r, target).start()
    x_copy(0, r, sibling).start()

    for copy in mp_copies:
        copy.wait_recv()
    total = mpart[0]
    for j in range(1, n_row):
        total = total + mpart[j]
    mass[c] = total
    ms_copies = to_peers("col", c, n_col, mass, ms_send, ms_recv)

    def forward(s):
        for ch in range(CHUNKS):
            for way in (0, 1):
                @pl.when(here(way, s))
                def _():
                    z_copy(way, s, ch).wait_recv()
                    for j in range(1, n_layer):
                        y_copy(way, s, ch, j, l).start()
    def unpack(buf, block):
        scale = 1.0 / mass[block]

        def tile_row(tr, carry):
            rows = pl.ds(pl.multiple_of(tr * EDGE, EDGE), EDGE)
            for tc in range(tiles_c):
                cols = slice(tc * EDGE, (tc + 1) * EDGE)
                tile = buf[ranks[block, tr, tc]].astype(jnp.float32)
                left[block, rows, cols] = (tile * scale[:, cols]).astype(jnp.bfloat16)
            return carry

        lax.fori_loop(0, tiles_r, tile_row, 0)

    def foreign(s):
        for way in (0, 1):
            @pl.when(here(way, s))
            def _():
                for ch in range(CHUNKS):
                    for j in range(1, n_layer):
                        y_copy(way, s, ch, j, lax.rem(l + n_layer - j, n_layer)).wait_recv()
                unpack(
                    (from_left if way == 0 else from_right)[s - 1],
                    c - s if way == 0 else c + s,
                )

    chunk_rows = min(height, 512)

    def products(near, far):
        def one(block, carry):
            distance = jnp.abs(block - c)

            @pl.when((distance >= near) & (distance < far))
            def _():
                section, offset = block // per, (block % per) * width
                right = rbuf[section, pl.ds(pl.multiple_of(offset, EDGE), width), :]

                def rows(i, inner):
                    span = pl.ds(pl.multiple_of(i * chunk_rows, EDGE), chunk_rows)
                    acc[span, :] += jnp.dot(
                        left[block, span, :], right, preferred_element_type=jnp.float32
                    )
                    return inner

                lax.fori_loop(0, height // chunk_rows, rows, 0)

            return carry

        lax.fori_loop(0, n_col, one, 0)

    for s in range(1, max(steps, 2)):
        forward(s)
    for j, target in enumerate(across):
        x_copy(1 + j, lax.rem(r + n_row - 2 * (j + 1), n_row), target).wait_recv()
        x_copy(pairs + j, lax.rem(r + n_row - 2 * (j + 1), n_row), sibling).start()
    x_copy(0, sibling, sibling).wait_recv()
    for j in range(len(across)):
        x_copy(pairs + j, lax.rem(sibling + n_row - 2 * (j + 1), n_row), sibling).wait_recv()
    for copy in (*rank_copies, *ms_copies):
        copy.wait_recv()
    unpack(pack, c)
    for s in range(1, steps - 1):
        foreign(s)
    products(0, max(steps - 1, 1))
    if steps >= 2:
        forward(steps)
    for s in range(max(steps - 1, 1), steps + 1):
        foreign(s)
    products(max(steps - 1, 1), n_col)

    inflated = acc[...] * acc[...]
    acc[...] = inflated
    wpart[r] = jnp.sum(inflated, axis=0, keepdims=True)
    for copy in to_peers("row", r, n_row, wpart, w_send, w_recv):
        copy.wait_recv()
    total = wpart[0]
    for j in range(1, n_row):
        total = total + wpart[j]
    scale_ref[...] = (height * n_row * 1.0) / total

    for copy in sends:
        copy.wait_send()
    for j, target in enumerate(across):
        x_copy(1 + j, r, target).wait_send()
        x_copy(pairs + j, r, sibling).wait_send()
    x_copy(0, r, sibling).wait_send()
    for s in range(1, steps + 1):
        for way in (0, 1):
            @pl.when(sends_on(way, s))
            def _():
                for ch in range(CHUNKS):
                    z_copy(way, s, ch).wait_send()

            @pl.when(here(way, s))
            def _():
                for ch in range(CHUNKS):
                    for j in range(1, n_layer):
                        y_copy(way, s, ch, j, l).wait_send()


def scaled(inflated_ref, scale_ref, out_ref):
    out_ref[...] = inflated_ref[...] * scale_ref[...]


def shards(values, tile_mask):
    n_row, n_col, n_layer = (lax.axis_size(a) for a in ("row", "col", "layer"))
    height, width = values.shape
    tiles_r, tiles_c = tile_mask.shape
    live = tiles_r * tiles_c // 2
    half = width // n_layer
    dims = (n_row, n_col, n_layer, tiles_r, tiles_c, live)
    steps = n_col - 1
    dma = pltpu.SemaphoreType.DMA
    inflated, scale = pl.pallas_call(
        functools.partial(kernel, dims),
        out_shape=(
            pltpu.VMEM((height, half), jnp.float32),
            pltpu.VMEM((1, half), jnp.float32),
        ),
        in_specs=[pl.BlockSpec(memory_space=pl.ANY)] * 2,
        out_specs=(pl.BlockSpec(memory_space=pltpu.VMEM),) * 2,
        scratch_shapes=[
            pltpu.VMEM((tiles_r * tiles_c, EDGE, EDGE), jnp.bfloat16),
            pltpu.VMEM((live + 1, EDGE, EDGE), jnp.bfloat16),
            pltpu.VMEM((n_row, height, half), jnp.bfloat16),
            pltpu.VMEM((n_col, height, width), jnp.bfloat16),
            pltpu.SMEM((tiles_r, tiles_c), jnp.int32),
            pltpu.SMEM((n_col, tiles_r, tiles_c), jnp.int32),
            pltpu.VMEM((n_row, 1, width), jnp.float32),
            pltpu.VMEM((n_col, 1, width), jnp.float32),
            pltpu.VMEM((n_row, 1, half), jnp.float32),
            *[pltpu.VMEM((live + 1, EDGE, EDGE), jnp.bfloat16)] * steps,
            dma((2,)),
            dma((2, steps, CHUNKS)),
            dma((2, steps, CHUNKS)),
            dma((2, steps, CHUNKS, n_layer - 1)),
            dma((2, steps, CHUNKS, n_layer - 1)),
            dma((n_row,)),
            dma((n_row,)),
            dma((steps,)),
            dma((steps,)),
            dma((n_row - 1,)),
            dma((n_row - 1,)),
            dma((steps,)),
            dma((steps,)),
            dma((n_row - 1,)),
            dma((n_row - 1,)),
        ],
        compiler_params=pltpu.CompilerParams(
            collective_id=0, has_side_effects=True, vmem_limit_bytes=56 * 2**20
        ),
        name="markov_step",
    )(values, tile_mask)
    return pl.pallas_call(
        scaled,
        out_shape=jax.ShapeDtypeStruct((height, half), jnp.float32),
        in_specs=[pl.BlockSpec(memory_space=pltpu.VMEM)] * 2,
        out_specs=pl.BlockSpec(memory_space=pltpu.VMEM),
        compiler_params=pltpu.CompilerParams(vmem_limit_bytes=8 * 2**20),
        name="scaled",
    )(inflated, scale)


def solution(mesh):
    return jax.shard_map(
        shards,
        mesh=mesh,
        in_specs=(P("row", "col"), P("row", "col")),
        out_specs=P("row", ("col", "layer")),
        check_vma=False,
    )
```

```python
import functools

import jax
import jax.numpy as jnp
from jax import lax
from jax.experimental import pallas as pl
from jax.experimental.pallas import tpu as pltpu
from jax.sharding import PartitionSpec as P

MESH = pl.DeviceIdType.MESH
EDGE = 128
CHUNKS = 2


def kernel(
    dims, v_ref, m_ref, acc, scale_ref,
    by_tile, pack, rbuf, left, mask, ranks, mpart, mass, wpart, *rest,
):
    n_row, n_col, n_layer, tiles_r, tiles_c, live = dims
    steps = n_col - 1
    from_left = rest[:steps]
    from_right = from_left[::-1]
    (in_sem, z_send, z_recv, y_send, y_recv, x_send, x_recv, rank_send, rank_recv,
     mp_send, mp_recv, ms_send, ms_recv, w_send, w_recv) = rest[steps:]
    height, width = tiles_r * EDGE, tiles_c * EDGE
    half = width // n_layer
    half_tiles = tiles_c // n_layer
    tiles = tiles_r * tiles_c
    part = live // n_layer
    chunk = part // CHUNKS
    per = height // width
    r = lax.axis_index("row")
    c = lax.axis_index("col")
    l = lax.axis_index("layer")

    barrier = pltpu.get_barrier_semaphore()
    for axis, me, size in (("row", r, n_row), ("layer", l, n_layer)):
        for j in range(1, size):
            pl.semaphore_signal(
                barrier, inc=1, device_id={axis: lax.rem(me + j, size)}, device_id_type=MESH
            )

    @pl.when(c > 0)
    def _():
        pl.semaphore_signal(barrier, inc=1, device_id={"col": c - 1}, device_id_type=MESH)

    @pl.when(c + 1 < n_col)
    def _():
        pl.semaphore_signal(barrier, inc=1, device_id={"col": c + 1}, device_id_type=MESH)

    if steps >= 2:
        @pl.when(c == 0)
        def _():
            pl.semaphore_signal(barrier, inc=1, device_id={"col": steps}, device_id_type=MESH)

    mask_in = pltpu.make_async_copy(m_ref, mask, in_sem.at[0])
    mask_in.start()
    for t in range(tiles):
        tr, tc = t // tiles_c, t % tiles_c
        pltpu.make_async_copy(
            v_ref.at[tr * EDGE : (tr + 1) * EDGE, tc * EDGE : (tc + 1) * EDGE],
            by_tile.at[t], in_sem.at[1],
        ).start()
    zero_tile = jnp.zeros((EDGE, EDGE), jnp.bfloat16)
    for buf in (pack, *from_left):
        buf[live] = zero_tile
    acc[...] = jnp.zeros_like(acc)
    mask_in.wait()

    def rank_list(flags):
        count = jnp.int32(0)
        out = []
        for flag in flags:
            out.append(flag * count + (1 - flag) * live)
            count = count + flag
        return out

    flags = [mask[t // tiles_c, t % tiles_c] for t in range(tiles)]
    count = jnp.int32(0)
    upto = []
    for t in range(tiles):
        count = count + flags[t]
        upto.append(count)
    pltpu.make_async_copy(by_tile, by_tile, in_sem.at[1]).wait()
    for s in range(live):
        index = jnp.int32(0)
        for t in range(tiles - 1):
            index = index + lax.select(upto[t] <= s, jnp.int32(1), jnp.int32(0))
        pack[s] = by_tile[index]
    own_ranks = rank_list(flags)
    for t in range(tiles):
        ranks[c, t // tiles_c, t % tiles_c] = own_ranks[t]

    neighbours = lax.select(c > 0, 1, 0) + lax.select(c + 1 < n_col, 1, 0)
    if steps >= 2:
        neighbours = neighbours + lax.select(c == steps, 1, 0)
    pl.semaphore_wait(barrier, n_row - 1 + n_layer - 1 + neighbours)

    sends = []

    def slots(layer, ch):
        return pl.ds(layer * part + ch * chunk, chunk)

    def direct(way, s):
        return way == 1 and s == steps and steps >= 2

    def z_copy(way, s, ch):
        bufs = from_left if way == 0 else from_right
        src = pack if s == 1 or direct(way, s) else bufs[s - 2]
        hops = s if direct(way, s) else 1
        where = slots(l, ch)
        return pltpu.make_async_remote_copy(
            src_ref=src.at[where], dst_ref=bufs[s - 1].at[where],
            send_sem=z_send.at[way, s - 1, ch], recv_sem=z_recv.at[way, s - 1, ch],
            device_id={"col": c + hops if way == 0 else c - hops}, device_id_type=MESH,
        )

    def y_copy(way, s, ch, j, layer):
        buf = (from_left if way == 0 else from_right)[s - 1]
        where = slots(layer, ch)
        return pltpu.make_async_remote_copy(
            src_ref=buf.at[where], dst_ref=buf.at[where],
            send_sem=y_send.at[way, s - 1, ch, j - 1], recv_sem=y_recv.at[way, s - 1, ch, j - 1],
            device_id={"layer": lax.rem(l + j, n_layer)}, device_id_type=MESH,
        )

    def here(way, s):
        return c >= s if way == 0 else c + s < n_col

    def passes_on(way, s):
        if way == 0:
            return (c + 1 < n_col) & (c >= s - 1)
        return (c >= 1) & (c + s - 1 < n_col)

    def sends_on(way, s):
        return c == steps if direct(way, s) else passes_on(way, s)

    def z_start(s, ch):
        for way in (0, 1):
            @pl.when(sends_on(way, s))
            def _():
                z_copy(way, s, ch).start()

    for ch in range(CHUNKS):
        if steps >= 2:
            @pl.when(sends_on(1, steps))
            def _():
                z_copy(1, steps, ch).start()
        z_start(1, ch)

    def to_peers(axis, me, size, ref, send, recv):
        copies = []
        for j in range(1, size):
            copy = pltpu.make_async_remote_copy(
                src_ref=ref.at[me], dst_ref=ref.at[me],
                send_sem=send.at[j - 1], recv_sem=recv.at[j - 1],
                device_id={axis: lax.rem(me + j, size)}, device_id_type=MESH,
            )
            copy.start()
            sends.append(copy)
            copies.append(copy)
        return copies

    def hand_on(ref, send, recv, way, s):
        block = c - (s - 1) if way == 0 else c + (s - 1)
        return pltpu.make_async_remote_copy(
            src_ref=ref.at[block], dst_ref=ref.at[block],
            send_sem=send.at[way, s - 1], recv_sem=recv.at[way, s - 1],
            device_id={"col": c + 1 if way == 0 else c - 1}, device_id_type=MESH,
        )

    def received(ref, send, recv, way, s):
        block = c - s if way == 0 else c + s
        return pltpu.make_async_remote_copy(
            src_ref=ref.at[block], dst_ref=ref.at[block],
            send_sem=send.at[way, s - 1], recv_sem=recv.at[way, s - 1],
            device_id={"col": c + 1 if way == 0 else c - 1}, device_id_type=MESH,
        )

    small = ((ranks, rank_send, rank_recv), (mass, ms_send, ms_recv))

    for tc in range(tiles_c):
        total = jnp.zeros((EDGE, EDGE), jnp.float32)
        for tr in range(tiles_r):
            total = total + pack[own_ranks[tr * tiles_c + tc]].astype(jnp.float32)
        mpart[r, :, tc * EDGE : (tc + 1) * EDGE] = jnp.sum(total, axis=0, keepdims=True)

    mp_copies = to_peers("row", r, n_row, mpart, mp_send, mp_recv)
    for way in (0, 1):
        @pl.when(sends_on(way, 1))
        def _():
            hand_on(*small[0], way, 1).start()

    for tr in range(tiles_r):
        for j in range(half_tiles):
            rank = ranks[c, tr, l * half_tiles + j]
            rbuf[r, tr * EDGE : (tr + 1) * EDGE, j * EDGE : (j + 1) * EDGE] = pack[rank]

    sibling = r + 1 - 2 * lax.rem(r, 2)
    pairs = n_row // 2

    def x_copy(k, section, target):
        return pltpu.make_async_remote_copy(
            src_ref=rbuf.at[section], dst_ref=rbuf.at[section],
            send_sem=x_send.at[k], recv_sem=x_recv.at[k],
            device_id={"row": target}, device_id_type=MESH,
        )

    across = [lax.rem(r + 2 * j, n_row) for j in range(1, pairs)]
    for j, target in enumerate(across):
        x_copy(1 + j, r, target).start()
    x_copy(0, r, sibling).start()

    for copy in mp_copies:
        copy.wait_recv()
    total = mpart[0]
    for j in range(1, n_row):
        total = total + mpart[j]
    mass[c] = total
    for way in (0, 1):
        @pl.when(sends_on(way, 1))
        def _():
            hand_on(*small[1], way, 1).start()

    def forward(s):
        for ch in range(CHUNKS):
            for way in (0, 1):
                @pl.when(here(way, s))
                def _():
                    z_copy(way, s, ch).wait_recv()
                    if s < steps and not direct(way, s + 1):
                        @pl.when(sends_on(way, s + 1))
                        def _():
                            z_copy(way, s + 1, ch).start()
                    for j in range(1, n_layer):
                        y_copy(way, s, ch, j, l).start()
        for way in (0, 1):
            @pl.when(here(way, s))
            def _():
                for group in small:
                    received(*group, way, s).wait_recv()
                if s < steps:
                    @pl.when(passes_on(way, s + 1))
                    def _():
                        for group in small:
                            hand_on(*group, way, s + 1).start()

    def unpack(buf, block):
        scale = 1.0 / mass[block]

        def tile_row(tr, carry):
            rows = pl.ds(pl.multiple_of(tr * EDGE, EDGE), EDGE)
            for tc in range(tiles_c):
                cols = slice(tc * EDGE, (tc + 1) * EDGE)
                tile = buf[ranks[block, tr, tc]].astype(jnp.float32)
                left[block, rows, cols] = (tile * scale[:, cols]).astype(jnp.bfloat16)
            return carry

        lax.fori_loop(0, tiles_r, tile_row, 0)

    def foreign(s):
        for way in (0, 1):
            @pl.when(here(way, s))
            def _():
                for ch in range(CHUNKS):
                    for j in range(1, n_layer):
                        y_copy(way, s, ch, j, lax.rem(l + n_layer - j, n_layer)).wait_recv()
                unpack(
                    (from_left if way == 0 else from_right)[s - 1],
                    c - s if way == 0 else c + s,
                )

    chunk_rows = min(height, 512)

    def products(near, far):
        def one(block, carry):
            distance = jnp.abs(block - c)

            @pl.when((distance >= near) & (distance < far))
            def _():
                section, offset = block // per, (block % per) * width
                right = rbuf[section, pl.ds(pl.multiple_of(offset, EDGE), width), :]

                def rows(i, inner):
                    span = pl.ds(pl.multiple_of(i * chunk_rows, EDGE), chunk_rows)
                    acc[span, :] += jnp.dot(
                        left[block, span, :], right, preferred_element_type=jnp.float32
                    )
                    return inner

                lax.fori_loop(0, height // chunk_rows, rows, 0)

            return carry

        lax.fori_loop(0, n_col, one, 0)

    for s in range(1, max(steps, 2)):
        forward(s)
    for j, target in enumerate(across):
        x_copy(1 + j, lax.rem(r + n_row - 2 * (j + 1), n_row), target).wait_recv()
        x_copy(pairs + j, lax.rem(r + n_row - 2 * (j + 1), n_row), sibling).start()
    x_copy(0, sibling, sibling).wait_recv()
    for j in range(len(across)):
        x_copy(pairs + j, lax.rem(sibling + n_row - 2 * (j + 1), n_row), sibling).wait_recv()
    unpack(pack, c)
    for s in range(1, steps - 1):
        foreign(s)
    products(0, max(steps - 1, 1))
    if steps >= 2:
        forward(steps)
    for s in range(max(steps - 1, 1), steps + 1):
        foreign(s)
    products(max(steps - 1, 1), n_col)

    inflated = acc[...] * acc[...]
    acc[...] = inflated
    wpart[r] = jnp.sum(inflated, axis=0, keepdims=True)
    for copy in to_peers("row", r, n_row, wpart, w_send, w_recv):
        copy.wait_recv()
    total = wpart[0]
    for j in range(1, n_row):
        total = total + wpart[j]
    scale_ref[...] = (height * n_row * 1.0) / total

    for copy in sends:
        copy.wait_send()
    for j, target in enumerate(across):
        x_copy(1 + j, r, target).wait_send()
        x_copy(pairs + j, r, sibling).wait_send()
    x_copy(0, r, sibling).wait_send()
    for s in range(1, steps + 1):
        for way in (0, 1):
            @pl.when(sends_on(way, s))
            def _():
                for ch in range(CHUNKS):
                    z_copy(way, s, ch).wait_send()

            @pl.when(passes_on(way, s))
            def _():
                for group in small:
                    hand_on(*group, way, s).wait_send()

            @pl.when(here(way, s))
            def _():
                for ch in range(CHUNKS):
                    for j in range(1, n_layer):
                        y_copy(way, s, ch, j, l).wait_send()


def scaled(inflated_ref, scale_ref, out_ref):
    out_ref[...] = inflated_ref[...] * scale_ref[...]


def shards(values, tile_mask):
    n_row, n_col, n_layer = (lax.axis_size(a) for a in ("row", "col", "layer"))
    height, width = values.shape
    tiles_r, tiles_c = tile_mask.shape
    live = tiles_r * tiles_c // 2
    half = width // n_layer
    dims = (n_row, n_col, n_layer, tiles_r, tiles_c, live)
    steps = n_col - 1
    dma = pltpu.SemaphoreType.DMA
    inflated, scale = pl.pallas_call(
        functools.partial(kernel, dims),
        out_shape=(
            pltpu.VMEM((height, half), jnp.float32),
            pltpu.VMEM((1, half), jnp.float32),
        ),
        in_specs=[pl.BlockSpec(memory_space=pl.ANY)] * 2,
        out_specs=(pl.BlockSpec(memory_space=pltpu.VMEM),) * 2,
        scratch_shapes=[
            pltpu.VMEM((tiles_r * tiles_c, EDGE, EDGE), jnp.bfloat16),
            pltpu.VMEM((live + 1, EDGE, EDGE), jnp.bfloat16),
            pltpu.VMEM((n_row, height, half), jnp.bfloat16),
            pltpu.VMEM((n_col, height, width), jnp.bfloat16),
            pltpu.SMEM((tiles_r, tiles_c), jnp.int32),
            pltpu.SMEM((n_col, tiles_r, tiles_c), jnp.int32),
            pltpu.VMEM((n_row, 1, width), jnp.float32),
            pltpu.VMEM((n_col, 1, width), jnp.float32),
            pltpu.VMEM((n_row, 1, half), jnp.float32),
            *[pltpu.VMEM((live + 1, EDGE, EDGE), jnp.bfloat16)] * steps,
            dma((2,)),
            dma((2, steps, CHUNKS)),
            dma((2, steps, CHUNKS)),
            dma((2, steps, CHUNKS, n_layer - 1)),
            dma((2, steps, CHUNKS, n_layer - 1)),
            dma((n_row,)),
            dma((n_row,)),
            dma((2, steps)),
            dma((2, steps)),
            dma((n_row - 1,)),
            dma((n_row - 1,)),
            dma((2, steps)),
            dma((2, steps)),
            dma((n_row - 1,)),
            dma((n_row - 1,)),
        ],
        compiler_params=pltpu.CompilerParams(
            collective_id=0, has_side_effects=True, vmem_limit_bytes=56 * 2**20
        ),
        name="markov_step",
    )(values, tile_mask)
    return pl.pallas_call(
        scaled,
        out_shape=jax.ShapeDtypeStruct((height, half), jnp.float32),
        in_specs=[pl.BlockSpec(memory_space=pltpu.VMEM)] * 2,
        out_specs=pl.BlockSpec(memory_space=pltpu.VMEM),
        compiler_params=pltpu.CompilerParams(vmem_limit_bytes=8 * 2**20),
        name="scaled",
    )(inflated, scale)


def solution(mesh):
    return jax.shard_map(
        shards,
        mesh=mesh,
        in_specs=(P("row", "col"), P("row", "col")),
        out_specs=P("row", ("col", "layer")),
        check_vma=False,
    )
```

```python
import functools

import jax
import jax.numpy as jnp
from jax import lax
from jax.experimental import pallas as pl
from jax.experimental.pallas import tpu as pltpu
from jax.sharding import PartitionSpec as P

MESH = pl.DeviceIdType.MESH
EDGE = 128
CHUNKS = 1


def kernel(
    dims, v_ref, m_ref, acc, scale_ref,
    own, by_tile, pack, rbuf, left, mask, ranks, mpart, mass, wpart, *rest,
):
    n_row, n_col, n_layer, tiles_r, tiles_c, live = dims
    steps = n_col - 1
    from_left = rest[:steps]
    from_right = from_left[::-1]
    (in_sem, z_send, z_recv, y_send, y_recv, x_send, x_recv, rank_send, rank_recv,
     mp_send, mp_recv, ms_send, ms_recv, w_send, w_recv) = rest[steps:]
    height, width = tiles_r * EDGE, tiles_c * EDGE
    half = width // n_layer
    half_tiles = tiles_c // n_layer
    tiles = tiles_r * tiles_c
    part = live // n_layer
    chunk = part // CHUNKS
    per = height // width
    r = lax.axis_index("row")
    c = lax.axis_index("col")
    l = lax.axis_index("layer")

    barrier = pltpu.get_barrier_semaphore()
    for axis, me, size in (("row", r, n_row), ("layer", l, n_layer)):
        for j in range(1, size):
            pl.semaphore_signal(
                barrier, inc=1, device_id={axis: lax.rem(me + j, size)}, device_id_type=MESH
            )

    @pl.when(c > 0)
    def _():
        pl.semaphore_signal(barrier, inc=1, device_id={"col": c - 1}, device_id_type=MESH)

    @pl.when(c + 1 < n_col)
    def _():
        pl.semaphore_signal(barrier, inc=1, device_id={"col": c + 1}, device_id_type=MESH)

    mask_in = pltpu.make_async_copy(m_ref, mask, in_sem.at[0])
    mask_in.start()
    block_in = pltpu.make_async_copy(v_ref, own, in_sem.at[1])
    block_in.start()
    zero_tile = jnp.zeros((EDGE, EDGE), jnp.bfloat16)
    for buf in (pack, *from_left):
        buf[live] = zero_tile
    acc[...] = jnp.zeros_like(acc)
    mask_in.wait()

    def rank_list(flags):
        count = jnp.int32(0)
        out = []
        for flag in flags:
            out.append(flag * count + (1 - flag) * live)
            count = count + flag
        return out

    flags = [mask[t // tiles_c, t % tiles_c] for t in range(tiles)]
    count = jnp.int32(0)
    upto = []
    for t in range(tiles):
        count = count + flags[t]
        upto.append(count)
    block_in.wait()
    for t in range(tiles):
        tr, tc = t // tiles_c, t % tiles_c
        by_tile[t] = own[tr * EDGE : (tr + 1) * EDGE, tc * EDGE : (tc + 1) * EDGE]
    for s in range(live):
        index = jnp.int32(0)
        for t in range(tiles - 1):
            index = index + lax.select(upto[t] <= s, jnp.int32(1), jnp.int32(0))
        pack[s] = by_tile[index]
    own_ranks = rank_list(flags)
    for t in range(tiles):
        ranks[c, t // tiles_c, t % tiles_c] = own_ranks[t]

    for tc in range(tiles_c):
        total = jnp.zeros((EDGE, EDGE), jnp.float32)
        for tr in range(tiles_r):
            total = total + pack[own_ranks[tr * tiles_c + tc]].astype(jnp.float32)
        mpart[r, :, tc * EDGE : (tc + 1) * EDGE] = jnp.sum(total, axis=0, keepdims=True)

    for tr in range(tiles_r):
        for j in range(half_tiles):
            rank = ranks[c, tr, l * half_tiles + j]
            rbuf[r, tr * EDGE : (tr + 1) * EDGE, j * EDGE : (j + 1) * EDGE] = pack[rank]

    neighbours = lax.select(c > 0, 1, 0) + lax.select(c + 1 < n_col, 1, 0)
    pl.semaphore_wait(barrier, n_row - 1 + n_layer - 1 + neighbours)

    sibling = r + 1 - 2 * lax.rem(r, 2)
    pairs = n_row // 2

    def x_copy(k, section, target):
        return pltpu.make_async_remote_copy(
            src_ref=rbuf.at[section], dst_ref=rbuf.at[section],
            send_sem=x_send.at[k], recv_sem=x_recv.at[k],
            device_id={"row": target}, device_id_type=MESH,
        )

    across = [lax.rem(r + 2 * j, n_row) for j in range(1, pairs)]
    for j, target in enumerate(across):
        x_copy(1 + j, r, target).start()
    sends = []

    def slots(layer, ch):
        return pl.ds(layer * part + ch * chunk, chunk)

    def z_copy(way, s, ch):
        bufs = from_left if way == 0 else from_right
        src = pack if s == 1 else bufs[s - 2]
        where = slots(l, ch)
        return pltpu.make_async_remote_copy(
            src_ref=src.at[where], dst_ref=bufs[s - 1].at[where],
            send_sem=z_send.at[way, s - 1, ch], recv_sem=z_recv.at[way, s - 1, ch],
            device_id={"col": c + 1 if way == 0 else c - 1}, device_id_type=MESH,
        )

    def y_copy(way, s, ch, j, layer):
        buf = (from_left if way == 0 else from_right)[s - 1]
        where = slots(layer, ch)
        return pltpu.make_async_remote_copy(
            src_ref=buf.at[where], dst_ref=buf.at[where],
            send_sem=y_send.at[way, s - 1, ch, j - 1], recv_sem=y_recv.at[way, s - 1, ch, j - 1],
            device_id={"layer": lax.rem(l + j, n_layer)}, device_id_type=MESH,
        )

    def here(way, s):
        return c >= s if way == 0 else c + s < n_col

    def sends_on(way, s):
        if way == 0:
            return (c + 1 < n_col) & (c >= s - 1)
        return (c >= 1) & (c + s - 1 < n_col)

    def z_start(s, ch):
        for way in (0, 1):
            @pl.when(sends_on(way, s))
            def _():
                z_copy(way, s, ch).start()

    for ch in range(CHUNKS):
        z_start(1, ch)

    def to_peers(axis, me, size, ref, send, recv):
        copies = []
        for j in range(1, size):
            copy = pltpu.make_async_remote_copy(
                src_ref=ref.at[me], dst_ref=ref.at[me],
                send_sem=send.at[j - 1], recv_sem=recv.at[j - 1],
                device_id={axis: lax.rem(me + j, size)}, device_id_type=MESH,
            )
            copy.start()
            sends.append(copy)
            copies.append(copy)
        return copies

    def hand_on(ref, send, recv, way, s):
        block = c - (s - 1) if way == 0 else c + (s - 1)
        return pltpu.make_async_remote_copy(
            src_ref=ref.at[block], dst_ref=ref.at[block],
            send_sem=send.at[way, s - 1], recv_sem=recv.at[way, s - 1],
            device_id={"col": c + 1 if way == 0 else c - 1}, device_id_type=MESH,
        )

    def received(ref, send, recv, way, s):
        block = c - s if way == 0 else c + s
        return pltpu.make_async_remote_copy(
            src_ref=ref.at[block], dst_ref=ref.at[block],
            send_sem=send.at[way, s - 1], recv_sem=recv.at[way, s - 1],
            device_id={"col": c + 1 if way == 0 else c - 1}, device_id_type=MESH,
        )

    small = ((ranks, rank_send, rank_recv), (mass, ms_send, ms_recv))

    mp_copies = to_peers("row", r, n_row, mpart, mp_send, mp_recv)
    for way in (0, 1):
        @pl.when(sends_on(way, 1))
        def _():
            hand_on(*small[0], way, 1).start()

    x_copy(0, r, sibling).start()

    for copy in mp_copies:
        copy.wait_recv()
    total = mpart[0]
    for j in range(1, n_row):
        total = total + mpart[j]
    mass[c] = total
    for way in (0, 1):
        @pl.when(sends_on(way, 1))
        def _():
            hand_on(*small[1], way, 1).start()

    def forward(s):
        for ch in range(CHUNKS):
            for way in (0, 1):
                @pl.when(here(way, s))
                def _():
                    z_copy(way, s, ch).wait_recv()
                    if s < steps:
                        @pl.when(sends_on(way, s + 1))
                        def _():
                            z_copy(way, s + 1, ch).start()
                    for j in range(1, n_layer):
                        y_copy(way, s, ch, j, l).start()
        for way in (0, 1):
            @pl.when(here(way, s))
            def _():
                for group in small:
                    received(*group, way, s).wait_recv()
                if s < steps:
                    @pl.when(sends_on(way, s + 1))
                    def _():
                        for group in small:
                            hand_on(*group, way, s + 1).start()

    def unpack(buf, block):
        scale = 1.0 / mass[block]

        def tile_row(tr, carry):
            rows = pl.ds(pl.multiple_of(tr * EDGE, EDGE), EDGE)
            for tc in range(tiles_c):
                cols = slice(tc * EDGE, (tc + 1) * EDGE)
                tile = buf[ranks[block, tr, tc]].astype(jnp.float32)
                left[block, rows, cols] = (tile * scale[:, cols]).astype(jnp.bfloat16)
            return carry

        lax.fori_loop(0, tiles_r, tile_row, 0)

    def foreign(s):
        for way in (0, 1):
            @pl.when(here(way, s))
            def _():
                for ch in range(CHUNKS):
                    for j in range(1, n_layer):
                        y_copy(way, s, ch, j, lax.rem(l + n_layer - j, n_layer)).wait_recv()
                unpack(
                    (from_left if way == 0 else from_right)[s - 1],
                    c - s if way == 0 else c + s,
                )

    chunk_rows = min(height, 512)

    def products(near, far):
        def one(block, carry):
            distance = jnp.abs(block - c)

            @pl.when((distance >= near) & (distance < far))
            def _():
                section, offset = block // per, (block % per) * width
                right = rbuf[section, pl.ds(pl.multiple_of(offset, EDGE), width), :]

                def rows(i, inner):
                    span = pl.ds(pl.multiple_of(i * chunk_rows, EDGE), chunk_rows)
                    acc[span, :] += jnp.dot(
                        left[block, span, :], right, preferred_element_type=jnp.float32
                    )
                    return inner

                lax.fori_loop(0, height // chunk_rows, rows, 0)

            return carry

        lax.fori_loop(0, n_col, one, 0)

    for s in range(1, max(steps, 2)):
        forward(s)
    for j, target in enumerate(across):
        x_copy(1 + j, lax.rem(r + n_row - 2 * (j + 1), n_row), target).wait_recv()
        x_copy(pairs + j, lax.rem(r + n_row - 2 * (j + 1), n_row), sibling).start()
    if steps >= 2:
        forward(steps)
    x_copy(0, sibling, sibling).wait_recv()
    for j in range(len(across)):
        x_copy(pairs + j, lax.rem(sibling + n_row - 2 * (j + 1), n_row), sibling).wait_recv()

    unpack(pack, c)
    for s in range(1, steps):
        foreign(s)
    products(0, steps)
    foreign(steps)
    products(steps, n_col)

    inflated = acc[...] * acc[...]
    acc[...] = inflated
    wpart[r] = jnp.sum(inflated, axis=0, keepdims=True)
    w_copies = to_peers("row", r, n_row, wpart, w_send, w_recv)

    for copy in sends:
        copy.wait_send()
    for j, target in enumerate(across):
        x_copy(1 + j, r, target).wait_send()
        x_copy(pairs + j, r, sibling).wait_send()
    x_copy(0, r, sibling).wait_send()
    for s in range(1, steps + 1):
        for way in (0, 1):
            @pl.when(sends_on(way, s))
            def _():
                for ch in range(CHUNKS):
                    z_copy(way, s, ch).wait_send()
                for group in small:
                    hand_on(*group, way, s).wait_send()

            @pl.when(here(way, s))
            def _():
                for ch in range(CHUNKS):
                    for j in range(1, n_layer):
                        y_copy(way, s, ch, j, l).wait_send()

    for copy in w_copies:
        copy.wait_recv()
    total = wpart[0]
    for j in range(1, n_row):
        total = total + wpart[j]
    scale_ref[...] = (height * n_row * 1.0) / total


def scaled(inflated_ref, scale_ref, out_ref):
    out_ref[...] = inflated_ref[...] * scale_ref[...]


def shards(values, tile_mask):
    n_row, n_col, n_layer = (lax.axis_size(a) for a in ("row", "col", "layer"))
    height, width = values.shape
    tiles_r, tiles_c = tile_mask.shape
    live = tiles_r * tiles_c // 2
    half = width // n_layer
    dims = (n_row, n_col, n_layer, tiles_r, tiles_c, live)
    steps = n_col - 1
    dma = pltpu.SemaphoreType.DMA
    inflated, scale = pl.pallas_call(
        functools.partial(kernel, dims),
        out_shape=(
            pltpu.VMEM((height, half), jnp.float32),
            pltpu.VMEM((1, half), jnp.float32),
        ),
        in_specs=[pl.BlockSpec(memory_space=pl.ANY)] * 2,
        out_specs=(pl.BlockSpec(memory_space=pltpu.VMEM),) * 2,
        scratch_shapes=[
            pltpu.VMEM((height, width), jnp.bfloat16),
            pltpu.VMEM((tiles_r * tiles_c, EDGE, EDGE), jnp.bfloat16),
            pltpu.VMEM((live + 1, EDGE, EDGE), jnp.bfloat16),
            pltpu.VMEM((n_row, height, half), jnp.bfloat16),
            pltpu.VMEM((n_col, height, width), jnp.bfloat16),
            pltpu.SMEM((tiles_r, tiles_c), jnp.int32),
            pltpu.SMEM((n_col, tiles_r, tiles_c), jnp.int32),
            pltpu.VMEM((n_row, 1, width), jnp.float32),
            pltpu.VMEM((n_col, 1, width), jnp.float32),
            pltpu.VMEM((n_row, 1, half), jnp.float32),
            *[pltpu.VMEM((live + 1, EDGE, EDGE), jnp.bfloat16)] * steps,
            dma((2,)),
            dma((2, steps, CHUNKS)),
            dma((2, steps, CHUNKS)),
            dma((2, steps, CHUNKS, n_layer - 1)),
            dma((2, steps, CHUNKS, n_layer - 1)),
            dma((n_row,)),
            dma((n_row,)),
            dma((2, steps)),
            dma((2, steps)),
            dma((n_row - 1,)),
            dma((n_row - 1,)),
            dma((2, steps)),
            dma((2, steps)),
            dma((n_row - 1,)),
            dma((n_row - 1,)),
        ],
        compiler_params=pltpu.CompilerParams(
            collective_id=0, has_side_effects=True, vmem_limit_bytes=56 * 2**20
        ),
        name="markov_step",
    )(values, tile_mask)
    return pl.pallas_call(
        scaled,
        out_shape=jax.ShapeDtypeStruct((height, half), jnp.float32),
        in_specs=[pl.BlockSpec(memory_space=pltpu.VMEM)] * 2,
        out_specs=pl.BlockSpec(memory_space=pltpu.VMEM),
        compiler_params=pltpu.CompilerParams(vmem_limit_bytes=8 * 2**20),
        name="scaled",
    )(inflated, scale)


def solution(mesh):
    return jax.shard_map(
        shards,
        mesh=mesh,
        in_specs=(P("row", "col"), P("row", "col")),
        out_specs=P("row", ("col", "layer")),
        check_vma=False,
    )
```

```python
import functools

import jax
import jax.numpy as jnp
from jax import lax
from jax.experimental import pallas as pl
from jax.experimental.pallas import tpu as pltpu
from jax.sharding import PartitionSpec as P

MESH = pl.DeviceIdType.MESH
EDGE = 128
CHUNKS = 2
X_CHUNKS = 4


def kernel(
    dims, v_ref, m_ref, acc, scale_ref,
    by_tile, pack, rbuf, left, mask, ranks, mpart, mass, wpart, *rest,
):
    n_row, n_col, n_layer, tiles_r, tiles_c, live = dims
    steps = n_col - 1
    from_left = rest[:steps]
    from_right = from_left[::-1]
    (in_sem, z_send, z_recv, y_send, y_recv, x_send, x_recv, rank_send, rank_recv,
     mp_send, mp_recv, ms_send, ms_recv, w_send, w_recv) = rest[steps:]
    height, width = tiles_r * EDGE, tiles_c * EDGE
    half = width // n_layer
    half_tiles = tiles_c // n_layer
    tiles = tiles_r * tiles_c
    part = live // n_layer
    chunk = part // CHUNKS
    per = height // width
    r = lax.axis_index("row")
    c = lax.axis_index("col")
    l = lax.axis_index("layer")

    barrier = pltpu.get_barrier_semaphore()
    for axis, me, size in (("row", r, n_row), ("layer", l, n_layer)):
        for j in range(1, size):
            pl.semaphore_signal(
                barrier, inc=1, device_id={axis: lax.rem(me + j, size)}, device_id_type=MESH
            )

    @pl.when(c > 0)
    def _():
        pl.semaphore_signal(barrier, inc=1, device_id={"col": c - 1}, device_id_type=MESH)

    @pl.when(c + 1 < n_col)
    def _():
        pl.semaphore_signal(barrier, inc=1, device_id={"col": c + 1}, device_id_type=MESH)

    mask_in = pltpu.make_async_copy(m_ref, mask, in_sem.at[0])
    mask_in.start()
    for t in range(tiles):
        tr, tc = t // tiles_c, t % tiles_c
        pltpu.make_async_copy(
            v_ref.at[tr * EDGE : (tr + 1) * EDGE, tc * EDGE : (tc + 1) * EDGE],
            by_tile.at[t], in_sem.at[1],
        ).start()
    zero_tile = jnp.zeros((EDGE, EDGE), jnp.bfloat16)
    for buf in (pack, *from_left):
        buf[live] = zero_tile
    acc[...] = jnp.zeros_like(acc)
    mask_in.wait()

    def rank_list(flags):
        count = jnp.int32(0)
        out = []
        for flag in flags:
            out.append(flag * count + (1 - flag) * live)
            count = count + flag
        return out

    flags = [mask[t // tiles_c, t % tiles_c] for t in range(tiles)]
    count = jnp.int32(0)
    upto = []
    for t in range(tiles):
        count = count + flags[t]
        upto.append(count)
    pltpu.make_async_copy(by_tile, by_tile, in_sem.at[1]).wait()
    for s in range(live):
        index = jnp.int32(0)
        for t in range(tiles - 1):
            index = index + lax.select(upto[t] <= s, jnp.int32(1), jnp.int32(0))
        pack[s] = by_tile[index]
    own_ranks = rank_list(flags)
    for t in range(tiles):
        ranks[c, t // tiles_c, t % tiles_c] = own_ranks[t]

    for tc in range(tiles_c):
        total = jnp.zeros((EDGE, EDGE), jnp.float32)
        for tr in range(tiles_r):
            total = total + pack[own_ranks[tr * tiles_c + tc]].astype(jnp.float32)
        mpart[r, :, tc * EDGE : (tc + 1) * EDGE] = jnp.sum(total, axis=0, keepdims=True)

    for tr in range(tiles_r):
        for j in range(half_tiles):
            rank = ranks[c, tr, l * half_tiles + j]
            rbuf[r, tr * EDGE : (tr + 1) * EDGE, j * EDGE : (j + 1) * EDGE] = pack[rank]

    neighbours = lax.select(c > 0, 1, 0) + lax.select(c + 1 < n_col, 1, 0)
    pl.semaphore_wait(barrier, n_row - 1 + n_layer - 1 + neighbours)

    sibling = r + 1 - 2 * lax.rem(r, 2)
    pairs = n_row // 2

    x_rows = height // X_CHUNKS

    def x_copies(k, section, target):
        span = [pl.ds(q * x_rows, x_rows) for q in range(X_CHUNKS)]
        return [
            pltpu.make_async_remote_copy(
                src_ref=rbuf.at[section, span[q]], dst_ref=rbuf.at[section, span[q]],
                send_sem=x_send.at[k, q], recv_sem=x_recv.at[k, q],
                device_id={"row": target}, device_id_type=MESH,
            )
            for q in range(X_CHUNKS)
        ]

    across = [lax.rem(r + 2 * j, n_row) for j in range(1, pairs)]
    for j, target in enumerate(across):
        for copy in x_copies(1 + j, r, target):
            copy.start()

    sends = []

    def slots(layer, ch):
        return pl.ds(layer * part + ch * chunk, chunk)

    def z_copy(way, s, ch):
        bufs = from_left if way == 0 else from_right
        src = pack if s == 1 else bufs[s - 2]
        where = slots(l, ch)
        return pltpu.make_async_remote_copy(
            src_ref=src.at[where], dst_ref=bufs[s - 1].at[where],
            send_sem=z_send.at[way, s - 1, ch], recv_sem=z_recv.at[way, s - 1, ch],
            device_id={"col": c + 1 if way == 0 else c - 1}, device_id_type=MESH,
        )

    def y_copy(way, s, ch, j, layer):
        buf = (from_left if way == 0 else from_right)[s - 1]
        where = slots(layer, ch)
        return pltpu.make_async_remote_copy(
            src_ref=buf.at[where], dst_ref=buf.at[where],
            send_sem=y_send.at[way, s - 1, ch, j - 1], recv_sem=y_recv.at[way, s - 1, ch, j - 1],
            device_id={"layer": lax.rem(l + j, n_layer)}, device_id_type=MESH,
        )

    def here(way, s):
        return c >= s if way == 0 else c + s < n_col

    def sends_on(way, s):
        if way == 0:
            return (c + 1 < n_col) & (c >= s - 1)
        return (c >= 1) & (c + s - 1 < n_col)

    def z_start(s, ch):
        for way in (0, 1):
            @pl.when(sends_on(way, s))
            def _():
                z_copy(way, s, ch).start()

    for ch in range(CHUNKS):
        z_start(1, ch)

    def to_peers(axis, me, size, ref, send, recv):
        copies = []
        for j in range(1, size):
            copy = pltpu.make_async_remote_copy(
                src_ref=ref.at[me], dst_ref=ref.at[me],
                send_sem=send.at[j - 1], recv_sem=recv.at[j - 1],
                device_id={axis: lax.rem(me + j, size)}, device_id_type=MESH,
            )
            copy.start()
            sends.append(copy)
            copies.append(copy)
        return copies

    def hand_on(ref, send, recv, way, s):
        block = c - (s - 1) if way == 0 else c + (s - 1)
        return pltpu.make_async_remote_copy(
            src_ref=ref.at[block], dst_ref=ref.at[block],
            send_sem=send.at[way, s - 1], recv_sem=recv.at[way, s - 1],
            device_id={"col": c + 1 if way == 0 else c - 1}, device_id_type=MESH,
        )

    def received(ref, send, recv, way, s):
        block = c - s if way == 0 else c + s
        return pltpu.make_async_remote_copy(
            src_ref=ref.at[block], dst_ref=ref.at[block],
            send_sem=send.at[way, s - 1], recv_sem=recv.at[way, s - 1],
            device_id={"col": c + 1 if way == 0 else c - 1}, device_id_type=MESH,
        )

    small = ((ranks, rank_send, rank_recv), (mass, ms_send, ms_recv))

    mp_copies = to_peers("row", r, n_row, mpart, mp_send, mp_recv)
    for way in (0, 1):
        @pl.when(sends_on(way, 1))
        def _():
            hand_on(*small[0], way, 1).start()

    for copy in x_copies(0, r, sibling):
        copy.start()

    for copy in mp_copies:
        copy.wait_recv()
    total = mpart[0]
    for j in range(1, n_row):
        total = total + mpart[j]
    mass[c] = total
    for way in (0, 1):
        @pl.when(sends_on(way, 1))
        def _():
            hand_on(*small[1], way, 1).start()

    def forward(s):
        for ch in range(CHUNKS):
            for way in (0, 1):
                @pl.when(here(way, s))
                def _():
                    z_copy(way, s, ch).wait_recv()
                    if s < steps:
                        @pl.when(sends_on(way, s + 1))
                        def _():
                            z_copy(way, s + 1, ch).start()
                    for j in range(1, n_layer):
                        y_copy(way, s, ch, j, l).start()
        for way in (0, 1):
            @pl.when(here(way, s))
            def _():
                for group in small:
                    received(*group, way, s).wait_recv()
                if s < steps:
                    @pl.when(sends_on(way, s + 1))
                    def _():
                        for group in small:
                            hand_on(*group, way, s + 1).start()

    def unpack(buf, block):
        scale = 1.0 / mass[block]

        def tile_row(tr, carry):
            rows = pl.ds(pl.multiple_of(tr * EDGE, EDGE), EDGE)
            for tc in range(tiles_c):
                cols = slice(tc * EDGE, (tc + 1) * EDGE)
                tile = buf[ranks[block, tr, tc]].astype(jnp.float32)
                left[block, rows, cols] = (tile * scale[:, cols]).astype(jnp.bfloat16)
            return carry

        lax.fori_loop(0, tiles_r, tile_row, 0)

    def foreign(s):
        for way in (0, 1):
            @pl.when(here(way, s))
            def _():
                for ch in range(CHUNKS):
                    for j in range(1, n_layer):
                        y_copy(way, s, ch, j, lax.rem(l + n_layer - j, n_layer)).wait_recv()
                unpack(
                    (from_left if way == 0 else from_right)[s - 1],
                    c - s if way == 0 else c + s,
                )

    chunk_rows = min(height, 512)

    def products(near, far):
        def one(block, carry):
            distance = jnp.abs(block - c)

            @pl.when((distance >= near) & (distance < far))
            def _():
                section, offset = block // per, (block % per) * width
                right = rbuf[section, pl.ds(pl.multiple_of(offset, EDGE), width), :]

                def rows(i, inner):
                    span = pl.ds(pl.multiple_of(i * chunk_rows, EDGE), chunk_rows)
                    acc[span, :] += jnp.dot(
                        left[block, span, :], right, preferred_element_type=jnp.float32
                    )
                    return inner

                lax.fori_loop(0, height // chunk_rows, rows, 0)

            return carry

        lax.fori_loop(0, n_col, one, 0)

    for s in range(1, max(steps, 2)):
        forward(s)
    for j, target in enumerate(across):
        section = lax.rem(r + n_row - 2 * (j + 1), n_row)
        for here_copy, on_copy in zip(
            x_copies(1 + j, section, target), x_copies(pairs + j, section, sibling)
        ):
            here_copy.wait_recv()
            on_copy.start()
    if steps >= 2:
        forward(steps)
    for copy in x_copies(0, sibling, sibling):
        copy.wait_recv()
    for j in range(len(across)):
        for copy in x_copies(pairs + j, lax.rem(sibling + n_row - 2 * (j + 1), n_row), sibling):
            copy.wait_recv()

    unpack(pack, c)
    for s in range(1, steps):
        foreign(s)
    products(0, steps)
    foreign(steps)
    products(steps, n_col)

    inflated = acc[...] * acc[...]
    acc[...] = inflated
    wpart[r] = jnp.sum(inflated, axis=0, keepdims=True)
    w_copies = to_peers("row", r, n_row, wpart, w_send, w_recv)

    for copy in sends:
        copy.wait_send()
    for j, target in enumerate(across):
        for copy in (*x_copies(1 + j, r, target), *x_copies(pairs + j, r, sibling)):
            copy.wait_send()
    for copy in x_copies(0, r, sibling):
        copy.wait_send()
    for s in range(1, steps + 1):
        for way in (0, 1):
            @pl.when(sends_on(way, s))
            def _():
                for ch in range(CHUNKS):
                    z_copy(way, s, ch).wait_send()
                for group in small:
                    hand_on(*group, way, s).wait_send()

            @pl.when(here(way, s))
            def _():
                for ch in range(CHUNKS):
                    for j in range(1, n_layer):
                        y_copy(way, s, ch, j, l).wait_send()

    for copy in w_copies:
        copy.wait_recv()
    total = wpart[0]
    for j in range(1, n_row):
        total = total + wpart[j]
    scale_ref[...] = (height * n_row * 1.0) / total


def scaled(inflated_ref, scale_ref, out_ref):
    out_ref[...] = inflated_ref[...] * scale_ref[...]


def shards(values, tile_mask):
    n_row, n_col, n_layer = (lax.axis_size(a) for a in ("row", "col", "layer"))
    height, width = values.shape
    tiles_r, tiles_c = tile_mask.shape
    live = tiles_r * tiles_c // 2
    half = width // n_layer
    dims = (n_row, n_col, n_layer, tiles_r, tiles_c, live)
    steps = n_col - 1
    dma = pltpu.SemaphoreType.DMA
    inflated, scale = pl.pallas_call(
        functools.partial(kernel, dims),
        out_shape=(
            pltpu.VMEM((height, half), jnp.float32),
            pltpu.VMEM((1, half), jnp.float32),
        ),
        in_specs=[pl.BlockSpec(memory_space=pl.ANY)] * 2,
        out_specs=(pl.BlockSpec(memory_space=pltpu.VMEM),) * 2,
        scratch_shapes=[
            pltpu.VMEM((tiles_r * tiles_c, EDGE, EDGE), jnp.bfloat16),
            pltpu.VMEM((live + 1, EDGE, EDGE), jnp.bfloat16),
            pltpu.VMEM((n_row, height, half), jnp.bfloat16),
            pltpu.VMEM((n_col, height, width), jnp.bfloat16),
            pltpu.SMEM((tiles_r, tiles_c), jnp.int32),
            pltpu.SMEM((n_col, tiles_r, tiles_c), jnp.int32),
            pltpu.VMEM((n_row, 1, width), jnp.float32),
            pltpu.VMEM((n_col, 1, width), jnp.float32),
            pltpu.VMEM((n_row, 1, half), jnp.float32),
            *[pltpu.VMEM((live + 1, EDGE, EDGE), jnp.bfloat16)] * steps,
            dma((2,)),
            dma((2, steps, CHUNKS)),
            dma((2, steps, CHUNKS)),
            dma((2, steps, CHUNKS, n_layer - 1)),
            dma((2, steps, CHUNKS, n_layer - 1)),
            dma((n_row, X_CHUNKS)),
            dma((n_row, X_CHUNKS)),
            dma((2, steps)),
            dma((2, steps)),
            dma((n_row - 1,)),
            dma((n_row - 1,)),
            dma((2, steps)),
            dma((2, steps)),
            dma((n_row - 1,)),
            dma((n_row - 1,)),
        ],
        compiler_params=pltpu.CompilerParams(
            collective_id=0, has_side_effects=True, vmem_limit_bytes=56 * 2**20
        ),
        name="markov_step",
    )(values, tile_mask)
    return pl.pallas_call(
        scaled,
        out_shape=jax.ShapeDtypeStruct((height, half), jnp.float32),
        in_specs=[pl.BlockSpec(memory_space=pltpu.VMEM)] * 2,
        out_specs=pl.BlockSpec(memory_space=pltpu.VMEM),
        compiler_params=pltpu.CompilerParams(vmem_limit_bytes=8 * 2**20),
        name="scaled",
    )(inflated, scale)


def solution(mesh):
    return jax.shard_map(
        shards,
        mesh=mesh,
        in_specs=(P("row", "col"), P("row", "col")),
        out_specs=P("row", ("col", "layer")),
        check_vma=False,
    )
```

```python
import functools

import jax
import jax.numpy as jnp
from jax import lax
from jax.experimental import pallas as pl
from jax.experimental.pallas import tpu as pltpu
from jax.sharding import PartitionSpec as P

MESH = pl.DeviceIdType.MESH
EDGE = 128
CHUNKS = 2


def kernel(
    dims, v_ref, m_ref, acc, scale_ref,
    by_tile, pack, rbuf, left, mask, ranks, mpart, mass, wpart, *rest,
):
    n_row, n_col, n_layer, tiles_r, tiles_c, live = dims
    steps = n_col - 1
    from_left = rest[:steps]
    from_right = from_left[::-1]
    (in_sem, z_send, z_recv, y_send, y_recv, x_send, x_recv, rank_send, rank_recv,
     mp_send, mp_recv, ms_send, ms_recv, w_send, w_recv) = rest[steps:]
    height, width = tiles_r * EDGE, tiles_c * EDGE
    half = width // n_layer
    half_tiles = tiles_c // n_layer
    tiles = tiles_r * tiles_c
    part = live // n_layer
    chunk = part // CHUNKS
    per = height // width
    r = lax.axis_index("row")
    c = lax.axis_index("col")
    l = lax.axis_index("layer")

    barrier = pltpu.get_barrier_semaphore()
    for axis, me, size in (("row", r, n_row), ("layer", l, n_layer)):
        for j in range(1, size):
            pl.semaphore_signal(
                barrier, inc=1, device_id={axis: lax.rem(me + j, size)}, device_id_type=MESH
            )

    @pl.when(c > 0)
    def _():
        pl.semaphore_signal(barrier, inc=1, device_id={"col": c - 1}, device_id_type=MESH)

    @pl.when(c + 1 < n_col)
    def _():
        pl.semaphore_signal(barrier, inc=1, device_id={"col": c + 1}, device_id_type=MESH)

    mask_in = pltpu.make_async_copy(m_ref, mask, in_sem.at[0])
    mask_in.start()
    for t in range(tiles):
        tr, tc = t // tiles_c, t % tiles_c
        pltpu.make_async_copy(
            v_ref.at[tr * EDGE : (tr + 1) * EDGE, tc * EDGE : (tc + 1) * EDGE],
            by_tile.at[t], in_sem.at[1],
        ).start()
    zero_tile = jnp.zeros((EDGE, EDGE), jnp.bfloat16)
    for buf in (pack, *from_left):
        buf[live] = zero_tile
    acc[...] = jnp.zeros_like(acc)
    mask_in.wait()

    def rank_list(flags):
        count = jnp.int32(0)
        out = []
        for flag in flags:
            out.append(flag * count + (1 - flag) * live)
            count = count + flag
        return out

    flags = [mask[t // tiles_c, t % tiles_c] for t in range(tiles)]
    count = jnp.int32(0)
    upto = []
    for t in range(tiles):
        count = count + flags[t]
        upto.append(count)
    pltpu.make_async_copy(by_tile, by_tile, in_sem.at[1]).wait()
    for s in range(live):
        index = jnp.int32(0)
        for t in range(tiles - 1):
            index = index + lax.select(upto[t] <= s, jnp.int32(1), jnp.int32(0))
        pack[s] = by_tile[index]
    own_ranks = rank_list(flags)
    for t in range(tiles):
        ranks[c, t // tiles_c, t % tiles_c] = own_ranks[t]

    for tc in range(tiles_c):
        total = jnp.zeros((EDGE, EDGE), jnp.float32)
        for tr in range(tiles_r):
            total = total + pack[own_ranks[tr * tiles_c + tc]].astype(jnp.float32)
        mpart[r, :, tc * EDGE : (tc + 1) * EDGE] = jnp.sum(total, axis=0, keepdims=True)

    neighbours = lax.select(c > 0, 1, 0) + lax.select(c + 1 < n_col, 1, 0)
    pl.semaphore_wait(barrier, n_row - 1 + n_layer - 1 + neighbours)

    sends = []

    def to_peers(axis, me, size, ref, send, recv):
        copies = []
        for j in range(1, size):
            copy = pltpu.make_async_remote_copy(
                src_ref=ref.at[me], dst_ref=ref.at[me],
                send_sem=send.at[j - 1], recv_sem=recv.at[j - 1],
                device_id={axis: lax.rem(me + j, size)}, device_id_type=MESH,
            )
            copy.start()
            sends.append(copy)
            copies.append(copy)
        return copies

    mp_copies = to_peers("row", r, n_row, mpart, mp_send, mp_recv)

    def slots(layer, ch):
        return pl.ds(layer * part + ch * chunk, chunk)

    def z_copy(way, s, ch):
        bufs = from_left if way == 0 else from_right
        src = pack if s == 1 else bufs[s - 2]
        where = slots(l, ch)
        return pltpu.make_async_remote_copy(
            src_ref=src.at[where], dst_ref=bufs[s - 1].at[where],
            send_sem=z_send.at[way, s - 1, ch], recv_sem=z_recv.at[way, s - 1, ch],
            device_id={"col": c + 1 if way == 0 else c - 1}, device_id_type=MESH,
        )

    def y_copy(way, s, ch, j, layer):
        buf = (from_left if way == 0 else from_right)[s - 1]
        where = slots(layer, ch)
        return pltpu.make_async_remote_copy(
            src_ref=buf.at[where], dst_ref=buf.at[where],
            send_sem=y_send.at[way, s - 1, ch, j - 1], recv_sem=y_recv.at[way, s - 1, ch, j - 1],
            device_id={"layer": lax.rem(l + j, n_layer)}, device_id_type=MESH,
        )

    def here(way, s):
        return c >= s if way == 0 else c + s < n_col

    def sends_on(way, s):
        if way == 0:
            return (c + 1 < n_col) & (c >= s - 1)
        return (c >= 1) & (c + s - 1 < n_col)

    def z_start(s, ch):
        for way in (0, 1):
            @pl.when(sends_on(way, s))
            def _():
                z_copy(way, s, ch).start()

    for ch in range(CHUNKS):
        z_start(1, ch)

    def hand_on(ref, send, recv, way, s):
        block = c - (s - 1) if way == 0 else c + (s - 1)
        return pltpu.make_async_remote_copy(
            src_ref=ref.at[block], dst_ref=ref.at[block],
            send_sem=send.at[way, s - 1], recv_sem=recv.at[way, s - 1],
            device_id={"col": c + 1 if way == 0 else c - 1}, device_id_type=MESH,
        )

    def received(ref, send, recv, way, s):
        block = c - s if way == 0 else c + s
        return pltpu.make_async_remote_copy(
            src_ref=ref.at[block], dst_ref=ref.at[block],
            send_sem=send.at[way, s - 1], recv_sem=recv.at[way, s - 1],
            device_id={"col": c + 1 if way == 0 else c - 1}, device_id_type=MESH,
        )

    small = ((ranks, rank_send, rank_recv), (mass, ms_send, ms_recv))

    for way in (0, 1):
        @pl.when(sends_on(way, 1))
        def _():
            hand_on(*small[0], way, 1).start()

    for tr in range(tiles_r):
        for j in range(half_tiles):
            rank = ranks[c, tr, l * half_tiles + j]
            rbuf[r, tr * EDGE : (tr + 1) * EDGE, j * EDGE : (j + 1) * EDGE] = pack[rank]

    for copy in mp_copies:
        copy.wait_recv()
    total = mpart[0]
    for j in range(1, n_row):
        total = total + mpart[j]
    mass[c] = total
    for way in (0, 1):
        @pl.when(sends_on(way, 1))
        def _():
            hand_on(*small[1], way, 1).start()

    sibling = r + 1 - 2 * lax.rem(r, 2)
    pairs = n_row // 2

    def x_copy(k, section, target):
        return pltpu.make_async_remote_copy(
            src_ref=rbuf.at[section], dst_ref=rbuf.at[section],
            send_sem=x_send.at[k], recv_sem=x_recv.at[k],
            device_id={"row": target}, device_id_type=MESH,
        )

    across = [lax.rem(r + 2 * j, n_row) for j in range(1, pairs)]
    for j, target in enumerate(across):
        x_copy(1 + j, r, target).start()
    x_copy(0, r, sibling).start()

    def forward(s):
        for ch in range(CHUNKS):
            for way in (0, 1):
                @pl.when(here(way, s))
                def _():
                    z_copy(way, s, ch).wait_recv()
                    if s < steps:
                        @pl.when(sends_on(way, s + 1))
                        def _():
                            z_copy(way, s + 1, ch).start()
                    for j in range(1, n_layer):
                        y_copy(way, s, ch, j, l).start()
        for way in (0, 1):
            @pl.when(here(way, s))
            def _():
                for group in small:
                    received(*group, way, s).wait_recv()
                if s < steps:
                    @pl.when(sends_on(way, s + 1))
                    def _():
                        for group in small:
                            hand_on(*group, way, s + 1).start()

    def unpack(buf, block):
        scale = 1.0 / mass[block]

        def tile_row(tr, carry):
            rows = pl.ds(pl.multiple_of(tr * EDGE, EDGE), EDGE)
            for tc in range(tiles_c):
                cols = slice(tc * EDGE, (tc + 1) * EDGE)
                tile = buf[ranks[block, tr, tc]].astype(jnp.float32)
                left[block, rows, cols] = (tile * scale[:, cols]).astype(jnp.bfloat16)
            return carry

        lax.fori_loop(0, tiles_r, tile_row, 0)

    def foreign(s):
        for way in (0, 1):
            @pl.when(here(way, s))
            def _():
                for ch in range(CHUNKS):
                    for j in range(1, n_layer):
                        y_copy(way, s, ch, j, lax.rem(l + n_layer - j, n_layer)).wait_recv()
                unpack(
                    (from_left if way == 0 else from_right)[s - 1],
                    c - s if way == 0 else c + s,
                )

    chunk_rows = min(height, 512)

    def products(near, far):
        def one(block, carry):
            distance = jnp.abs(block - c)

            @pl.when((distance >= near) & (distance < far))
            def _():
                section, offset = block // per, (block % per) * width
                right = rbuf[section, pl.ds(pl.multiple_of(offset, EDGE), width), :]

                def rows(i, inner):
                    span = pl.ds(pl.multiple_of(i * chunk_rows, EDGE), chunk_rows)
                    acc[span, :] += jnp.dot(
                        left[block, span, :], right, preferred_element_type=jnp.float32
                    )
                    return inner

                lax.fori_loop(0, height // chunk_rows, rows, 0)

            return carry

        lax.fori_loop(0, n_col, one, 0)

    for s in range(1, max(steps, 2)):
        forward(s)
    for j, target in enumerate(across):
        x_copy(1 + j, lax.rem(r + n_row - 2 * (j + 1), n_row), target).wait_recv()
        x_copy(pairs + j, lax.rem(r + n_row - 2 * (j + 1), n_row), sibling).start()
    x_copy(0, sibling, sibling).wait_recv()
    for j in range(len(across)):
        x_copy(pairs + j, lax.rem(sibling + n_row - 2 * (j + 1), n_row), sibling).wait_recv()
    unpack(pack, c)
    for s in range(1, steps - 1):
        foreign(s)
    products(0, max(steps - 1, 1))
    if steps >= 2:
        forward(steps)
    for s in range(max(steps - 1, 1), steps + 1):
        foreign(s)
    products(max(steps - 1, 1), n_col)

    inflated = acc[...] * acc[...]
    acc[...] = inflated
    wpart[r] = jnp.sum(inflated, axis=0, keepdims=True)
    w_copies = to_peers("row", r, n_row, wpart, w_send, w_recv)

    for copy in sends:
        copy.wait_send()
    for j, target in enumerate(across):
        x_copy(1 + j, r, target).wait_send()
        x_copy(pairs + j, r, sibling).wait_send()
    x_copy(0, r, sibling).wait_send()
    for s in range(1, steps + 1):
        for way in (0, 1):
            @pl.when(sends_on(way, s))
            def _():
                for ch in range(CHUNKS):
                    z_copy(way, s, ch).wait_send()
                for group in small:
                    hand_on(*group, way, s).wait_send()

            @pl.when(here(way, s))
            def _():
                for ch in range(CHUNKS):
                    for j in range(1, n_layer):
                        y_copy(way, s, ch, j, l).wait_send()

    for copy in w_copies:
        copy.wait_recv()
    total = wpart[0]
    for j in range(1, n_row):
        total = total + wpart[j]
    scale_ref[...] = (height * n_row * 1.0) / total


def scaled(inflated_ref, scale_ref, out_ref):
    out_ref[...] = inflated_ref[...] * scale_ref[...]


def shards(values, tile_mask):
    n_row, n_col, n_layer = (lax.axis_size(a) for a in ("row", "col", "layer"))
    height, width = values.shape
    tiles_r, tiles_c = tile_mask.shape
    live = tiles_r * tiles_c // 2
    half = width // n_layer
    dims = (n_row, n_col, n_layer, tiles_r, tiles_c, live)
    steps = n_col - 1
    dma = pltpu.SemaphoreType.DMA
    inflated, scale = pl.pallas_call(
        functools.partial(kernel, dims),
        out_shape=(
            pltpu.VMEM((height, half), jnp.float32),
            pltpu.VMEM((1, half), jnp.float32),
        ),
        in_specs=[pl.BlockSpec(memory_space=pl.ANY)] * 2,
        out_specs=(pl.BlockSpec(memory_space=pltpu.VMEM),) * 2,
        scratch_shapes=[
            pltpu.VMEM((tiles_r * tiles_c, EDGE, EDGE), jnp.bfloat16),
            pltpu.VMEM((live + 1, EDGE, EDGE), jnp.bfloat16),
            pltpu.VMEM((n_row, height, half), jnp.bfloat16),
            pltpu.VMEM((n_col, height, width), jnp.bfloat16),
            pltpu.SMEM((tiles_r, tiles_c), jnp.int32),
            pltpu.SMEM((n_col, tiles_r, tiles_c), jnp.int32),
            pltpu.VMEM((n_row, 1, width), jnp.float32),
            pltpu.VMEM((n_col, 1, width), jnp.float32),
            pltpu.VMEM((n_row, 1, half), jnp.float32),
            *[pltpu.VMEM((live + 1, EDGE, EDGE), jnp.bfloat16)] * steps,
            dma((2,)),
            dma((2, steps, CHUNKS)),
            dma((2, steps, CHUNKS)),
            dma((2, steps, CHUNKS, n_layer - 1)),
            dma((2, steps, CHUNKS, n_layer - 1)),
            dma((n_row,)),
            dma((n_row,)),
            dma((2, steps)),
            dma((2, steps)),
            dma((n_row - 1,)),
            dma((n_row - 1,)),
            dma((2, steps)),
            dma((2, steps)),
            dma((n_row - 1,)),
            dma((n_row - 1,)),
        ],
        compiler_params=pltpu.CompilerParams(
            collective_id=0, has_side_effects=True, vmem_limit_bytes=56 * 2**20
        ),
        name="markov_step",
    )(values, tile_mask)
    return pl.pallas_call(
        scaled,
        out_shape=jax.ShapeDtypeStruct((height, half), jnp.float32),
        in_specs=[pl.BlockSpec(memory_space=pltpu.VMEM)] * 2,
        out_specs=pl.BlockSpec(memory_space=pltpu.VMEM),
        compiler_params=pltpu.CompilerParams(vmem_limit_bytes=8 * 2**20),
        name="scaled",
    )(inflated, scale)


def solution(mesh):
    return jax.shard_map(
        shards,
        mesh=mesh,
        in_specs=(P("row", "col"), P("row", "col")),
        out_specs=P("row", ("col", "layer")),
        check_vma=False,
    )
```

```python
import functools

import jax
import jax.numpy as jnp
from jax import lax
from jax.experimental import pallas as pl
from jax.experimental.pallas import tpu as pltpu
from jax.sharding import PartitionSpec as P

MESH = pl.DeviceIdType.MESH
EDGE = 128
CHUNKS = 2


def kernel(
    dims, v_ref, m_ref, acc, scale_ref,
    by_tile, pack, rbuf, left, mask, ranks, mpart, mass, wpart, *rest,
):
    n_row, n_col, n_layer, tiles_r, tiles_c, live = dims
    steps = n_col - 1
    from_left = rest[:steps]
    from_right = from_left[::-1]
    (in_sem, z_send, z_recv, y_send, y_recv, x_send, x_recv, rank_send, rank_recv,
     mp_send, mp_recv, ms_send, ms_recv, w_send, w_recv) = rest[steps:]
    height, width = tiles_r * EDGE, tiles_c * EDGE
    half = width // n_layer
    half_tiles = tiles_c // n_layer
    tiles = tiles_r * tiles_c
    part = live // n_layer
    chunk = part // CHUNKS
    per = height // width
    r = lax.axis_index("row")
    c = lax.axis_index("col")
    l = lax.axis_index("layer")

    barrier = pltpu.get_barrier_semaphore()
    for axis, me, size in (("row", r, n_row), ("layer", l, n_layer)):
        for j in range(1, size):
            pl.semaphore_signal(
                barrier, inc=1, device_id={axis: lax.rem(me + j, size)}, device_id_type=MESH
            )

    @pl.when(c > 0)
    def _():
        pl.semaphore_signal(barrier, inc=1, device_id={"col": c - 1}, device_id_type=MESH)

    @pl.when(c + 1 < n_col)
    def _():
        pl.semaphore_signal(barrier, inc=1, device_id={"col": c + 1}, device_id_type=MESH)

    mask_in = pltpu.make_async_copy(m_ref, mask, in_sem.at[0])
    mask_in.start()
    for t in range(tiles):
        tr, tc = t // tiles_c, t % tiles_c
        pltpu.make_async_copy(
            v_ref.at[tr * EDGE : (tr + 1) * EDGE, tc * EDGE : (tc + 1) * EDGE],
            by_tile.at[t], in_sem.at[1],
        ).start()
    zero_tile = jnp.zeros((EDGE, EDGE), jnp.bfloat16)
    for buf in (pack, *from_left):
        buf[live] = zero_tile
    acc[...] = jnp.zeros_like(acc)
    mask_in.wait()

    def rank_list(flags):
        count = jnp.int32(0)
        out = []
        for flag in flags:
            out.append(flag * count + (1 - flag) * live)
            count = count + flag
        return out

    flags = [mask[t // tiles_c, t % tiles_c] for t in range(tiles)]
    count = jnp.int32(0)
    upto = []
    for t in range(tiles):
        count = count + flags[t]
        upto.append(count)
    pltpu.make_async_copy(by_tile, by_tile, in_sem.at[1]).wait()
    for s in range(live):
        index = jnp.int32(0)
        for t in range(tiles - 1):
            index = index + lax.select(upto[t] <= s, jnp.int32(1), jnp.int32(0))
        pack[s] = by_tile[index]
    own_ranks = rank_list(flags)
    for t in range(tiles):
        ranks[c, t // tiles_c, t % tiles_c] = own_ranks[t]

    for tc in range(tiles_c):
        total = jnp.zeros((EDGE, EDGE), jnp.float32)
        for tr in range(tiles_r):
            total = total + pack[own_ranks[tr * tiles_c + tc]].astype(jnp.float32)
        mpart[r, :, tc * EDGE : (tc + 1) * EDGE] = jnp.sum(total, axis=0, keepdims=True)

    neighbours = lax.select(c > 0, 1, 0) + lax.select(c + 1 < n_col, 1, 0)
    pl.semaphore_wait(barrier, n_row - 1 + n_layer - 1 + neighbours)

    sends = []

    def to_peers(axis, me, size, ref, send, recv):
        copies = []
        for j in range(1, size):
            copy = pltpu.make_async_remote_copy(
                src_ref=ref.at[me], dst_ref=ref.at[me],
                send_sem=send.at[j - 1], recv_sem=recv.at[j - 1],
                device_id={axis: lax.rem(me + j, size)}, device_id_type=MESH,
            )
            copy.start()
            sends.append(copy)
            copies.append(copy)
        return copies

    mp_copies = to_peers("row", r, n_row, mpart, mp_send, mp_recv)

    def slots(layer, ch):
        return pl.ds(layer * part + ch * chunk, chunk)

    def z_copy(way, s, ch):
        bufs = from_left if way == 0 else from_right
        src = pack if s == 1 else bufs[s - 2]
        where = slots(l, ch)
        return pltpu.make_async_remote_copy(
            src_ref=src.at[where], dst_ref=bufs[s - 1].at[where],
            send_sem=z_send.at[way, s - 1, ch], recv_sem=z_recv.at[way, s - 1, ch],
            device_id={"col": c + 1 if way == 0 else c - 1}, device_id_type=MESH,
        )

    def y_copy(way, s, ch, j, layer):
        buf = (from_left if way == 0 else from_right)[s - 1]
        where = slots(layer, ch)
        return pltpu.make_async_remote_copy(
            src_ref=buf.at[where], dst_ref=buf.at[where],
            send_sem=y_send.at[way, s - 1, ch, j - 1], recv_sem=y_recv.at[way, s - 1, ch, j - 1],
            device_id={"layer": lax.rem(l + j, n_layer)}, device_id_type=MESH,
        )

    def here(way, s):
        return c >= s if way == 0 else c + s < n_col

    def sends_on(way, s):
        if way == 0:
            return (c + 1 < n_col) & (c >= s - 1)
        return (c >= 1) & (c + s - 1 < n_col)

    def z_start(s, ch):
        for way in (0, 1):
            @pl.when(sends_on(way, s))
            def _():
                z_copy(way, s, ch).start()

    for ch in range(CHUNKS):
        z_start(1, ch)

    def hand_on(ref, send, recv, way, s):
        block = c - (s - 1) if way == 0 else c + (s - 1)
        return pltpu.make_async_remote_copy(
            src_ref=ref.at[block], dst_ref=ref.at[block],
            send_sem=send.at[way, s - 1], recv_sem=recv.at[way, s - 1],
            device_id={"col": c + 1 if way == 0 else c - 1}, device_id_type=MESH,
        )

    def received(ref, send, recv, way, s):
        block = c - s if way == 0 else c + s
        return pltpu.make_async_remote_copy(
            src_ref=ref.at[block], dst_ref=ref.at[block],
            send_sem=send.at[way, s - 1], recv_sem=recv.at[way, s - 1],
            device_id={"col": c + 1 if way == 0 else c - 1}, device_id_type=MESH,
        )

    small = ((ranks, rank_send, rank_recv), (mass, ms_send, ms_recv))

    for way in (0, 1):
        @pl.when(sends_on(way, 1))
        def _():
            hand_on(*small[0], way, 1).start()

    for tr in range(tiles_r):
        for j in range(half_tiles):
            rank = ranks[c, tr, l * half_tiles + j]
            rbuf[r, tr * EDGE : (tr + 1) * EDGE, j * EDGE : (j + 1) * EDGE] = pack[rank]

    sibling = r + 1 - 2 * lax.rem(r, 2)
    pairs = n_row // 2

    def x_copy(k, section, target):
        return pltpu.make_async_remote_copy(
            src_ref=rbuf.at[section], dst_ref=rbuf.at[section],
            send_sem=x_send.at[k], recv_sem=x_recv.at[k],
            device_id={"row": target}, device_id_type=MESH,
        )

    across = [lax.rem(r + 2 * j, n_row) for j in range(1, pairs)]
    def x_start():
        for j, target in enumerate(across):
            x_copy(1 + j, r, target).start()
        x_copy(0, r, sibling).start()

    at_end = (c == 0) | (c == n_col - 1)

    @pl.when(at_end)
    def _():
        x_start()

    for copy in mp_copies:
        copy.wait_recv()
    total = mpart[0]
    for j in range(1, n_row):
        total = total + mpart[j]
    mass[c] = total
    for way in (0, 1):
        @pl.when(sends_on(way, 1))
        def _():
            hand_on(*small[1], way, 1).start()

    def forward(s):
        for ch in range(CHUNKS):
            for way in (0, 1):
                @pl.when(here(way, s))
                def _():
                    z_copy(way, s, ch).wait_recv()
                    if s < steps:
                        @pl.when(sends_on(way, s + 1))
                        def _():
                            z_copy(way, s + 1, ch).start()
                    for j in range(1, n_layer):
                        y_copy(way, s, ch, j, l).start()
        for way in (0, 1):
            @pl.when(here(way, s))
            def _():
                for group in small:
                    received(*group, way, s).wait_recv()
                if s < steps:
                    @pl.when(sends_on(way, s + 1))
                    def _():
                        for group in small:
                            hand_on(*group, way, s + 1).start()

    def unpack(buf, block):
        scale = 1.0 / mass[block]

        def tile_row(tr, carry):
            rows = pl.ds(pl.multiple_of(tr * EDGE, EDGE), EDGE)
            for tc in range(tiles_c):
                cols = slice(tc * EDGE, (tc + 1) * EDGE)
                tile = buf[ranks[block, tr, tc]].astype(jnp.float32)
                left[block, rows, cols] = (tile * scale[:, cols]).astype(jnp.bfloat16)
            return carry

        lax.fori_loop(0, tiles_r, tile_row, 0)

    def foreign(s):
        for way in (0, 1):
            @pl.when(here(way, s))
            def _():
                for ch in range(CHUNKS):
                    for j in range(1, n_layer):
                        y_copy(way, s, ch, j, lax.rem(l + n_layer - j, n_layer)).wait_recv()
                unpack(
                    (from_left if way == 0 else from_right)[s - 1],
                    c - s if way == 0 else c + s,
                )

    chunk_rows = min(height, 512)

    def products(near, far):
        def one(block, carry):
            distance = jnp.abs(block - c)

            @pl.when((distance >= near) & (distance < far))
            def _():
                section, offset = block // per, (block % per) * width
                right = rbuf[section, pl.ds(pl.multiple_of(offset, EDGE), width), :]

                def rows(i, inner):
                    span = pl.ds(pl.multiple_of(i * chunk_rows, EDGE), chunk_rows)
                    acc[span, :] += jnp.dot(
                        left[block, span, :], right, preferred_element_type=jnp.float32
                    )
                    return inner

                lax.fori_loop(0, height // chunk_rows, rows, 0)

            return carry

        lax.fori_loop(0, n_col, one, 0)

    for s in range(1, max(steps, 2)):
        forward(s)
        if s == 1:
            @pl.when(jnp.logical_not(at_end))
            def _():
                x_start()
    for j, target in enumerate(across):
        x_copy(1 + j, lax.rem(r + n_row - 2 * (j + 1), n_row), target).wait_recv()
        x_copy(pairs + j, lax.rem(r + n_row - 2 * (j + 1), n_row), sibling).start()
    if steps >= 2:
        forward(steps)
    x_copy(0, sibling, sibling).wait_recv()
    for j in range(len(across)):
        x_copy(pairs + j, lax.rem(sibling + n_row - 2 * (j + 1), n_row), sibling).wait_recv()
    unpack(pack, c)
    for s in range(1, steps):
        foreign(s)
    products(0, steps)
    foreign(steps)
    products(steps, n_col)

    inflated = acc[...] * acc[...]
    acc[...] = inflated
    wpart[r] = jnp.sum(inflated, axis=0, keepdims=True)
    w_copies = to_peers("row", r, n_row, wpart, w_send, w_recv)

    for copy in sends:
        copy.wait_send()
    for j, target in enumerate(across):
        x_copy(1 + j, r, target).wait_send()
        x_copy(pairs + j, r, sibling).wait_send()
    x_copy(0, r, sibling).wait_send()
    for s in range(1, steps + 1):
        for way in (0, 1):
            @pl.when(sends_on(way, s))
            def _():
                for ch in range(CHUNKS):
                    z_copy(way, s, ch).wait_send()
                for group in small:
                    hand_on(*group, way, s).wait_send()

            @pl.when(here(way, s))
            def _():
                for ch in range(CHUNKS):
                    for j in range(1, n_layer):
                        y_copy(way, s, ch, j, l).wait_send()

    for copy in w_copies:
        copy.wait_recv()
    total = wpart[0]
    for j in range(1, n_row):
        total = total + wpart[j]
    scale_ref[...] = (height * n_row * 1.0) / total


def scaled(inflated_ref, scale_ref, out_ref):
    out_ref[...] = inflated_ref[...] * scale_ref[...]


def shards(values, tile_mask):
    n_row, n_col, n_layer = (lax.axis_size(a) for a in ("row", "col", "layer"))
    height, width = values.shape
    tiles_r, tiles_c = tile_mask.shape
    live = tiles_r * tiles_c // 2
    half = width // n_layer
    dims = (n_row, n_col, n_layer, tiles_r, tiles_c, live)
    steps = n_col - 1
    dma = pltpu.SemaphoreType.DMA
    inflated, scale = pl.pallas_call(
        functools.partial(kernel, dims),
        out_shape=(
            pltpu.VMEM((height, half), jnp.float32),
            pltpu.VMEM((1, half), jnp.float32),
        ),
        in_specs=[pl.BlockSpec(memory_space=pl.ANY)] * 2,
        out_specs=(pl.BlockSpec(memory_space=pltpu.VMEM),) * 2,
        scratch_shapes=[
            pltpu.VMEM((tiles_r * tiles_c, EDGE, EDGE), jnp.bfloat16),
            pltpu.VMEM((live + 1, EDGE, EDGE), jnp.bfloat16),
            pltpu.VMEM((n_row, height, half), jnp.bfloat16),
            pltpu.VMEM((n_col, height, width), jnp.bfloat16),
            pltpu.SMEM((tiles_r, tiles_c), jnp.int32),
            pltpu.SMEM((n_col, tiles_r, tiles_c), jnp.int32),
            pltpu.VMEM((n_row, 1, width), jnp.float32),
            pltpu.VMEM((n_col, 1, width), jnp.float32),
            pltpu.VMEM((n_row, 1, half), jnp.float32),
            *[pltpu.VMEM((live + 1, EDGE, EDGE), jnp.bfloat16)] * steps,
            dma((2,)),
            dma((2, steps, CHUNKS)),
            dma((2, steps, CHUNKS)),
            dma((2, steps, CHUNKS, n_layer - 1)),
            dma((2, steps, CHUNKS, n_layer - 1)),
            dma((n_row,)),
            dma((n_row,)),
            dma((2, steps)),
            dma((2, steps)),
            dma((n_row - 1,)),
            dma((n_row - 1,)),
            dma((2, steps)),
            dma((2, steps)),
            dma((n_row - 1,)),
            dma((n_row - 1,)),
        ],
        compiler_params=pltpu.CompilerParams(
            collective_id=0, has_side_effects=True, vmem_limit_bytes=56 * 2**20
        ),
        name="markov_step",
    )(values, tile_mask)
    return pl.pallas_call(
        scaled,
        out_shape=jax.ShapeDtypeStruct((height, half), jnp.float32),
        in_specs=[pl.BlockSpec(memory_space=pltpu.VMEM)] * 2,
        out_specs=pl.BlockSpec(memory_space=pltpu.VMEM),
        compiler_params=pltpu.CompilerParams(vmem_limit_bytes=8 * 2**20),
        name="scaled",
    )(inflated, scale)


def solution(mesh):
    return jax.shard_map(
        shards,
        mesh=mesh,
        in_specs=(P("row", "col"), P("row", "col")),
        out_specs=P("row", ("col", "layer")),
        check_vma=False,
    )
```

```python
import functools

import jax
import jax.numpy as jnp
from jax import lax
from jax.experimental import pallas as pl
from jax.experimental.pallas import tpu as pltpu
from jax.sharding import PartitionSpec as P

MESH = pl.DeviceIdType.MESH
EDGE = 128
CHUNKS = 2


def kernel(
    dims, v_ref, m_ref, acc, scale_ref,
    by_tile, pack, rbuf, left, mask, ranks, mpart, mass, wpart, *rest,
):
    n_row, n_col, n_layer, tiles_r, tiles_c, live = dims
    steps = n_col - 1
    from_left = rest[:steps]
    from_right = from_left[::-1]
    (in_sem, z_send, z_recv, y_send, y_recv, x_send, x_recv, rank_send, rank_recv,
     mp_send, mp_recv, ms_send, ms_recv, w_send, w_recv) = rest[steps:]
    height, width = tiles_r * EDGE, tiles_c * EDGE
    half = width // n_layer
    half_tiles = tiles_c // n_layer
    tiles = tiles_r * tiles_c
    part = live // n_layer
    chunk = part // CHUNKS
    per = height // width
    r = lax.axis_index("row")
    c = lax.axis_index("col")
    l = lax.axis_index("layer")

    barrier = pltpu.get_barrier_semaphore()
    for axis, me, size in (("row", r, n_row), ("layer", l, n_layer)):
        for j in range(1, size):
            pl.semaphore_signal(
                barrier, inc=1, device_id={axis: lax.rem(me + j, size)}, device_id_type=MESH
            )

    @pl.when(c > 0)
    def _():
        pl.semaphore_signal(barrier, inc=1, device_id={"col": c - 1}, device_id_type=MESH)

    @pl.when(c + 1 < n_col)
    def _():
        pl.semaphore_signal(barrier, inc=1, device_id={"col": c + 1}, device_id_type=MESH)

    mask_in = pltpu.make_async_copy(m_ref, mask, in_sem.at[0])
    mask_in.start()
    for t in range(tiles):
        tr, tc = t // tiles_c, t % tiles_c
        pltpu.make_async_copy(
            v_ref.at[tr * EDGE : (tr + 1) * EDGE, tc * EDGE : (tc + 1) * EDGE],
            by_tile.at[t], in_sem.at[1],
        ).start()
    zero_tile = jnp.zeros((EDGE, EDGE), jnp.bfloat16)
    for buf in (pack, *from_left):
        buf[live] = zero_tile
    acc[...] = jnp.zeros_like(acc)
    mask_in.wait()

    def rank_list(flags):
        count = jnp.int32(0)
        out = []
        for flag in flags:
            out.append(flag * count + (1 - flag) * live)
            count = count + flag
        return out

    flags = [mask[t // tiles_c, t % tiles_c] for t in range(tiles)]
    count = jnp.int32(0)
    upto = []
    for t in range(tiles):
        count = count + flags[t]
        upto.append(count)
    pltpu.make_async_copy(by_tile, by_tile, in_sem.at[1]).wait()
    for s in range(live):
        index = jnp.int32(0)
        for t in range(tiles - 1):
            index = index + lax.select(upto[t] <= s, jnp.int32(1), jnp.int32(0))
        pack[s] = by_tile[index]
    own_ranks = rank_list(flags)
    for t in range(tiles):
        ranks[c, t // tiles_c, t % tiles_c] = own_ranks[t]

    for tc in range(tiles_c):
        total = jnp.zeros((EDGE, EDGE), jnp.float32)
        for tr in range(tiles_r):
            total = total + pack[own_ranks[tr * tiles_c + tc]].astype(jnp.float32)
        mpart[r, :, tc * EDGE : (tc + 1) * EDGE] = jnp.sum(total, axis=0, keepdims=True)

    neighbours = lax.select(c > 0, 1, 0) + lax.select(c + 1 < n_col, 1, 0)
    pl.semaphore_wait(barrier, n_row - 1 + n_layer - 1 + neighbours)

    sends = []

    def to_peers(axis, me, size, ref, send, recv):
        copies = []
        for j in range(1, size):
            copy = pltpu.make_async_remote_copy(
                src_ref=ref.at[me], dst_ref=ref.at[me],
                send_sem=send.at[j - 1], recv_sem=recv.at[j - 1],
                device_id={axis: lax.rem(me + j, size)}, device_id_type=MESH,
            )
            copy.start()
            sends.append(copy)
            copies.append(copy)
        return copies

    mp_copies = to_peers("row", r, n_row, mpart, mp_send, mp_recv)

    def slots(layer, ch):
        return pl.ds(layer * part + ch * chunk, chunk)

    def z_copy(way, s, ch):
        bufs = from_left if way == 0 else from_right
        src = pack if s == 1 else bufs[s - 2]
        where = slots(l, ch)
        return pltpu.make_async_remote_copy(
            src_ref=src.at[where], dst_ref=bufs[s - 1].at[where],
            send_sem=z_send.at[way, s - 1, ch], recv_sem=z_recv.at[way, s - 1, ch],
            device_id={"col": c + 1 if way == 0 else c - 1}, device_id_type=MESH,
        )

    def y_copy(way, s, ch, j, layer):
        buf = (from_left if way == 0 else from_right)[s - 1]
        where = slots(layer, ch)
        return pltpu.make_async_remote_copy(
            src_ref=buf.at[where], dst_ref=buf.at[where],
            send_sem=y_send.at[way, s - 1, ch, j - 1], recv_sem=y_recv.at[way, s - 1, ch, j - 1],
            device_id={"layer": lax.rem(l + j, n_layer)}, device_id_type=MESH,
        )

    def here(way, s):
        return c >= s if way == 0 else c + s < n_col

    def sends_on(way, s):
        if way == 0:
            return (c + 1 < n_col) & (c >= s - 1)
        return (c >= 1) & (c + s - 1 < n_col)

    def z_start(s, ch):
        for way in (0, 1):
            @pl.when(sends_on(way, s))
            def _():
                z_copy(way, s, ch).start()

    for ch in range(CHUNKS):
        z_start(1, ch)

    def hand_on(ref, send, recv, way, s):
        block = c - (s - 1) if way == 0 else c + (s - 1)
        return pltpu.make_async_remote_copy(
            src_ref=ref.at[block], dst_ref=ref.at[block],
            send_sem=send.at[way, s - 1], recv_sem=recv.at[way, s - 1],
            device_id={"col": c + 1 if way == 0 else c - 1}, device_id_type=MESH,
        )

    def received(ref, send, recv, way, s):
        block = c - s if way == 0 else c + s
        return pltpu.make_async_remote_copy(
            src_ref=ref.at[block], dst_ref=ref.at[block],
            send_sem=send.at[way, s - 1], recv_sem=recv.at[way, s - 1],
            device_id={"col": c + 1 if way == 0 else c - 1}, device_id_type=MESH,
        )

    small = ((ranks, rank_send, rank_recv), (mass, ms_send, ms_recv))

    for way in (0, 1):
        @pl.when(sends_on(way, 1))
        def _():
            hand_on(*small[0], way, 1).start()

    for tr in range(tiles_r):
        for j in range(half_tiles):
            rank = ranks[c, tr, l * half_tiles + j]
            rbuf[r, tr * EDGE : (tr + 1) * EDGE, j * EDGE : (j + 1) * EDGE] = pack[rank]

    sibling = r + 1 - 2 * lax.rem(r, 2)
    pairs = n_row // 2

    def x_copy(k, section, target):
        return pltpu.make_async_remote_copy(
            src_ref=rbuf.at[section], dst_ref=rbuf.at[section],
            send_sem=x_send.at[k], recv_sem=x_recv.at[k],
            device_id={"row": target}, device_id_type=MESH,
        )

    across = [lax.rem(r + 2 * j, n_row) for j in range(1, pairs)]
    def x_start():
        for j, target in enumerate(across):
            x_copy(1 + j, r, target).start()

    at_end = (c == 0) | (c == n_col - 1)

    @pl.when(at_end)
    def _():
        x_start()

    for copy in mp_copies:
        copy.wait_recv()
    total = mpart[0]
    for j in range(1, n_row):
        total = total + mpart[j]
    mass[c] = total
    for way in (0, 1):
        @pl.when(sends_on(way, 1))
        def _():
            hand_on(*small[1], way, 1).start()

    def forward(s):
        for ch in range(CHUNKS):
            for way in (0, 1):
                @pl.when(here(way, s))
                def _():
                    z_copy(way, s, ch).wait_recv()
                    if s < steps:
                        @pl.when(sends_on(way, s + 1))
                        def _():
                            z_copy(way, s + 1, ch).start()
                    for j in range(1, n_layer):
                        y_copy(way, s, ch, j, l).start()
        for way in (0, 1):
            @pl.when(here(way, s))
            def _():
                for group in small:
                    received(*group, way, s).wait_recv()
                if s < steps:
                    @pl.when(sends_on(way, s + 1))
                    def _():
                        for group in small:
                            hand_on(*group, way, s + 1).start()

    def unpack(buf, block):
        scale = 1.0 / mass[block]

        def tile_row(tr, carry):
            rows = pl.ds(pl.multiple_of(tr * EDGE, EDGE), EDGE)
            for tc in range(tiles_c):
                cols = slice(tc * EDGE, (tc + 1) * EDGE)
                tile = buf[ranks[block, tr, tc]].astype(jnp.float32)
                left[block, rows, cols] = (tile * scale[:, cols]).astype(jnp.bfloat16)
            return carry

        lax.fori_loop(0, tiles_r, tile_row, 0)

    def foreign(s):
        for way in (0, 1):
            @pl.when(here(way, s))
            def _():
                for ch in range(CHUNKS):
                    for j in range(1, n_layer):
                        y_copy(way, s, ch, j, lax.rem(l + n_layer - j, n_layer)).wait_recv()
                unpack(
                    (from_left if way == 0 else from_right)[s - 1],
                    c - s if way == 0 else c + s,
                )

    chunk_rows = min(height, 512)

    def products(near, far):
        def one(block, carry):
            distance = jnp.abs(block - c)

            @pl.when((distance >= near) & (distance < far))
            def _():
                section, offset = block // per, (block % per) * width
                right = rbuf[section, pl.ds(pl.multiple_of(offset, EDGE), width), :]

                def rows(i, inner):
                    span = pl.ds(pl.multiple_of(i * chunk_rows, EDGE), chunk_rows)
                    acc[span, :] += jnp.dot(
                        left[block, span, :], right, preferred_element_type=jnp.float32
                    )
                    return inner

                lax.fori_loop(0, height // chunk_rows, rows, 0)

            return carry

        lax.fori_loop(0, n_col, one, 0)

    for s in range(1, max(steps, 2)):
        forward(s)
        if s == 1:
            @pl.when(jnp.logical_not(at_end))
            def _():
                x_start()
    x_copy(0, r, sibling).start()
    for j, target in enumerate(across):
        x_copy(1 + j, lax.rem(r + n_row - 2 * (j + 1), n_row), target).wait_recv()
        x_copy(pairs + j, lax.rem(r + n_row - 2 * (j + 1), n_row), sibling).start()
    if steps >= 2:
        forward(steps)
    x_copy(0, sibling, sibling).wait_recv()
    for j in range(len(across)):
        x_copy(pairs + j, lax.rem(sibling + n_row - 2 * (j + 1), n_row), sibling).wait_recv()
    unpack(pack, c)
    for s in range(1, steps):
        foreign(s)
    products(0, steps)
    foreign(steps)
    products(steps, n_col)

    inflated = acc[...] * acc[...]
    acc[...] = inflated
    wpart[r] = jnp.sum(inflated, axis=0, keepdims=True)
    w_copies = to_peers("row", r, n_row, wpart, w_send, w_recv)

    for copy in sends:
        copy.wait_send()
    for j, target in enumerate(across):
        x_copy(1 + j, r, target).wait_send()
        x_copy(pairs + j, r, sibling).wait_send()
    x_copy(0, r, sibling).wait_send()
    for s in range(1, steps + 1):
        for way in (0, 1):
            @pl.when(sends_on(way, s))
            def _():
                for ch in range(CHUNKS):
                    z_copy(way, s, ch).wait_send()
                for group in small:
                    hand_on(*group, way, s).wait_send()

            @pl.when(here(way, s))
            def _():
                for ch in range(CHUNKS):
                    for j in range(1, n_layer):
                        y_copy(way, s, ch, j, l).wait_send()

    for copy in w_copies:
        copy.wait_recv()
    total = wpart[0]
    for j in range(1, n_row):
        total = total + wpart[j]
    scale_ref[...] = (height * n_row * 1.0) / total


def scaled(inflated_ref, scale_ref, out_ref):
    out_ref[...] = inflated_ref[...] * scale_ref[...]


def shards(values, tile_mask):
    n_row, n_col, n_layer = (lax.axis_size(a) for a in ("row", "col", "layer"))
    height, width = values.shape
    tiles_r, tiles_c = tile_mask.shape
    live = tiles_r * tiles_c // 2
    half = width // n_layer
    dims = (n_row, n_col, n_layer, tiles_r, tiles_c, live)
    steps = n_col - 1
    dma = pltpu.SemaphoreType.DMA
    inflated, scale = pl.pallas_call(
        functools.partial(kernel, dims),
        out_shape=(
            pltpu.VMEM((height, half), jnp.float32),
            pltpu.VMEM((1, half), jnp.float32),
        ),
        in_specs=[pl.BlockSpec(memory_space=pl.ANY)] * 2,
        out_specs=(pl.BlockSpec(memory_space=pltpu.VMEM),) * 2,
        scratch_shapes=[
            pltpu.VMEM((tiles_r * tiles_c, EDGE, EDGE), jnp.bfloat16),
            pltpu.VMEM((live + 1, EDGE, EDGE), jnp.bfloat16),
            pltpu.VMEM((n_row, height, half), jnp.bfloat16),
            pltpu.VMEM((n_col, height, width), jnp.bfloat16),
            pltpu.SMEM((tiles_r, tiles_c), jnp.int32),
            pltpu.SMEM((n_col, tiles_r, tiles_c), jnp.int32),
            pltpu.VMEM((n_row, 1, width), jnp.float32),
            pltpu.VMEM((n_col, 1, width), jnp.float32),
            pltpu.VMEM((n_row, 1, half), jnp.float32),
            *[pltpu.VMEM((live + 1, EDGE, EDGE), jnp.bfloat16)] * steps,
            dma((2,)),
            dma((2, steps, CHUNKS)),
            dma((2, steps, CHUNKS)),
            dma((2, steps, CHUNKS, n_layer - 1)),
            dma((2, steps, CHUNKS, n_layer - 1)),
            dma((n_row,)),
            dma((n_row,)),
            dma((2, steps)),
            dma((2, steps)),
            dma((n_row - 1,)),
            dma((n_row - 1,)),
            dma((2, steps)),
            dma((2, steps)),
            dma((n_row - 1,)),
            dma((n_row - 1,)),
        ],
        compiler_params=pltpu.CompilerParams(
            collective_id=0, has_side_effects=True, vmem_limit_bytes=56 * 2**20
        ),
        name="markov_step",
    )(values, tile_mask)
    return pl.pallas_call(
        scaled,
        out_shape=jax.ShapeDtypeStruct((height, half), jnp.float32),
        in_specs=[pl.BlockSpec(memory_space=pltpu.VMEM)] * 2,
        out_specs=pl.BlockSpec(memory_space=pltpu.VMEM),
        compiler_params=pltpu.CompilerParams(vmem_limit_bytes=8 * 2**20),
        name="scaled",
    )(inflated, scale)


def solution(mesh):
    return jax.shard_map(
        shards,
        mesh=mesh,
        in_specs=(P("row", "col"), P("row", "col")),
        out_specs=P("row", ("col", "layer")),
        check_vma=False,
    )
```

```python
import functools

import jax
import jax.numpy as jnp
from jax import lax
from jax.experimental import pallas as pl
from jax.experimental.pallas import tpu as pltpu
from jax.sharding import PartitionSpec as P

MESH = pl.DeviceIdType.MESH
EDGE = 128
CHUNKS = 4


def kernel(
    dims, v_ref, m_ref, acc, scale_ref,
    by_tile, pack, rbuf, left, mask, ranks, mpart, mass, wpart, *rest,
):
    n_row, n_col, n_layer, tiles_r, tiles_c, live = dims
    steps = n_col - 1
    from_left = rest[:steps]
    from_right = from_left[::-1]
    (in_sem, z_send, z_recv, y_send, y_recv, x_send, x_recv, rank_send, rank_recv,
     mp_send, mp_recv, ms_send, ms_recv, w_send, w_recv) = rest[steps:]
    height, width = tiles_r * EDGE, tiles_c * EDGE
    half = width // n_layer
    half_tiles = tiles_c // n_layer
    tiles = tiles_r * tiles_c
    part = live // n_layer
    chunk = part // CHUNKS
    per = height // width
    r = lax.axis_index("row")
    c = lax.axis_index("col")
    l = lax.axis_index("layer")

    barrier = pltpu.get_barrier_semaphore()
    for axis, me, size in (("row", r, n_row), ("layer", l, n_layer)):
        for j in range(1, size):
            pl.semaphore_signal(
                barrier, inc=1, device_id={axis: lax.rem(me + j, size)}, device_id_type=MESH
            )

    @pl.when(c > 0)
    def _():
        pl.semaphore_signal(barrier, inc=1, device_id={"col": c - 1}, device_id_type=MESH)

    @pl.when(c + 1 < n_col)
    def _():
        pl.semaphore_signal(barrier, inc=1, device_id={"col": c + 1}, device_id_type=MESH)

    mask_in = pltpu.make_async_copy(m_ref, mask, in_sem.at[0])
    mask_in.start()
    for t in range(tiles):
        tr, tc = t // tiles_c, t % tiles_c
        pltpu.make_async_copy(
            v_ref.at[tr * EDGE : (tr + 1) * EDGE, tc * EDGE : (tc + 1) * EDGE],
            by_tile.at[t], in_sem.at[1],
        ).start()
    zero_tile = jnp.zeros((EDGE, EDGE), jnp.bfloat16)
    for buf in (pack, *from_left):
        buf[live] = zero_tile
    acc[...] = jnp.zeros_like(acc)
    mask_in.wait()

    def rank_list(flags):
        count = jnp.int32(0)
        out = []
        for flag in flags:
            out.append(flag * count + (1 - flag) * live)
            count = count + flag
        return out

    flags = [mask[t // tiles_c, t % tiles_c] for t in range(tiles)]
    count = jnp.int32(0)
    upto = []
    for t in range(tiles):
        count = count + flags[t]
        upto.append(count)
    pltpu.make_async_copy(by_tile, by_tile, in_sem.at[1]).wait()
    for s in range(live):
        index = jnp.int32(0)
        for t in range(tiles - 1):
            index = index + lax.select(upto[t] <= s, jnp.int32(1), jnp.int32(0))
        pack[s] = by_tile[index]
    own_ranks = rank_list(flags)
    for t in range(tiles):
        ranks[c, t // tiles_c, t % tiles_c] = own_ranks[t]

    for tc in range(tiles_c):
        total = jnp.zeros((EDGE, EDGE), jnp.float32)
        for tr in range(tiles_r):
            total = total + pack[own_ranks[tr * tiles_c + tc]].astype(jnp.float32)
        mpart[r, :, tc * EDGE : (tc + 1) * EDGE] = jnp.sum(total, axis=0, keepdims=True)

    neighbours = lax.select(c > 0, 1, 0) + lax.select(c + 1 < n_col, 1, 0)
    pl.semaphore_wait(barrier, n_row - 1 + n_layer - 1 + neighbours)

    sends = []

    def to_peers(axis, me, size, ref, send, recv):
        copies = []
        for j in range(1, size):
            copy = pltpu.make_async_remote_copy(
                src_ref=ref.at[me], dst_ref=ref.at[me],
                send_sem=send.at[j - 1], recv_sem=recv.at[j - 1],
                device_id={axis: lax.rem(me + j, size)}, device_id_type=MESH,
            )
            copy.start()
            sends.append(copy)
            copies.append(copy)
        return copies

    mp_copies = to_peers("row", r, n_row, mpart, mp_send, mp_recv)

    def slots(layer, ch):
        return pl.ds(layer * part + ch * chunk, chunk)

    def z_copy(way, s, ch):
        bufs = from_left if way == 0 else from_right
        src = pack if s == 1 else bufs[s - 2]
        where = slots(l, ch)
        return pltpu.make_async_remote_copy(
            src_ref=src.at[where], dst_ref=bufs[s - 1].at[where],
            send_sem=z_send.at[way, s - 1, ch], recv_sem=z_recv.at[way, s - 1, ch],
            device_id={"col": c + 1 if way == 0 else c - 1}, device_id_type=MESH,
        )

    def y_copy(way, s, ch, j, layer):
        buf = (from_left if way == 0 else from_right)[s - 1]
        where = slots(layer, ch)
        return pltpu.make_async_remote_copy(
            src_ref=buf.at[where], dst_ref=buf.at[where],
            send_sem=y_send.at[way, s - 1, ch, j - 1], recv_sem=y_recv.at[way, s - 1, ch, j - 1],
            device_id={"layer": lax.rem(l + j, n_layer)}, device_id_type=MESH,
        )

    def here(way, s):
        return c >= s if way == 0 else c + s < n_col

    def sends_on(way, s):
        if way == 0:
            return (c + 1 < n_col) & (c >= s - 1)
        return (c >= 1) & (c + s - 1 < n_col)

    def z_start(s, ch):
        for way in (0, 1):
            @pl.when(sends_on(way, s))
            def _():
                z_copy(way, s, ch).start()

    for ch in range(CHUNKS):
        z_start(1, ch)

    def hand_on(ref, send, recv, way, s):
        block = c - (s - 1) if way == 0 else c + (s - 1)
        return pltpu.make_async_remote_copy(
            src_ref=ref.at[block], dst_ref=ref.at[block],
            send_sem=send.at[way, s - 1], recv_sem=recv.at[way, s - 1],
            device_id={"col": c + 1 if way == 0 else c - 1}, device_id_type=MESH,
        )

    def received(ref, send, recv, way, s):
        block = c - s if way == 0 else c + s
        return pltpu.make_async_remote_copy(
            src_ref=ref.at[block], dst_ref=ref.at[block],
            send_sem=send.at[way, s - 1], recv_sem=recv.at[way, s - 1],
            device_id={"col": c + 1 if way == 0 else c - 1}, device_id_type=MESH,
        )

    small = ((ranks, rank_send, rank_recv), (mass, ms_send, ms_recv))

    for way in (0, 1):
        @pl.when(sends_on(way, 1))
        def _():
            hand_on(*small[0], way, 1).start()

    for tr in range(tiles_r):
        for j in range(half_tiles):
            rank = ranks[c, tr, l * half_tiles + j]
            rbuf[r, tr * EDGE : (tr + 1) * EDGE, j * EDGE : (j + 1) * EDGE] = pack[rank]

    sibling = r + 1 - 2 * lax.rem(r, 2)
    pairs = n_row // 2

    def x_copy(k, section, target):
        return pltpu.make_async_remote_copy(
            src_ref=rbuf.at[section], dst_ref=rbuf.at[section],
            send_sem=x_send.at[k], recv_sem=x_recv.at[k],
            device_id={"row": target}, device_id_type=MESH,
        )

    across = [lax.rem(r + 2 * j, n_row) for j in range(1, pairs)]
    def x_start():
        for j, target in enumerate(across):
            x_copy(1 + j, r, target).start()

    at_end = (c == 0) | (c == n_col - 1)

    @pl.when(at_end)
    def _():
        x_start()

    for copy in mp_copies:
        copy.wait_recv()
    total = mpart[0]
    for j in range(1, n_row):
        total = total + mpart[j]
    mass[c] = total
    for way in (0, 1):
        @pl.when(sends_on(way, 1))
        def _():
            hand_on(*small[1], way, 1).start()

    def forward(s):
        for ch in range(CHUNKS):
            for way in (0, 1):
                @pl.when(here(way, s))
                def _():
                    z_copy(way, s, ch).wait_recv()
                    if s < steps:
                        @pl.when(sends_on(way, s + 1))
                        def _():
                            z_copy(way, s + 1, ch).start()
                    for j in range(1, n_layer):
                        y_copy(way, s, ch, j, l).start()
        for way in (0, 1):
            @pl.when(here(way, s))
            def _():
                for group in small:
                    received(*group, way, s).wait_recv()
                if s < steps:
                    @pl.when(sends_on(way, s + 1))
                    def _():
                        for group in small:
                            hand_on(*group, way, s + 1).start()

    def unpack(buf, block):
        scale = 1.0 / mass[block]

        def tile_row(tr, carry):
            rows = pl.ds(pl.multiple_of(tr * EDGE, EDGE), EDGE)
            for tc in range(tiles_c):
                cols = slice(tc * EDGE, (tc + 1) * EDGE)
                tile = buf[ranks[block, tr, tc]].astype(jnp.float32)
                left[block, rows, cols] = (tile * scale[:, cols]).astype(jnp.bfloat16)
            return carry

        lax.fori_loop(0, tiles_r, tile_row, 0)

    def foreign(s):
        for way in (0, 1):
            @pl.when(here(way, s))
            def _():
                for ch in range(CHUNKS):
                    for j in range(1, n_layer):
                        y_copy(way, s, ch, j, lax.rem(l + n_layer - j, n_layer)).wait_recv()
                unpack(
                    (from_left if way == 0 else from_right)[s - 1],
                    c - s if way == 0 else c + s,
                )

    chunk_rows = min(height, 512)

    def products(near, far):
        def one(block, carry):
            distance = jnp.abs(block - c)

            @pl.when((distance >= near) & (distance < far))
            def _():
                section, offset = block // per, (block % per) * width
                right = rbuf[section, pl.ds(pl.multiple_of(offset, EDGE), width), :]

                def rows(i, inner):
                    span = pl.ds(pl.multiple_of(i * chunk_rows, EDGE), chunk_rows)
                    acc[span, :] += jnp.dot(
                        left[block, span, :], right, preferred_element_type=jnp.float32
                    )
                    return inner

                lax.fori_loop(0, height // chunk_rows, rows, 0)

            return carry

        lax.fori_loop(0, n_col, one, 0)

    for s in range(1, max(steps, 2)):
        forward(s)
        if s == 1:
            @pl.when(jnp.logical_not(at_end))
            def _():
                x_start()
    x_copy(0, r, sibling).start()
    for j, target in enumerate(across):
        x_copy(1 + j, lax.rem(r + n_row - 2 * (j + 1), n_row), target).wait_recv()
        x_copy(pairs + j, lax.rem(r + n_row - 2 * (j + 1), n_row), sibling).start()
    if steps >= 2:
        forward(steps)
    x_copy(0, sibling, sibling).wait_recv()
    for j in range(len(across)):
        x_copy(pairs + j, lax.rem(sibling + n_row - 2 * (j + 1), n_row), sibling).wait_recv()
    unpack(pack, c)
    for s in range(1, steps):
        foreign(s)
    products(0, steps)
    foreign(steps)
    products(steps, n_col)

    inflated = acc[...] * acc[...]
    acc[...] = inflated
    wpart[r] = jnp.sum(inflated, axis=0, keepdims=True)
    w_copies = to_peers("row", r, n_row, wpart, w_send, w_recv)

    for copy in sends:
        copy.wait_send()
    for j, target in enumerate(across):
        x_copy(1 + j, r, target).wait_send()
        x_copy(pairs + j, r, sibling).wait_send()
    x_copy(0, r, sibling).wait_send()
    for s in range(1, steps + 1):
        for way in (0, 1):
            @pl.when(sends_on(way, s))
            def _():
                for ch in range(CHUNKS):
                    z_copy(way, s, ch).wait_send()
                for group in small:
                    hand_on(*group, way, s).wait_send()

            @pl.when(here(way, s))
            def _():
                for ch in range(CHUNKS):
                    for j in range(1, n_layer):
                        y_copy(way, s, ch, j, l).wait_send()

    for copy in w_copies:
        copy.wait_recv()
    total = wpart[0]
    for j in range(1, n_row):
        total = total + wpart[j]
    scale_ref[...] = (height * n_row * 1.0) / total


def scaled(inflated_ref, scale_ref, out_ref):
    out_ref[...] = inflated_ref[...] * scale_ref[...]


def shards(values, tile_mask):
    n_row, n_col, n_layer = (lax.axis_size(a) for a in ("row", "col", "layer"))
    height, width = values.shape
    tiles_r, tiles_c = tile_mask.shape
    live = tiles_r * tiles_c // 2
    half = width // n_layer
    dims = (n_row, n_col, n_layer, tiles_r, tiles_c, live)
    steps = n_col - 1
    dma = pltpu.SemaphoreType.DMA
    inflated, scale = pl.pallas_call(
        functools.partial(kernel, dims),
        out_shape=(
            pltpu.VMEM((height, half), jnp.float32),
            pltpu.VMEM((1, half), jnp.float32),
        ),
        in_specs=[pl.BlockSpec(memory_space=pl.ANY)] * 2,
        out_specs=(pl.BlockSpec(memory_space=pltpu.VMEM),) * 2,
        scratch_shapes=[
            pltpu.VMEM((tiles_r * tiles_c, EDGE, EDGE), jnp.bfloat16),
            pltpu.VMEM((live + 1, EDGE, EDGE), jnp.bfloat16),
            pltpu.VMEM((n_row, height, half), jnp.bfloat16),
            pltpu.VMEM((n_col, height, width), jnp.bfloat16),
            pltpu.SMEM((tiles_r, tiles_c), jnp.int32),
            pltpu.SMEM((n_col, tiles_r, tiles_c), jnp.int32),
            pltpu.VMEM((n_row, 1, width), jnp.float32),
            pltpu.VMEM((n_col, 1, width), jnp.float32),
            pltpu.VMEM((n_row, 1, half), jnp.float32),
            *[pltpu.VMEM((live + 1, EDGE, EDGE), jnp.bfloat16)] * steps,
            dma((2,)),
            dma((2, steps, CHUNKS)),
            dma((2, steps, CHUNKS)),
            dma((2, steps, CHUNKS, n_layer - 1)),
            dma((2, steps, CHUNKS, n_layer - 1)),
            dma((n_row,)),
            dma((n_row,)),
            dma((2, steps)),
            dma((2, steps)),
            dma((n_row - 1,)),
            dma((n_row - 1,)),
            dma((2, steps)),
            dma((2, steps)),
            dma((n_row - 1,)),
            dma((n_row - 1,)),
        ],
        compiler_params=pltpu.CompilerParams(
            collective_id=0, has_side_effects=True, vmem_limit_bytes=56 * 2**20
        ),
        name="markov_step",
    )(values, tile_mask)
    return pl.pallas_call(
        scaled,
        out_shape=jax.ShapeDtypeStruct((height, half), jnp.float32),
        in_specs=[pl.BlockSpec(memory_space=pltpu.VMEM)] * 2,
        out_specs=pl.BlockSpec(memory_space=pltpu.VMEM),
        compiler_params=pltpu.CompilerParams(vmem_limit_bytes=8 * 2**20),
        name="scaled",
    )(inflated, scale)


def solution(mesh):
    return jax.shard_map(
        shards,
        mesh=mesh,
        in_specs=(P("row", "col"), P("row", "col")),
        out_specs=P("row", ("col", "layer")),
        check_vma=False,
    )
```

```python
import functools

import jax
import jax.numpy as jnp
from jax import lax
from jax.experimental import pallas as pl
from jax.experimental.pallas import tpu as pltpu
from jax.sharding import PartitionSpec as P

MESH = pl.DeviceIdType.MESH
EDGE = 128
CHUNKS = 4


def kernel(
    dims, v_ref, m_ref, acc, scale_ref,
    by_tile, pack, rbuf, left, mask, ranks, mpart, mass, wpart, *rest,
):
    n_row, n_col, n_layer, tiles_r, tiles_c, live = dims
    steps = n_col - 1
    from_left = rest[:steps]
    from_right = from_left[::-1]
    (in_sem, z_send, z_recv, y_send, y_recv, x_send, x_recv, rank_send, rank_recv,
     mp_send, mp_recv, ms_send, ms_recv, w_send, w_recv) = rest[steps:]
    height, width = tiles_r * EDGE, tiles_c * EDGE
    half = width // n_layer
    half_tiles = tiles_c // n_layer
    tiles = tiles_r * tiles_c
    part = live // n_layer
    chunk = part // CHUNKS
    per = height // width
    r = lax.axis_index("row")
    c = lax.axis_index("col")
    l = lax.axis_index("layer")

    barrier = pltpu.get_barrier_semaphore()
    for axis, me, size in (("row", r, n_row), ("layer", l, n_layer)):
        for j in range(1, size):
            pl.semaphore_signal(
                barrier, inc=1, device_id={axis: lax.rem(me + j, size)}, device_id_type=MESH
            )

    @pl.when(c > 0)
    def _():
        pl.semaphore_signal(barrier, inc=1, device_id={"col": c - 1}, device_id_type=MESH)

    @pl.when(c + 1 < n_col)
    def _():
        pl.semaphore_signal(barrier, inc=1, device_id={"col": c + 1}, device_id_type=MESH)

    mask_in = pltpu.make_async_copy(m_ref, mask, in_sem.at[0])
    mask_in.start()
    for t in range(tiles):
        tr, tc = t // tiles_c, t % tiles_c
        pltpu.make_async_copy(
            v_ref.at[tr * EDGE : (tr + 1) * EDGE, tc * EDGE : (tc + 1) * EDGE],
            by_tile.at[t], in_sem.at[1],
        ).start()
    zero_tile = jnp.zeros((EDGE, EDGE), jnp.bfloat16)
    for buf in (pack, *from_left):
        buf[live] = zero_tile
    acc[...] = jnp.zeros_like(acc)
    mask_in.wait()

    def rank_list(flags):
        count = jnp.int32(0)
        out = []
        for flag in flags:
            out.append(flag * count + (1 - flag) * live)
            count = count + flag
        return out

    flags = [mask[t // tiles_c, t % tiles_c] for t in range(tiles)]
    count = jnp.int32(0)
    upto = []
    for t in range(tiles):
        count = count + flags[t]
        upto.append(count)
    pltpu.make_async_copy(by_tile, by_tile, in_sem.at[1]).wait()
    for s in range(live):
        index = jnp.int32(0)
        for t in range(tiles - 1):
            index = index + lax.select(upto[t] <= s, jnp.int32(1), jnp.int32(0))
        pack[s] = by_tile[index]
    own_ranks = rank_list(flags)
    for t in range(tiles):
        ranks[c, t // tiles_c, t % tiles_c] = own_ranks[t]

    for tc in range(tiles_c):
        total = jnp.zeros((EDGE, EDGE), jnp.float32)
        for tr in range(tiles_r):
            total = total + pack[own_ranks[tr * tiles_c + tc]].astype(jnp.float32)
        mpart[r, :, tc * EDGE : (tc + 1) * EDGE] = jnp.sum(total, axis=0, keepdims=True)

    neighbours = lax.select(c > 0, 1, 0) + lax.select(c + 1 < n_col, 1, 0)
    pl.semaphore_wait(barrier, n_row - 1 + n_layer - 1 + neighbours)

    sends = []

    def to_peers(axis, me, size, ref, send, recv):
        copies = []
        for j in range(1, size):
            copy = pltpu.make_async_remote_copy(
                src_ref=ref.at[me], dst_ref=ref.at[me],
                send_sem=send.at[j - 1], recv_sem=recv.at[j - 1],
                device_id={axis: lax.rem(me + j, size)}, device_id_type=MESH,
            )
            copy.start()
            sends.append(copy)
            copies.append(copy)
        return copies

    mp_copies = to_peers("row", r, n_row, mpart, mp_send, mp_recv)

    def slots(layer, ch):
        return pl.ds(layer * part + ch * chunk, chunk)

    def z_copy(way, s, ch):
        bufs = from_left if way == 0 else from_right
        src = pack if s == 1 else bufs[s - 2]
        where = slots(l, ch)
        return pltpu.make_async_remote_copy(
            src_ref=src.at[where], dst_ref=bufs[s - 1].at[where],
            send_sem=z_send.at[way, s - 1, ch], recv_sem=z_recv.at[way, s - 1, ch],
            device_id={"col": c + 1 if way == 0 else c - 1}, device_id_type=MESH,
        )

    def y_copy(way, s, ch, j, layer):
        buf = (from_left if way == 0 else from_right)[s - 1]
        where = slots(layer, ch)
        return pltpu.make_async_remote_copy(
            src_ref=buf.at[where], dst_ref=buf.at[where],
            send_sem=y_send.at[way, s - 1, ch, j - 1], recv_sem=y_recv.at[way, s - 1, ch, j - 1],
            device_id={"layer": lax.rem(l + j, n_layer)}, device_id_type=MESH,
        )

    def here(way, s):
        return c >= s if way == 0 else c + s < n_col

    def sends_on(way, s):
        if way == 0:
            return (c + 1 < n_col) & (c >= s - 1)
        return (c >= 1) & (c + s - 1 < n_col)

    def z_start(s, ch):
        for way in (0, 1):
            @pl.when(sends_on(way, s))
            def _():
                z_copy(way, s, ch).start()

    for ch in range(CHUNKS):
        z_start(1, ch)

    def hand_on(ref, send, recv, way, s):
        block = c - (s - 1) if way == 0 else c + (s - 1)
        return pltpu.make_async_remote_copy(
            src_ref=ref.at[block], dst_ref=ref.at[block],
            send_sem=send.at[way, s - 1], recv_sem=recv.at[way, s - 1],
            device_id={"col": c + 1 if way == 0 else c - 1}, device_id_type=MESH,
        )

    def received(ref, send, recv, way, s):
        block = c - s if way == 0 else c + s
        return pltpu.make_async_remote_copy(
            src_ref=ref.at[block], dst_ref=ref.at[block],
            send_sem=send.at[way, s - 1], recv_sem=recv.at[way, s - 1],
            device_id={"col": c + 1 if way == 0 else c - 1}, device_id_type=MESH,
        )

    small = ((ranks, rank_send, rank_recv), (mass, ms_send, ms_recv))

    for way in (0, 1):
        @pl.when(sends_on(way, 1))
        def _():
            hand_on(*small[0], way, 1).start()

    for tr in range(tiles_r):
        for j in range(half_tiles):
            rank = ranks[c, tr, l * half_tiles + j]
            rbuf[r, tr * EDGE : (tr + 1) * EDGE, j * EDGE : (j + 1) * EDGE] = pack[rank]

    sibling = r + 1 - 2 * lax.rem(r, 2)
    pairs = n_row // 2

    def x_copy(k, section, target):
        return pltpu.make_async_remote_copy(
            src_ref=rbuf.at[section], dst_ref=rbuf.at[section],
            send_sem=x_send.at[k], recv_sem=x_recv.at[k],
            device_id={"row": target}, device_id_type=MESH,
        )

    across = [lax.rem(r + 2 * j, n_row) for j in range(1, pairs)]
    def x_start():
        for j, target in enumerate(across):
            x_copy(1 + j, r, target).start()

    at_end = (c == 0) | (c == n_col - 1)

    @pl.when(at_end)
    def _():
        x_start()

    for copy in mp_copies:
        copy.wait_recv()
    total = mpart[0]
    for j in range(1, n_row):
        total = total + mpart[j]
    mass[c] = total
    for way in (0, 1):
        @pl.when(sends_on(way, 1))
        def _():
            hand_on(*small[1], way, 1).start()

    def forward(s):
        for ch in range(CHUNKS):
            for way in (0, 1):
                @pl.when(here(way, s))
                def _():
                    z_copy(way, s, ch).wait_recv()
                    if s < steps:
                        @pl.when(sends_on(way, s + 1))
                        def _():
                            z_copy(way, s + 1, ch).start()
                    for j in range(1, n_layer):
                        y_copy(way, s, ch, j, l).start()
        if s == 1:
            @pl.when(jnp.logical_not(at_end))
            def _():
                x_start()
        for way in (0, 1):
            @pl.when(here(way, s))
            def _():
                for group in small:
                    received(*group, way, s).wait_recv()
                if s < steps:
                    @pl.when(sends_on(way, s + 1))
                    def _():
                        for group in small:
                            hand_on(*group, way, s + 1).start()

    def unpack(buf, block):
        scale = 1.0 / mass[block]

        def tile_row(tr, carry):
            rows = pl.ds(pl.multiple_of(tr * EDGE, EDGE), EDGE)
            for tc in range(tiles_c):
                cols = slice(tc * EDGE, (tc + 1) * EDGE)
                tile = buf[ranks[block, tr, tc]].astype(jnp.float32)
                left[block, rows, cols] = (tile * scale[:, cols]).astype(jnp.bfloat16)
            return carry

        lax.fori_loop(0, tiles_r, tile_row, 0)

    def foreign(s):
        for way in (0, 1):
            @pl.when(here(way, s))
            def _():
                for ch in range(CHUNKS):
                    for j in range(1, n_layer):
                        y_copy(way, s, ch, j, lax.rem(l + n_layer - j, n_layer)).wait_recv()
                unpack(
                    (from_left if way == 0 else from_right)[s - 1],
                    c - s if way == 0 else c + s,
                )

    chunk_rows = min(height, 512)

    def products(near, far):
        def one(block, carry):
            distance = jnp.abs(block - c)

            @pl.when((distance >= near) & (distance < far))
            def _():
                section, offset = block // per, (block % per) * width
                right = rbuf[section, pl.ds(pl.multiple_of(offset, EDGE), width), :]

                def rows(i, inner):
                    span = pl.ds(pl.multiple_of(i * chunk_rows, EDGE), chunk_rows)
                    acc[span, :] += jnp.dot(
                        left[block, span, :], right, preferred_element_type=jnp.float32
                    )
                    return inner

                lax.fori_loop(0, height // chunk_rows, rows, 0)

            return carry

        lax.fori_loop(0, n_col, one, 0)

    for s in range(1, max(steps, 2)):
        forward(s)
    x_copy(0, r, sibling).start()
    for j, target in enumerate(across):
        x_copy(1 + j, lax.rem(r + n_row - 2 * (j + 1), n_row), target).wait_recv()
        x_copy(pairs + j, lax.rem(r + n_row - 2 * (j + 1), n_row), sibling).start()
    if steps >= 2:
        forward(steps)
    x_copy(0, sibling, sibling).wait_recv()
    for j in range(len(across)):
        x_copy(pairs + j, lax.rem(sibling + n_row - 2 * (j + 1), n_row), sibling).wait_recv()
    unpack(pack, c)
    for s in range(1, steps):
        foreign(s)
    products(0, steps)
    foreign(steps)
    products(steps, n_col)

    inflated = acc[...] * acc[...]
    acc[...] = inflated
    wpart[r] = jnp.sum(inflated, axis=0, keepdims=True)
    w_copies = to_peers("row", r, n_row, wpart, w_send, w_recv)

    for copy in sends:
        copy.wait_send()
    for j, target in enumerate(across):
        x_copy(1 + j, r, target).wait_send()
        x_copy(pairs + j, r, sibling).wait_send()
    x_copy(0, r, sibling).wait_send()
    for s in range(1, steps + 1):
        for way in (0, 1):
            @pl.when(sends_on(way, s))
            def _():
                for ch in range(CHUNKS):
                    z_copy(way, s, ch).wait_send()
                for group in small:
                    hand_on(*group, way, s).wait_send()

            @pl.when(here(way, s))
            def _():
                for ch in range(CHUNKS):
                    for j in range(1, n_layer):
                        y_copy(way, s, ch, j, l).wait_send()

    for copy in w_copies:
        copy.wait_recv()
    total = wpart[0]
    for j in range(1, n_row):
        total = total + wpart[j]
    scale_ref[...] = (height * n_row * 1.0) / total


def scaled(inflated_ref, scale_ref, out_ref):
    out_ref[...] = inflated_ref[...] * scale_ref[...]


def shards(values, tile_mask):
    n_row, n_col, n_layer = (lax.axis_size(a) for a in ("row", "col", "layer"))
    height, width = values.shape
    tiles_r, tiles_c = tile_mask.shape
    live = tiles_r * tiles_c // 2
    half = width // n_layer
    dims = (n_row, n_col, n_layer, tiles_r, tiles_c, live)
    steps = n_col - 1
    dma = pltpu.SemaphoreType.DMA
    inflated, scale = pl.pallas_call(
        functools.partial(kernel, dims),
        out_shape=(
            pltpu.VMEM((height, half), jnp.float32),
            pltpu.VMEM((1, half), jnp.float32),
        ),
        in_specs=[pl.BlockSpec(memory_space=pl.ANY)] * 2,
        out_specs=(pl.BlockSpec(memory_space=pltpu.VMEM),) * 2,
        scratch_shapes=[
            pltpu.VMEM((tiles_r * tiles_c, EDGE, EDGE), jnp.bfloat16),
            pltpu.VMEM((live + 1, EDGE, EDGE), jnp.bfloat16),
            pltpu.VMEM((n_row, height, half), jnp.bfloat16),
            pltpu.VMEM((n_col, height, width), jnp.bfloat16),
            pltpu.SMEM((tiles_r, tiles_c), jnp.int32),
            pltpu.SMEM((n_col, tiles_r, tiles_c), jnp.int32),
            pltpu.VMEM((n_row, 1, width), jnp.float32),
            pltpu.VMEM((n_col, 1, width), jnp.float32),
            pltpu.VMEM((n_row, 1, half), jnp.float32),
            *[pltpu.VMEM((live + 1, EDGE, EDGE), jnp.bfloat16)] * steps,
            dma((2,)),
            dma((2, steps, CHUNKS)),
            dma((2, steps, CHUNKS)),
            dma((2, steps, CHUNKS, n_layer - 1)),
            dma((2, steps, CHUNKS, n_layer - 1)),
            dma((n_row,)),
            dma((n_row,)),
            dma((2, steps)),
            dma((2, steps)),
            dma((n_row - 1,)),
            dma((n_row - 1,)),
            dma((2, steps)),
            dma((2, steps)),
            dma((n_row - 1,)),
            dma((n_row - 1,)),
        ],
        compiler_params=pltpu.CompilerParams(
            collective_id=0, has_side_effects=True, vmem_limit_bytes=56 * 2**20
        ),
        name="markov_step",
    )(values, tile_mask)
    return pl.pallas_call(
        scaled,
        out_shape=jax.ShapeDtypeStruct((height, half), jnp.float32),
        in_specs=[pl.BlockSpec(memory_space=pltpu.VMEM)] * 2,
        out_specs=pl.BlockSpec(memory_space=pltpu.VMEM),
        compiler_params=pltpu.CompilerParams(vmem_limit_bytes=8 * 2**20),
        name="scaled",
    )(inflated, scale)


def solution(mesh):
    return jax.shard_map(
        shards,
        mesh=mesh,
        in_specs=(P("row", "col"), P("row", "col")),
        out_specs=P("row", ("col", "layer")),
        check_vma=False,
    )
```

```python
import functools

import jax
import jax.numpy as jnp
from jax import lax
from jax.experimental import pallas as pl
from jax.experimental.pallas import tpu as pltpu
from jax.sharding import PartitionSpec as P

MESH = pl.DeviceIdType.MESH
EDGE = 128
CHUNKS = 4
X_CHUNKS = 2


def kernel(
    dims, v_ref, m_ref, acc, scale_ref,
    by_tile, pack, rbuf, left, mask, ranks, mpart, mass, wpart, *rest,
):
    n_row, n_col, n_layer, tiles_r, tiles_c, live = dims
    steps = n_col - 1
    from_left = rest[:steps]
    from_right = from_left[::-1]
    (in_sem, z_send, z_recv, y_send, y_recv, x_send, x_recv, rank_send, rank_recv,
     mp_send, mp_recv, ms_send, ms_recv, w_send, w_recv) = rest[steps:]
    height, width = tiles_r * EDGE, tiles_c * EDGE
    half = width // n_layer
    half_tiles = tiles_c // n_layer
    tiles = tiles_r * tiles_c
    part = live // n_layer
    chunk = part // CHUNKS
    per = height // width
    r = lax.axis_index("row")
    c = lax.axis_index("col")
    l = lax.axis_index("layer")

    barrier = pltpu.get_barrier_semaphore()
    for axis, me, size in (("row", r, n_row), ("layer", l, n_layer)):
        for j in range(1, size):
            pl.semaphore_signal(
                barrier, inc=1, device_id={axis: lax.rem(me + j, size)}, device_id_type=MESH
            )

    @pl.when(c > 0)
    def _():
        pl.semaphore_signal(barrier, inc=1, device_id={"col": c - 1}, device_id_type=MESH)

    @pl.when(c + 1 < n_col)
    def _():
        pl.semaphore_signal(barrier, inc=1, device_id={"col": c + 1}, device_id_type=MESH)

    mask_in = pltpu.make_async_copy(m_ref, mask, in_sem.at[0])
    mask_in.start()
    for t in range(tiles):
        tr, tc = t // tiles_c, t % tiles_c
        pltpu.make_async_copy(
            v_ref.at[tr * EDGE : (tr + 1) * EDGE, tc * EDGE : (tc + 1) * EDGE],
            by_tile.at[t], in_sem.at[1],
        ).start()
    zero_tile = jnp.zeros((EDGE, EDGE), jnp.bfloat16)
    for buf in (pack, *from_left):
        buf[live] = zero_tile
    acc[...] = jnp.zeros_like(acc)
    mask_in.wait()

    def rank_list(flags):
        count = jnp.int32(0)
        out = []
        for flag in flags:
            out.append(flag * count + (1 - flag) * live)
            count = count + flag
        return out

    flags = [mask[t // tiles_c, t % tiles_c] for t in range(tiles)]
    count = jnp.int32(0)
    upto = []
    for t in range(tiles):
        count = count + flags[t]
        upto.append(count)
    pltpu.make_async_copy(by_tile, by_tile, in_sem.at[1]).wait()
    for s in range(live):
        index = jnp.int32(0)
        for t in range(tiles - 1):
            index = index + lax.select(upto[t] <= s, jnp.int32(1), jnp.int32(0))
        pack[s] = by_tile[index]
    own_ranks = rank_list(flags)
    for t in range(tiles):
        ranks[c, t // tiles_c, t % tiles_c] = own_ranks[t]

    for tc in range(tiles_c):
        total = jnp.zeros((EDGE, EDGE), jnp.float32)
        for tr in range(tiles_r):
            total = total + pack[own_ranks[tr * tiles_c + tc]].astype(jnp.float32)
        mpart[r, :, tc * EDGE : (tc + 1) * EDGE] = jnp.sum(total, axis=0, keepdims=True)

    neighbours = lax.select(c > 0, 1, 0) + lax.select(c + 1 < n_col, 1, 0)
    pl.semaphore_wait(barrier, n_row - 1 + n_layer - 1 + neighbours)

    sends = []

    def to_peers(axis, me, size, ref, send, recv):
        copies = []
        for j in range(1, size):
            copy = pltpu.make_async_remote_copy(
                src_ref=ref.at[me], dst_ref=ref.at[me],
                send_sem=send.at[j - 1], recv_sem=recv.at[j - 1],
                device_id={axis: lax.rem(me + j, size)}, device_id_type=MESH,
            )
            copy.start()
            sends.append(copy)
            copies.append(copy)
        return copies

    mp_copies = to_peers("row", r, n_row, mpart, mp_send, mp_recv)

    def slots(layer, ch):
        return pl.ds(layer * part + ch * chunk, chunk)

    def z_copy(way, s, ch):
        bufs = from_left if way == 0 else from_right
        src = pack if s == 1 else bufs[s - 2]
        where = slots(l, ch)
        return pltpu.make_async_remote_copy(
            src_ref=src.at[where], dst_ref=bufs[s - 1].at[where],
            send_sem=z_send.at[way, s - 1, ch], recv_sem=z_recv.at[way, s - 1, ch],
            device_id={"col": c + 1 if way == 0 else c - 1}, device_id_type=MESH,
        )

    def y_copy(way, s, ch, j, layer):
        buf = (from_left if way == 0 else from_right)[s - 1]
        where = slots(layer, ch)
        return pltpu.make_async_remote_copy(
            src_ref=buf.at[where], dst_ref=buf.at[where],
            send_sem=y_send.at[way, s - 1, ch, j - 1], recv_sem=y_recv.at[way, s - 1, ch, j - 1],
            device_id={"layer": lax.rem(l + j, n_layer)}, device_id_type=MESH,
        )

    def here(way, s):
        return c >= s if way == 0 else c + s < n_col

    def sends_on(way, s):
        if way == 0:
            return (c + 1 < n_col) & (c >= s - 1)
        return (c >= 1) & (c + s - 1 < n_col)

    def z_start(s, ch):
        for way in (0, 1):
            @pl.when(sends_on(way, s))
            def _():
                z_copy(way, s, ch).start()

    for ch in range(CHUNKS):
        z_start(1, ch)

    def hand_on(ref, send, recv, way, s):
        block = c - (s - 1) if way == 0 else c + (s - 1)
        return pltpu.make_async_remote_copy(
            src_ref=ref.at[block], dst_ref=ref.at[block],
            send_sem=send.at[way, s - 1], recv_sem=recv.at[way, s - 1],
            device_id={"col": c + 1 if way == 0 else c - 1}, device_id_type=MESH,
        )

    def received(ref, send, recv, way, s):
        block = c - s if way == 0 else c + s
        return pltpu.make_async_remote_copy(
            src_ref=ref.at[block], dst_ref=ref.at[block],
            send_sem=send.at[way, s - 1], recv_sem=recv.at[way, s - 1],
            device_id={"col": c + 1 if way == 0 else c - 1}, device_id_type=MESH,
        )

    small = ((ranks, rank_send, rank_recv), (mass, ms_send, ms_recv))

    for way in (0, 1):
        @pl.when(sends_on(way, 1))
        def _():
            hand_on(*small[0], way, 1).start()

    for tr in range(tiles_r):
        for j in range(half_tiles):
            rank = ranks[c, tr, l * half_tiles + j]
            rbuf[r, tr * EDGE : (tr + 1) * EDGE, j * EDGE : (j + 1) * EDGE] = pack[rank]

    sibling = r + 1 - 2 * lax.rem(r, 2)
    pairs = n_row // 2

    x_rows = height // X_CHUNKS

    def x_copy(k, section, target, q):
        rows = pl.ds(q * x_rows, x_rows)
        return pltpu.make_async_remote_copy(
            src_ref=rbuf.at[section, rows], dst_ref=rbuf.at[section, rows],
            send_sem=x_send.at[k, q], recv_sem=x_recv.at[k, q],
            device_id={"row": target}, device_id_type=MESH,
        )

    across = [lax.rem(r + 2 * j, n_row) for j in range(1, pairs)]
    def x_start(q):
        for j, target in enumerate(across):
            x_copy(1 + j, r, target, q).start()

    at_end = (c == 0) | (c == n_col - 1)

    @pl.when(at_end)
    def _():
        for q in range(X_CHUNKS):
            x_start(q)

    for copy in mp_copies:
        copy.wait_recv()
    total = mpart[0]
    for j in range(1, n_row):
        total = total + mpart[j]
    mass[c] = total
    for way in (0, 1):
        @pl.when(sends_on(way, 1))
        def _():
            hand_on(*small[1], way, 1).start()

    def forward(s):
        for ch in range(CHUNKS):
            for way in (0, 1):
                @pl.when(here(way, s))
                def _():
                    z_copy(way, s, ch).wait_recv()
                    if s < steps:
                        @pl.when(sends_on(way, s + 1))
                        def _():
                            z_copy(way, s + 1, ch).start()
                    for j in range(1, n_layer):
                        y_copy(way, s, ch, j, l).start()
        if s <= X_CHUNKS and s < steps:
            @pl.when(jnp.logical_not(at_end))
            def _():
                for q in range(s - 1, X_CHUNKS if s == min(X_CHUNKS, steps - 1) else s):
                    x_start(q)
        for way in (0, 1):
            @pl.when(here(way, s))
            def _():
                for group in small:
                    received(*group, way, s).wait_recv()
                if s < steps:
                    @pl.when(sends_on(way, s + 1))
                    def _():
                        for group in small:
                            hand_on(*group, way, s + 1).start()

    def unpack(buf, block):
        scale = 1.0 / mass[block]

        def tile_row(tr, carry):
            rows = pl.ds(pl.multiple_of(tr * EDGE, EDGE), EDGE)
            for tc in range(tiles_c):
                cols = slice(tc * EDGE, (tc + 1) * EDGE)
                tile = buf[ranks[block, tr, tc]].astype(jnp.float32)
                left[block, rows, cols] = (tile * scale[:, cols]).astype(jnp.bfloat16)
            return carry

        lax.fori_loop(0, tiles_r, tile_row, 0)

    def foreign(s):
        for way in (0, 1):
            @pl.when(here(way, s))
            def _():
                for ch in range(CHUNKS):
                    for j in range(1, n_layer):
                        y_copy(way, s, ch, j, lax.rem(l + n_layer - j, n_layer)).wait_recv()
                unpack(
                    (from_left if way == 0 else from_right)[s - 1],
                    c - s if way == 0 else c + s,
                )

    chunk_rows = min(height, 512)

    def products(near, far):
        def one(block, carry):
            distance = jnp.abs(block - c)

            @pl.when((distance >= near) & (distance < far))
            def _():
                section, offset = block // per, (block % per) * width
                right = rbuf[section, pl.ds(pl.multiple_of(offset, EDGE), width), :]

                def rows(i, inner):
                    span = pl.ds(pl.multiple_of(i * chunk_rows, EDGE), chunk_rows)
                    acc[span, :] += jnp.dot(
                        left[block, span, :], right, preferred_element_type=jnp.float32
                    )
                    return inner

                lax.fori_loop(0, height // chunk_rows, rows, 0)

            return carry

        lax.fori_loop(0, n_col, one, 0)

    for s in range(1, max(steps, 2)):
        forward(s)
    for q in range(X_CHUNKS):
        x_copy(0, r, sibling, q).start()
    for q in range(X_CHUNKS):
        for j, target in enumerate(across):
            section = lax.rem(r + n_row - 2 * (j + 1), n_row)
            x_copy(1 + j, section, target, q).wait_recv()
            x_copy(pairs + j, section, sibling, q).start()
    if steps >= 2:
        forward(steps)
    for q in range(X_CHUNKS):
        x_copy(0, sibling, sibling, q).wait_recv()
        for j in range(len(across)):
            section = lax.rem(sibling + n_row - 2 * (j + 1), n_row)
            x_copy(pairs + j, section, sibling, q).wait_recv()
    unpack(pack, c)
    for s in range(1, steps):
        foreign(s)
    products(0, steps)
    foreign(steps)
    products(steps, n_col)

    inflated = acc[...] * acc[...]
    acc[...] = inflated
    wpart[r] = jnp.sum(inflated, axis=0, keepdims=True)
    w_copies = to_peers("row", r, n_row, wpart, w_send, w_recv)

    for copy in sends:
        copy.wait_send()
    for q in range(X_CHUNKS):
        for j, target in enumerate(across):
            x_copy(1 + j, r, target, q).wait_send()
            x_copy(pairs + j, r, sibling, q).wait_send()
        x_copy(0, r, sibling, q).wait_send()
    for s in range(1, steps + 1):
        for way in (0, 1):
            @pl.when(sends_on(way, s))
            def _():
                for ch in range(CHUNKS):
                    z_copy(way, s, ch).wait_send()
                for group in small:
                    hand_on(*group, way, s).wait_send()

            @pl.when(here(way, s))
            def _():
                for ch in range(CHUNKS):
                    for j in range(1, n_layer):
                        y_copy(way, s, ch, j, l).wait_send()

    for copy in w_copies:
        copy.wait_recv()
    total = wpart[0]
    for j in range(1, n_row):
        total = total + wpart[j]
    scale_ref[...] = (height * n_row * 1.0) / total


def scaled(inflated_ref, scale_ref, out_ref):
    out_ref[...] = inflated_ref[...] * scale_ref[...]


def shards(values, tile_mask):
    n_row, n_col, n_layer = (lax.axis_size(a) for a in ("row", "col", "layer"))
    height, width = values.shape
    tiles_r, tiles_c = tile_mask.shape
    live = tiles_r * tiles_c // 2
    half = width // n_layer
    dims = (n_row, n_col, n_layer, tiles_r, tiles_c, live)
    steps = n_col - 1
    dma = pltpu.SemaphoreType.DMA
    inflated, scale = pl.pallas_call(
        functools.partial(kernel, dims),
        out_shape=(
            pltpu.VMEM((height, half), jnp.float32),
            pltpu.VMEM((1, half), jnp.float32),
        ),
        in_specs=[pl.BlockSpec(memory_space=pl.ANY)] * 2,
        out_specs=(pl.BlockSpec(memory_space=pltpu.VMEM),) * 2,
        scratch_shapes=[
            pltpu.VMEM((tiles_r * tiles_c, EDGE, EDGE), jnp.bfloat16),
            pltpu.VMEM((live + 1, EDGE, EDGE), jnp.bfloat16),
            pltpu.VMEM((n_row, height, half), jnp.bfloat16),
            pltpu.VMEM((n_col, height, width), jnp.bfloat16),
            pltpu.SMEM((tiles_r, tiles_c), jnp.int32),
            pltpu.SMEM((n_col, tiles_r, tiles_c), jnp.int32),
            pltpu.VMEM((n_row, 1, width), jnp.float32),
            pltpu.VMEM((n_col, 1, width), jnp.float32),
            pltpu.VMEM((n_row, 1, half), jnp.float32),
            *[pltpu.VMEM((live + 1, EDGE, EDGE), jnp.bfloat16)] * steps,
            dma((2,)),
            dma((2, steps, CHUNKS)),
            dma((2, steps, CHUNKS)),
            dma((2, steps, CHUNKS, n_layer - 1)),
            dma((2, steps, CHUNKS, n_layer - 1)),
            dma((n_row, X_CHUNKS)),
            dma((n_row, X_CHUNKS)),
            dma((2, steps)),
            dma((2, steps)),
            dma((n_row - 1,)),
            dma((n_row - 1,)),
            dma((2, steps)),
            dma((2, steps)),
            dma((n_row - 1,)),
            dma((n_row - 1,)),
        ],
        compiler_params=pltpu.CompilerParams(
            collective_id=0, has_side_effects=True, vmem_limit_bytes=56 * 2**20
        ),
        name="markov_step",
    )(values, tile_mask)
    return pl.pallas_call(
        scaled,
        out_shape=jax.ShapeDtypeStruct((height, half), jnp.float32),
        in_specs=[pl.BlockSpec(memory_space=pltpu.VMEM)] * 2,
        out_specs=pl.BlockSpec(memory_space=pltpu.VMEM),
        compiler_params=pltpu.CompilerParams(vmem_limit_bytes=8 * 2**20),
        name="scaled",
    )(inflated, scale)


def solution(mesh):
    return jax.shard_map(
        shards,
        mesh=mesh,
        in_specs=(P("row", "col"), P("row", "col")),
        out_specs=P("row", ("col", "layer")),
        check_vma=False,
    )
```
